256 devices in a mesh: face: 8 (over z_hi, core), tile: 32 (over y, z_lo, x).
Axes of the slice: x: 4, y: 4, z: 8 (z_hi: 4, z_lo: 2; z = z_hi * 2 + z_lo), core: 2. Of those that a mesh axis runs over, the one named last changes fastest.
Arguments:
- activation: bfloat16 [16, 32, 24, 12, 128], P('face', 'tile'), may hold values from -6 to 6
- cotangent: bfloat16 [16, 32, 24, 12, 128], P('face', 'tile'), may hold values from -6 to 6
- weight_one: bfloat16 [9, 128, 128], replicated, may hold values from -0.1875 to 0.1875
- weight_two: bfloat16 [9, 128, 128], replicated, may hold values from -0.1875 to 0.1875
- weight_three: bfloat16 [9, 128, 128], replicated, may hold values from -0.1875 to 0.1875
- neighbor: int32 [12, 4], replicated, may hold values from 0 to 11, as said below
- turn: int32 [12, 4], replicated, may hold values from 0 to 7, as said below
Outputs:
- grad_input: bfloat16 [16, 32, 24, 12, 128], P('face', 'tile')
- grad_one: float32 [9, 128, 128], replicated
- grad_two: float32 [9, 128, 128], replicated
- grad_three: float32 [9, 128, 128], replicated
The draws below stay inside these ranges and needn't reach their ends.
Inputs may be any that keep to these rules, and one draw needn't show every extreme that they name: Face f's edge e meets edge turn[f, e] % 4 of face neighbor[f, e]; the meeting is mutual: that edge meets edge e of f back, with the same turn // 4; every one of the 12 x 4 edges meets exactly one other edge. `turn`: edge numbers 0 first row, 1 last row, 2 first column, 3 last column; 4 is added where the cells meet in reversed order.
All inputs are finite; a program needn't handle non-finite values.
Results may differ from the reference program's by a relative error of at most 0.015.
Values may be sent and summed in bfloat16 or wider, within the bound.
A program may use at most 64 MiB of HBM per device.

```python
import math
import jax
import jax.numpy as jnp
from jax import lax

C = 128
FACES = 12
TAPS = 9
TGR = 4
TH = 24
TGC = 8
TW = 12
NS = 96
TILES = 32
SLOTS = 16


def link_pairs(key):
    order = jax.random.permutation(key, FACES * 4).astype(jnp.int32)
    first = order[0::2]
    second = order[1::2]
    partner = jnp.zeros((FACES * 4,), jnp.int32).at[first].set(second).at[second].set(first)
    flips = jax.random.randint(jax.random.fold_in(key, 5), (FACES * 2,), 0, 2).astype(jnp.int32)
    reverse = jnp.zeros((FACES * 4,), jnp.int32).at[first].set(flips).at[second].set(flips)
    return (partner, reverse)


def draw_neighbor(key, part):
    partner, reverse = link_pairs(key)
    return (partner // 4).reshape(FACES, 4).astype(jnp.int32)


def draw_turn(key, part):
    partner, reverse = link_pairs(key)
    return (partner % 4 + 4 * reverse).reshape(FACES, 4).astype(jnp.int32)


def level_of(rng, shape, cuts, smallest, top_value):
    level, own = 1.0, jax.random.fold_in(rng, 6)
    for axis_at, blocks in cuts:
        draws = jnp.exp(jax.random.uniform(jax.random.fold_in(own, axis_at), (blocks,), jnp.float32, smallest / len(cuts), top_value / len(cuts)))
        level = level * jnp.repeat(draws, shape[axis_at] // blocks).reshape([-1 if axis == axis_at else 1 for axis in range(len(shape))])
    return level


def scatter_about(stream_key, shape, scale, bound, pieces=(), held_as=jnp.bfloat16):
    gain = level_of(stream_key, shape, pieces, -0.22, 0.18) if pieces else 1.0
    array = jax.random.normal(stream_key, shape, jnp.float32) * scale * gain
    return jnp.minimum(jnp.maximum(array, -bound), bound).astype(held_as)


def setup_inputs(seed: int = 0) -> dict:
    key_list = jax.random.split(jax.random.key(seed), 8)
    return {
        "activation": scatter_about(key_list[0], (SLOTS, TILES, TH, TW, C), 1.0, 6.0, ((0, 8), (1, 32))),
        "cotangent": scatter_about(key_list[1], (SLOTS, TILES, TH, TW, C), 1.0, 6.0, ((0, 8), (1, 32))),
        "weight_one": scatter_about(key_list[2], (TAPS, C, C), (TAPS * C) ** -0.5, 0.1875),
        "weight_two": scatter_about(key_list[3], (TAPS, C, C), (TAPS * C) ** -0.5, 0.1875),
        "weight_three": scatter_about(key_list[4], (TAPS, C, C), (TAPS * C) ** -0.5, 0.1875),
        "neighbor": draw_neighbor(jax.random.fold_in(key_list[7], 71), 0),
        "turn": draw_turn(jax.random.fold_in(key_list[7], 71), 0),
    }


def faces_of(field):
    grid = field[:FACES].reshape(FACES, TGR, TGC, TH, TW, C)
    return grid.transpose(0, 1, 3, 2, 4, 5).reshape(FACES, NS, NS, C)

def tiles_of(faces):
    grid = faces.reshape(FACES, TGR, TH, TGC, TW, C).transpose(0, 1, 3, 2, 4, 5)
    grid = grid.reshape(FACES, TILES, TH, TW, C)
    spare = jnp.zeros((SLOTS - FACES, TILES, TH, TW, C), faces.dtype)
    return jnp.concatenate([grid, spare], axis=0)

def extend(field, neighbor, turn):
    lines = jnp.stack([field[:, 0], field[:, -1], field[:, :, 0], field[:, :, -1]], axis=1)
    picked = lines[neighbor, turn % 4]
    cycle = jnp.where((turn // 4)[:, :, None, None] == 1, picked[:, :, ::-1], picked)
    side = field.shape[1]
    out = jnp.zeros((field.shape[0], side + 2, side + 2, field.shape[-1]), field.dtype)
    out = out.at[:, 1:-1, 1:-1].set(field)
    out = out.at[:, 0, 1:-1].set(cycle[:, 0])
    out = out.at[:, -1, 1:-1].set(cycle[:, 1])
    out = out.at[:, 1:-1, 0].set(cycle[:, 2])
    out = out.at[:, 1:-1, -1].set(cycle[:, 3])
    return out

def convolve(padded, weight):
    count, side, width = (padded.shape[0], padded.shape[1] - 2, padded.shape[2] - 2)
    total = jnp.zeros((count * side * width, weight.shape[-1]), jnp.float32)
    for dy in range(3):
        for dx in range(3):
            window = padded[:, dy:dy + side, dx:dx + width].reshape(-1, padded.shape[-1])
            total = total + jnp.dot(window, weight[3 * dy + dx], preferred_element_type=jnp.float32)
    return total.reshape(count, side, width, -1)

def spread(grad, weight):
    count, side, width, chan = grad.shape
    flat = grad.reshape(-1, chan)
    padded = jnp.zeros((count, side + 2, width + 2, chan), jnp.float32)
    for dy in range(3):
        for dx in range(3):
            term = lax.dot_general(flat, weight[3 * dy + dx], (((1,), (1,)), ((), ())), preferred_element_type=jnp.float32)
            padded = padded.at[:, dy:dy + side, dx:dx + width].add(term.reshape(count, side, width, chan))
    return padded

def weight_grad(padded, grad):
    side, width = (grad.shape[1], grad.shape[2])
    flat = grad.reshape(-1, grad.shape[-1])
    parts = []
    for dy in range(3):
        for dx in range(3):
            window = padded[:, dy:dy + side, dx:dx + width].reshape(-1, padded.shape[-1])
            parts.append(lax.dot_general(window, flat, (((0,), (0,)), ((), ())), preferred_element_type=jnp.float32))
    return jnp.stack(parts)

def gelu_back(pre, grad):
    unused, pullback = jax.vjp(jax.nn.gelu, pre)
    return pullback(grad)[0]

def reference(activation, cotangent, weight_one, weight_two, weight_three, neighbor, turn):
    inputs = faces_of(activation)
    upstream = faces_of(cotangent).astype(jnp.float32)
    blank = jnp.zeros((FACES, NS, NS, C), jnp.float32)
    unused, adjoint = jax.vjp(lambda v: extend(v, neighbor, turn), blank)

    def back(grad, weight):
        return adjoint(spread(grad, weight))[0]
    padded_zero = extend(inputs, neighbor, turn)
    pre_one = convolve(padded_zero, weight_one)
    hidden_one = jax.nn.gelu(pre_one).astype(jnp.bfloat16)
    padded_one = extend(hidden_one, neighbor, turn)
    pre_two = convolve(padded_one, weight_two)
    hidden_two = jax.nn.gelu(pre_two).astype(jnp.bfloat16)
    padded_two = extend(hidden_two, neighbor, turn)
    pre_three = convolve(padded_two, weight_three)
    scale = 1.0 / math.sqrt(FACES * NS * NS)
    delta_three = gelu_back(pre_three, upstream).astype(jnp.bfloat16)
    grad_three = weight_grad(padded_two, delta_three) * scale
    delta_two = gelu_back(pre_two, back(delta_three, weight_three)).astype(jnp.bfloat16)
    grad_two = weight_grad(padded_one, delta_two) * scale
    delta_one = gelu_back(pre_one, back(delta_two, weight_two)).astype(jnp.bfloat16)
    grad_one = weight_grad(padded_zero, delta_one) * scale
    grad_input = back(delta_one, weight_one).astype(jnp.bfloat16)
    return (tiles_of(grad_input), grad_one, grad_two, grad_three)
```

```python
import math

import jax
import jax.numpy as jnp
import numpy as np
from jax import lax
from jax.experimental import pallas as pl
from jax.experimental.pallas import tpu as pltpu
from jax.sharding import PartitionSpec as P

FACES = 12
TGR = 4
TGC = 8
TH = 24
TW = 12
C = 128
NS = 96
PITCH = 16
CELLS = TH * PITCH
GROUPS = 6
OWNERS = 24
CHUNK = 9 * C // OWNERS
KZ = 512
ROWS = 26 * PITCH
MESH = pl.DeviceIdType.MESH
BF = jnp.bfloat16
F32 = jnp.float32
TAP_TABLE = ((0, 1, 2), (6, 7, 8), (0, 3, 6), (2, 5, 8))


def spread_matrix():
    out = np.zeros((3, ROWS, KZ), np.float32)
    top, bottom, left, right = CELLS, CELLS + 16, CELLS + 32, CELLS + 64
    for dx in range(3):
        for yy in range(26):
            for x in range(TW):
                y, xx = yy - 1, x + dx - 1
                row = out[dx, yy * PITCH + x]
                inside_y, inside_x = 0 <= y < TH, 0 <= xx < TW
                if inside_y and inside_x:
                    row[y * PITCH + xx] = 1
                if y == -1:
                    row[top + xx + 1] = 1
                if y == TH:
                    row[bottom + xx + 1] = 1
                if not inside_x:
                    side = left if xx < 0 else right
                    row[side + (y + 1 if y < TW else 16 + y - TW + 1)] = 1
    return out.reshape(3 * ROWS, KZ)


def gelu_parts(x):
    c = math.sqrt(2.0 / math.pi)
    sq = x * x
    t = jnp.tanh(c * x * (1.0 + 0.044715 * sq))
    half = 0.5 * (1.0 + t)
    slope = half + 0.5 * x * (1.0 - t * t) * (c * (1.0 + 3.0 * 0.044715 * sq))
    return x * half, slope


def kernel(
    nbr, trn, act, cot, w1, w2, w3, spread,
    gin, grads,
    sel, z, xf, xb, slope, up, wst, wbk, sg, line,
    s1, nb, c1, s2, d2, gb, a1, pb, a2, gf,
    s1sem, nsem, csem, s2sem, d2sem, arsem_s, arsem_r,
):
    k = lax.axis_index("face")
    t = lax.axis_index("tile")
    row = t // TGC
    col = t % TGC
    active = k < GROUPS
    owner = t < OWNERS
    is_coll = (row >= 1) & (row <= 2) & (col >= 2) & (col <= 5)
    unit = (col - 2) * 2 + (row - 1)

    def collector(w):
        return (1 + w % 2) * TGC + 2 + w // 2

    def send(src, dst, ssem, rsem, dev):
        pltpu.make_async_remote_copy(
            src_ref=src, dst_ref=dst, send_sem=ssem, recv_sem=rsem, device_id=dev, device_id_type=MESH
        ).start()

    def await_bytes(ref, sem):
        pltpu.make_async_copy(ref, ref, sem).wait()

    slots = []
    for e in (0, 1):
        for i in range(3):
            slots.append((e, (col + 7 + i) % 8, False))
        for i in range(3):
            slots.append((e, (14 - col + i) % 8, True))
    for e in (2, 3):
        for i in range(4):
            slots.append((e, (2 * row + 7 + i) % 8, False))
        for i in range(4):
            slots.append((e, (13 - 2 * row + i) % 8, True))

    def build_sel():
        j = lax.broadcasted_iota(jnp.int32, (16, CELLS), 0)
        cell = lax.broadcasted_iota(jnp.int32, (16, CELLS), 1)
        for n, (e, w, rev) in enumerate(slots):
            pos = (96 - 12 * w) - j if rev else (12 * w - 1) + j
            local = pos - (12 * col if e < 2 else 24 * row)
            size = TW if e < 2 else TH
            base = (0, (TH - 1) * PITCH, 0, TW - 1)[e]
            stride = 1 if e < 2 else PITCH
            ok = (local >= 0) & (local < size) & (j < 14) & (cell == base + local * stride)
            sel[n * 16 : n * 16 + 16, :] = jnp.where(ok, 1.0, 0.0).astype(BF)

    def exchange_send(x):
        for f in range(2):
            cut = jnp.dot(sel[...], z[f, :CELLS], preferred_element_type=F32)
            s1[x, :, f] = cut.astype(BF).reshape(28, 16, C)

        @pl.when(row == 0)
        def _():
            for i in range(6):
                send(s1.at[x, i], c1.at[x, i], s1sem.at[x, 0], csem.at[x], (k, collector(slots[i][1])))

        @pl.when(row == TGR - 1)
        def _():
            for i in range(6):
                send(s1.at[x, 6 + i], c1.at[x, 6 + i], s1sem.at[x, 1], csem.at[x], (k, collector(slots[6 + i][1])))

        for e, edge in ((2, 0), (3, TGC - 1)):
            @pl.when(col == edge)
            def _():
                base = 12 + 8 * (e - 2)
                for i in range(8):
                    dst = 12 + 4 * (e - 2) + i // 2
                    send(s1.at[x, base + i], c1.at[x, dst], s1sem.at[x, e], csem.at[x], (k, collector(slots[base + i][1])))

        @pl.when(row > 0)
        def _():
            for i in range(3):
                send(s1.at[x, i], nb.at[x, 3 + i], s1sem.at[x, 0], nsem.at[x, 1], (k, (row - 1) * TGC + slots[i][1]))

        @pl.when(row < TGR - 1)
        def _():
            for i in range(3):
                send(s1.at[x, 6 + i], nb.at[x, i], s1sem.at[x, 1], nsem.at[x, 0], (k, (row + 1) * TGC + slots[i][1]))

        @pl.when(col > 0)
        def _():
            send(s1.at[x, 13:15], nb.at[x, 8:10], s1sem.at[x, 2], nsem.at[x, 3], (k, t - 1))

        @pl.when(col < TGC - 1)
        def _():
            send(s1.at[x, 21:23], nb.at[x, 6:8], s1sem.at[x, 3], nsem.at[x, 2], (k, t + 1))

    def sent(x):
        for e, edge in ((0, row == 0), (1, row == TGR - 1)):
            @pl.when(edge)
            def _():
                await_bytes(s1.at[x, 6 * e : 6 * e + 6], s1sem.at[x, e])

            @pl.when(jnp.logical_not(edge))
            def _():
                await_bytes(s1.at[x, 6 * e : 6 * e + 3], s1sem.at[x, e])

        for e, edge in ((2, col == 0), (3, col == TGC - 1)):
            base = 12 + 8 * (e - 2)

            @pl.when(edge)
            def _():
                await_bytes(s1.at[x, base : base + 8], s1sem.at[x, e])

            @pl.when(jnp.logical_not(edge))
            def _():
                await_bytes(s1.at[x, base : base + 2], s1sem.at[x, e])

        @pl.when(is_coll)
        def _():
            await_bytes(s2.at[x], s2sem.at[x])

    def collect(x):
        @pl.when(is_coll)
        def _():
            await_bytes(c1.at[x], csem.at[x])
            for e in range(4):
                for rev in range(2):
                    if e < 2:
                        first, count = 6 * e + 3 * rev, 3
                    else:
                        first, count = 12 + 4 * (e - 2) + 2 * rev, 2
                    total = c1[x, first].astype(F32)
                    for n in range(1, count):
                        total = total + c1[x, first + n].astype(F32)
                    line[2 * e + rev] = total.astype(BF)

            for g in range(GROUPS):
                for e in range(4):
                    for fl in range(2):
                        f = 2 * g + fl
                        code = trn[f, e]
                        s2[x, g, e, fl] = line[(code % 4) * 2 + code // 4, nbr[f, e] % 2]
                    tile = (unit, 24 + unit, (unit // 2) * TGC, (unit // 2) * TGC + TGC - 1)[e]
                    slot = 0 if e < 2 else 1 + unit % 2
                    send(s2.at[x, g, e], d2.at[x, slot, k], s2sem.at[x], d2sem.at[x, 0 if e < 2 else 1], (g, tile))

    def arrived(x, slot, f, e):
        group = nbr[jnp.minimum(2 * k + f, FACES - 1), e] // 2
        out = d2[x, slot, 0, f]
        for g in range(1, GROUPS):
            out = jnp.where(group == g, d2[x, slot, g, f], out)
        return out

    def halo_local(x):
        def summed(first, at):
            for f in range(2):
                z[f, at : at + 16] = (
                    nb[x, first, f].astype(F32) + nb[x, first + 1, f].astype(F32) + nb[x, first + 2, f].astype(F32)
                ).astype(BF)

        def blank(at, size):
            for f in range(2):
                z[f, at : at + size] = jnp.zeros((size, C), BF)

        for side, inner in ((0, row > 0), (1, row < TGR - 1)):
            @pl.when(inner)
            def _():
                await_bytes(nb.at[x, 3 * side : 3 * side + 3], nsem.at[x, side])
                summed(3 * side, CELLS + 16 * side)

            @pl.when(jnp.logical_not(inner))
            def _():
                blank(CELLS + 16 * side, 16)

        for side, inner in ((0, col > 0), (1, col < TGC - 1)):
            at = CELLS + 32 + 32 * side

            @pl.when(inner)
            def _():
                await_bytes(nb.at[x, 6 + 2 * side : 8 + 2 * side], nsem.at[x, 2 + side])
                for f in range(2):
                    for h in range(2):
                        z[f, at + 16 * h : at + 16 * h + 16] = nb[x, 6 + 2 * side + h, f]

            @pl.when(jnp.logical_not(inner))
            def _():
                blank(at, 32)

    def halo_cross(x):
        for e, edge in ((0, row == 0), (1, row == TGR - 1)):
            @pl.when(edge)
            def _():
                await_bytes(d2.at[x, 0], d2sem.at[x, 0])
                for f in range(2):
                    z[f, CELLS + 16 * e : CELLS + 16 * e + 16] = arrived(x, 0, f, e)

        for e, edge in ((2, col == 0), (3, col == TGC - 1)):
            @pl.when(edge)
            def _():
                await_bytes(d2.at[x, 1:3], d2sem.at[x, 1])
                at = CELLS + 32 + 32 * (e - 2)
                for f in range(2):
                    for h in range(2):
                        z[f, at + 16 * h : at + 16 * h + 16] = arrived(x, 1 + h, f, e)

    def widen(f, put):
        for dx in range(3):
            part = jnp.dot(spread[dx * ROWS : (dx + 1) * ROWS, :], z[f], preferred_element_type=F32)
            put(dx, part.astype(BF))

    def conv(x3, w3):
        total = None
        for dy in range(3):
            part = jnp.dot(
                x3[dy * PITCH : dy * PITCH + CELLS, :], w3[dy * 3 * C : (dy + 1) * 3 * C, :],
                preferred_element_type=F32,
            )
            total = part if total is None else total + part
        return total

    def correct(x, l):
        def taps(f, e):
            code = trn[jnp.minimum(2 * k + f, 11), e]
            other, rev = code % 4, code // 4
            first = jnp.where(other == 1, 6, jnp.where(other == 3, 2, 0))
            step = jnp.where(other < 2, 1, 3)
            out = []
            for s in range(3):
                order = jnp.where(rev == 1, 2 - s, s)
                tap = first + step * order
                out.append(wbk[l, tap])
            return out

        def product(windows, weights):
            total = None
            for n, win in enumerate(windows):
                sg[n, 0:16] = win.astype(F32)
            for s in range(3):
                pieces = [sg[n, 2 - s : 18 - s].astype(BF) for n in range(len(windows))]
                lhs = pieces[0] if len(pieces) == 1 else jnp.concatenate(pieces, axis=0)
                part = jnp.dot(lhs, weights[s], preferred_element_type=F32)
                total = part if total is None else total + part
            return total

        for e, edge in ((0, row == 0), (1, row == TGR - 1)):
            @pl.when(edge)
            def _():
                await_bytes(d2.at[x, 0], d2sem.at[x, 0])
                at = 0 if e == 0 else CELLS - PITCH
                for f in range(2):
                    more = product([arrived(x, 0, f, e)], taps(f, e))
                    up[f, at : at + 16] = up[f, at : at + 16] + more

        for e, edge in ((2, col == 0), (3, col == TGC - 1)):
            @pl.when(edge)
            def _():
                await_bytes(d2.at[x, 1:3], d2sem.at[x, 1])
                at = 0 if e == 2 else TW - 1
                for f in range(2):
                    more = product([arrived(x, 1, f, e), arrived(x, 2, f, e)], taps(f, e))
                    for h in range(2):
                        where = pl.ds(h * TW * PITCH + at, TW, stride=PITCH)
                        up[f, where, :] = up[f, where, :] + more[16 * h : 16 * h + TW]

    def reduce_send(l):
        @pl.loop(1, 32)
        def _(i):
            dst = (t + i) % 32

            @pl.when(dst < OWNERS)
            def _():
                send(
                    gb.at[l, pl.ds(dst * CHUNK, CHUNK)], a1.at[l, 31 - i],
                    arsem_s.at[l, 0], arsem_r.at[l, 0], (k, dst),
                )

    def reduce_mid(l):
        @pl.when(owner)
        def _():
            await_bytes(a1.at[l], arsem_r.at[l, 0])
            total = gb[l, pl.ds(t * CHUNK, CHUNK)].astype(F32)
            for s in range(31):
                total = total + a1[l, s].astype(F32)
            pb[l] = total.astype(BF)
            a2[l, k] = pb[l]
            for i in range(1, 8):
                send(pb.at[l], a2.at[l, k], arsem_s.at[l, 1], arsem_r.at[l, 1], ((k + i) % 8, t))

    def reduce_last(l):
        @pl.when(owner)
        def _():
            @pl.when(active)
            def _():
                await_bytes(a2.at[l, 0:5], arsem_r.at[l, 1])

            @pl.when(jnp.logical_not(active))
            def _():
                await_bytes(a2.at[l], arsem_r.at[l, 1])

            total = a2[l, 0].astype(F32)
            for s in range(1, GROUPS):
                total = total + a2[l, s].astype(F32)
            mine = pl.ds(t * CHUNK, CHUNK)
            gf[l, mine] = total.astype(BF)

            @pl.loop(1, 32)
            def _(i):
                send(gf.at[l, mine], gf.at[l, mine], arsem_s.at[l, 2], arsem_r.at[l, 2], (k, (t + i) % 32))

    def reduce_drain(l):
        @pl.when(owner)
        def _():
            await_bytes(gf.at[l, 0 : (OWNERS - 1) * CHUNK], arsem_r.at[l, 2])
            await_bytes(a1.at[l], arsem_s.at[l, 2])

            @pl.when(active)
            def _():
                await_bytes(gb.at[l, 0 : (OWNERS - 1) * CHUNK], arsem_s.at[l, 0])
                await_bytes(a1.at[l, 0:7], arsem_s.at[l, 1])

        @pl.when(jnp.logical_not(owner))
        def _():
            await_bytes(gf.at[l], arsem_r.at[l, 2])

            @pl.when(active)
            def _():
                await_bytes(gb.at[l], arsem_s.at[l, 0])

    @pl.when(active)
    def _():
        build_sel()
        for f in range(2):
            z[f, :CELLS] = act[f]
            z[f, CELLS:] = jnp.zeros((KZ - CELLS, C), BF)
        sg[...] = jnp.zeros_like(sg)
        exchange_send(0)
        for l, w in enumerate((w1, w2, w3)):
            for tap in range(9):
                wst[l, tap * C : (tap + 1) * C] = w[tap]
                wbk[l, tap] = w[tap].astype(F32).T.astype(BF)
        for f in range(2):
            up[f] = cot[f].astype(F32)

        @pl.loop(0, 3)
        def _(l):
            collect(l)
            halo_local(l)
            halo_cross(l)
            for f in range(2):
                def put(dx, part):
                    xf[l, f, :, dx * C : (dx + 1) * C] = part

                widen(f, put)
                pre = conv(xf[l, f], wst[l])
                hidden, tilt = gelu_parts(pre)
                slope[l, f] = tilt
                z[f, :CELLS] = hidden.astype(BF)

            @pl.when(l < 2)
            def _():
                exchange_send(l + 1)

        @pl.loop(0, 3)
        def _(i):
            l = 2 - i
            x = 3 + i
            for f in range(2):
                z[f, :CELLS] = (up[f] * slope[l, f]).astype(BF)
            exchange_send(x)
            collect(x)
            for dy in range(3):
                total = None
                for f in range(2):
                    part = lax.dot_general(
                        xf[l, f, dy * PITCH : dy * PITCH + CELLS, :], z[f, :CELLS],
                        (((0,), (0,)), ((), ())), preferred_element_type=F32,
                    )
                    total = part if total is None else total + part
                gb[l, dy * 3 * C : (dy + 1) * 3 * C] = total.astype(BF)
            reduce_send(l)

            @pl.when(i > 0)
            def _():
                reduce_mid(l + 1)

            @pl.when(i > 1)
            def _():
                reduce_last(l + 2)

            halo_local(x)
            for f in range(2):
                def put(dx, part):
                    xb[f, :, dx * C : (dx + 1) * C] = part

                widen(f, put)
                total = None
                for dy in range(3):
                    for dx in range(3):
                        part = jnp.dot(
                            xb[f, dy * PITCH : dy * PITCH + CELLS, dx * C : (dx + 1) * C], wbk[l, 8 - 3 * dy - dx],
                            preferred_element_type=F32,
                        )
                        total = part if total is None else total + part
                up[f] = total
            correct(x, l)

        for f in range(2):
            gin[f] = up[f].astype(BF)
        reduce_mid(0)
        reduce_last(1)
        reduce_last(0)

        @pl.loop(0, 6)
        def _(x):
            sent(x)

    @pl.when(jnp.logical_not(active))
    def _():
        gin[...] = jnp.zeros_like(gin)
        reduce_last(2)
        reduce_last(1)
        reduce_last(0)

    for l in range(3):
        reduce_drain(l)
        grads[l] = gf[l]


def shards(activation, cotangent, weight_one, weight_two, weight_three, neighbor, turn):
    def padded(field):
        return jnp.pad(field[:, 0], ((0, 0), (0, 0), (0, PITCH - TW), (0, 0))).reshape(2, CELLS, C)

    vmem = pl.BlockSpec(memory_space=pltpu.VMEM)
    smem = pl.BlockSpec(memory_space=pltpu.SMEM)
    dma = pltpu.SemaphoreType.DMA
    gin, grads = pl.pallas_call(
        kernel,
        out_shape=(
            jax.ShapeDtypeStruct((2, CELLS, C), BF),
            jax.ShapeDtypeStruct((3, 9 * C, C), BF),
        ),
        in_specs=[smem, smem] + [vmem] * 6,
        out_specs=(vmem, vmem),
        scratch_shapes=[
            pltpu.VMEM((28 * 16, CELLS), BF),
            pltpu.VMEM((2, KZ, C), BF),
            pltpu.VMEM((3, 2, ROWS, 3 * C), BF),
            pltpu.VMEM((2, ROWS, 3 * C), BF),
            pltpu.VMEM((3, 2, CELLS, C), F32),
            pltpu.VMEM((2, CELLS, C), F32),
            pltpu.VMEM((3, 9 * C, C), BF),
            pltpu.VMEM((3, 9, C, C), BF),
            pltpu.VMEM((2, 24, C), F32),
            pltpu.VMEM((8, 2, 16, C), BF),
            pltpu.VMEM((6, 28, 2, 16, C), BF),
            pltpu.VMEM((6, 10, 2, 16, C), BF),
            pltpu.VMEM((6, 20, 2, 16, C), BF),
            pltpu.VMEM((6, GROUPS, 4, 2, 16, C), BF),
            pltpu.VMEM((6, 3, GROUPS, 2, 16, C), BF),
            pltpu.VMEM((3, 9 * C, C), BF),
            pltpu.VMEM((3, 31, CHUNK, C), BF),
            pltpu.VMEM((3, CHUNK, C), BF),
            pltpu.VMEM((3, GROUPS, CHUNK, C), BF),
            pltpu.VMEM((3, 9 * C, C), BF),
            dma((6, 4)),
            dma((6, 4)),
            dma((6,)),
            dma((6,)),
            dma((6, 2)),
            dma((3, 3)),
            dma((3, 3)),
        ],
        compiler_params=pltpu.CompilerParams(
            has_side_effects=True, vmem_limit_bytes=48 * 1024 * 1024
        ),
        name="glued_convolutions",
    )(
        neighbor, turn, padded(activation), padded(cotangent), weight_one, weight_two, weight_three,
        jnp.asarray(spread_matrix(), BF),
    )
    grad_input = gin.reshape(2, 1, TH, PITCH, C)[:, :, :, :TW]
    scaled = grads.reshape(3, 9, C, C).astype(F32) * (1.0 / math.sqrt(FACES * NS * NS))
    return grad_input, scaled[0], scaled[1], scaled[2]


def solution(mesh):
    field = P("face", "tile", None, None, None)
    return jax.shard_map(
        shards,
        mesh=mesh,
        in_specs=(field, field, P(), P(), P(), P(), P()),
        out_specs=(field, P(), P(), P()),
        check_vma=False,
    )
```

```python
import math

import jax
import jax.numpy as jnp
import numpy as np
from jax import lax
from jax.experimental import pallas as pl
from jax.experimental.pallas import tpu as pltpu
from jax.sharding import PartitionSpec as P

FACES = 12
TGR = 4
TGC = 8
TH = 24
TW = 12
C = 128
NS = 96
PITCH = 16
CELLS = TH * PITCH
GROUPS = 6
OWNERS = 24
CHUNK = 9 * C // OWNERS
KZ = 512
ROWS = 26 * PITCH
MESH = pl.DeviceIdType.MESH
BF = jnp.bfloat16
F32 = jnp.float32
TAP_TABLE = ((0, 1, 2), (6, 7, 8), (0, 3, 6), (2, 5, 8))


def spread_matrix():
    out = np.zeros((3, ROWS, KZ), np.float32)
    top, bottom, left, right = CELLS, CELLS + 16, CELLS + 32, CELLS + 64
    for dx in range(3):
        for yy in range(26):
            for x in range(TW):
                y, xx = yy - 1, x + dx - 1
                row = out[dx, yy * PITCH + x]
                inside_y, inside_x = 0 <= y < TH, 0 <= xx < TW
                if inside_y and inside_x:
                    row[y * PITCH + xx] = 1
                if y == -1:
                    row[top + xx + 1] = 1
                if y == TH:
                    row[bottom + xx + 1] = 1
                if not inside_x:
                    side = left if xx < 0 else right
                    row[side + (y + 1 if y < TW else 16 + y - TW + 1)] = 1
    return out.reshape(3 * ROWS, KZ)


def gelu_parts(x):
    c = math.sqrt(2.0 / math.pi)
    sq = x * x
    t = jnp.tanh(c * x * (1.0 + 0.044715 * sq))
    half = 0.5 * (1.0 + t)
    slope = half + 0.5 * x * (1.0 - t * t) * (c * (1.0 + 3.0 * 0.044715 * sq))
    return x * half, slope


def kernel(
    nbr_h, trn_h, act_h, cot_h, w1_h, w2_h, w3_h, spread_h,
    gin, grads,
    nbr, trn, act, cot, spread, sel, z, xf, xb, slope, up, wst, wbk, sg, line,
    s1, nb, cr, cc, s2r, s2c, d2r, d2c, gb, a1, pb, a2, gf,
    insem, s1sem, nsem, crsem, ccsem, s2sem, d2sem, arsem_s, arsem_r,
):
    k = lax.axis_index("face")
    t = lax.axis_index("tile")
    row = t // TGC
    col = t % TGC
    active = k < GROUPS
    owner = t < OWNERS
    edges = (row == 0, row == TGR - 1, col == 0, col == TGC - 1)

    barrier = pltpu.get_barrier_semaphore()
    for i in range(1, 8):
        pl.semaphore_signal(barrier, inc=1, device_id=((k + i) % 8, t), device_id_type=MESH)

    @pl.loop(1, 32)
    def _(i):
        pl.semaphore_signal(barrier, inc=1, device_id=(k, (t + i) % 32), device_id_type=MESH)

    def send(src, dst, ssem, rsem, dev):
        pltpu.make_async_remote_copy(
            src_ref=src, dst_ref=dst, send_sem=ssem, recv_sem=rsem, device_id=dev, device_id_type=MESH
        ).start()

    def await_bytes(ref, sem):
        pltpu.make_async_copy(ref, ref, sem).wait()

    def mine(f):
        return jnp.minimum(2 * k + f, FACES - 1)

    slots = []
    for e in (0, 1):
        for i in range(3):
            slots.append((e, (col + 7 + i) % 8, False))
        for i in range(3):
            slots.append((e, (14 - col + i) % 8, True))
    for e in (2, 3):
        for i in range(4):
            slots.append((e, (2 * row + 7 + i) % 8, False))
        for i in range(4):
            slots.append((e, (13 - 2 * row + i) % 8, True))

    def build_sel():
        j = lax.broadcasted_iota(jnp.int32, (16, CELLS), 0)
        cell = lax.broadcasted_iota(jnp.int32, (16, CELLS), 1)
        for n, (e, w, rev) in enumerate(slots):
            pos = (96 - 12 * w) - j if rev else (12 * w - 1) + j
            local = pos - (12 * col if e < 2 else 24 * row)
            size = TW if e < 2 else TH
            base = (0, (TH - 1) * PITCH, 0, TW - 1)[e]
            stride = 1 if e < 2 else PITCH
            ok = (local >= 0) & (local < size) & (j < 14) & (cell == base + local * stride)
            sel[n * 16 : n * 16 + 16, :] = jnp.where(ok, 1.0, 0.0).astype(BF)

    def messages(x, e):
        span = 3 if e < 2 else 4
        first = 6 * e if e < 2 else 12 + 8 * (e - 2)
        for o in range(2):
            for i in range(span):
                n = first + span * o + i
                w = slots[n][1]
                h = w % 2
                at = 6 * e + 3 * o + i if e < 2 else 12 + 4 * (e - 2) + 2 * o + i // 2
                for far in range(2):
                    yield None, n, cr.at[x, at], crsem.at[x], 24 * far + w
                for far in range(2):
                    tile = (w // 2) * TGC + (TGC - 1) * far
                    if e >= 2:
                        yield None, n, cc.at[x, h, 8 + 4 * (e - 2) + 2 * o + i // 2], ccsem.at[x], tile
                    elif i == 0:
                        yield h == 1, n, cc.at[x, 1, 4 * e + 2 * o], ccsem.at[x], tile
                    elif i == 1:
                        yield None, n, cc.at[x, h, 4 * e + 2 * o + h], ccsem.at[x], tile
                    else:
                        yield h == 0, n, cc.at[x, 0, 4 * e + 2 * o + 1], ccsem.at[x], tile

    def exchange_send(x, v):
        for f in range(2):
            cut = jnp.dot(sel[...], v[f, :CELLS], preferred_element_type=F32)
            s1[x, :, f] = cut.astype(BF).reshape(28, 16, C)

        for e in range(4):
            @pl.when(edges[e])
            def _():
                for cond, n, dst, sem, tile in messages(x, e):
                    away, home = tile != t, tile == t
                    if cond is not None:
                        away, home = away & cond, home & cond

                    @pl.when(away)
                    def _():
                        send(s1.at[x, n], dst, s1sem.at[x, e], sem, (k, tile))

                    @pl.when(home)
                    def _():
                        pltpu.make_async_copy(s1.at[x, n], dst, sem).start()

        @pl.when(row > 0)
        def _():
            for i in range(3):
                send(s1.at[x, i], nb.at[x, 3 + i], s1sem.at[x, 0], nsem.at[x, 1], (k, (row - 1) * TGC + slots[i][1]))

        @pl.when(row < TGR - 1)
        def _():
            for i in range(3):
                send(s1.at[x, 6 + i], nb.at[x, i], s1sem.at[x, 1], nsem.at[x, 0], (k, (row + 1) * TGC + slots[i][1]))

        @pl.when(col > 0)
        def _():
            send(s1.at[x, 13:15], nb.at[x, 8:10], s1sem.at[x, 2], nsem.at[x, 3], (k, t - 1))

        @pl.when(col < TGC - 1)
        def _():
            send(s1.at[x, 21:23], nb.at[x, 6:8], s1sem.at[x, 3], nsem.at[x, 2], (k, t + 1))

    def sent(x):
        for e in range(4):
            first = 6 * e if e < 2 else 13 + 8 * (e - 2)

            @pl.when(edges[e])
            def _():
                for cond, n, dst, sem, tile in messages(x, e):
                    away = tile != t
                    if cond is not None:
                        away = away & cond

                    @pl.when(away)
                    def _():
                        await_bytes(s1.at[x, n], s1sem.at[x, e])

                if e < 2:
                    await_bytes(s2r.at[x, 0:5], s2sem.at[x, 0])
                else:
                    await_bytes(s2c.at[x, 0:5], s2sem.at[x, 1])

            @pl.when(jnp.logical_not(edges[e]))
            def _():
                await_bytes(s1.at[x, first : first + (3 if e < 2 else 2)], s1sem.at[x, e])

    def collect(x):
        def lines(buf, row_first, row_count, col_first):
            for e in range(4):
                for o in range(2):
                    if e < 2:
                        first, count = row_first(e, o), row_count
                    else:
                        first, count = col_first(e, o), 2
                    total = buf[first].astype(F32)
                    for n in range(1, count):
                        total = total + buf[first + n].astype(F32)
                    line[2 * e + o] = total.astype(BF)

        def pick(face, e):
            code = trn[face, e]
            return line[(code % 4) * 2 + code // 4, nbr[face, e] % 2]

        for e in range(2):
            @pl.when(edges[e])
            def _():
                await_bytes(cr.at[x], crsem.at[x])
                lines(cr.at[x], lambda e, o: 6 * e + 3 * o, 3, lambda e, o: 12 + 4 * (e - 2) + 2 * o)
                for g in range(GROUPS):
                    for f in range(2):
                        s2r[x, g, f] = pick(2 * g + f, e)
                d2r[x, k] = s2r[x, k]
                for i in range(1, GROUPS):
                    g = (k + i) % GROUPS
                    send(s2r.at[x, g], d2r.at[x, k], s2sem.at[x, 0], d2sem.at[x, 0], (g, t))

        for e in range(2, 4):
            @pl.when(edges[e])
            def _():
                await_bytes(cc.at[x], ccsem.at[x])
                for h in range(2):
                    lines(cc.at[x, h], lambda e, o: 4 * e + 2 * o, 2, lambda e, o: 8 + 4 * (e - 2) + 2 * o)
                    for g in range(GROUPS):
                        for f in range(2):
                            s2c[x, g, h, f] = pick(2 * g + f, e)
                d2c[x, k] = s2c[x, k]
                for i in range(1, GROUPS):
                    g = (k + i) % GROUPS
                    send(s2c.at[x, g], d2c.at[x, k], s2sem.at[x, 1], d2sem.at[x, 1], (g, t))

    def arrived(x, e, f, h=0):
        group = nbr[mine(f), e] // 2
        out = None
        for g in range(GROUPS):
            win = d2r[x, g, f] if e < 2 else d2c[x, g, h, f]
            out = win if out is None else jnp.where(group == g, win, out)
        return out

    def halo_local(x, v):
        for side in (0, 1):
            at = CELLS + 16 * side

            @pl.when(jnp.logical_not(edges[side]))
            def _():
                await_bytes(nb.at[x, 3 * side : 3 * side + 3], nsem.at[x, side])
                for f in range(2):
                    total = nb[x, 3 * side, f].astype(F32) + nb[x, 3 * side + 1, f].astype(F32)
                    v[f, at : at + 16] = (total + nb[x, 3 * side + 2, f].astype(F32)).astype(BF)

            @pl.when(edges[side])
            def _():
                for f in range(2):
                    v[f, at : at + 16] = jnp.zeros((16, C), BF)

        for side in (0, 1):
            at = CELLS + 32 + 32 * side

            @pl.when(jnp.logical_not(edges[2 + side]))
            def _():
                await_bytes(nb.at[x, 6 + 2 * side : 8 + 2 * side], nsem.at[x, 2 + side])
                for f in range(2):
                    for h in range(2):
                        v[f, at + 16 * h : at + 16 * h + 16] = nb[x, 6 + 2 * side + h, f]

            @pl.when(edges[2 + side])
            def _():
                for f in range(2):
                    v[f, at : at + 32] = jnp.zeros((32, C), BF)

    def widen(f, v, out):
        for dx in range(3):
            part = jnp.dot(spread[dx * ROWS : (dx + 1) * ROWS, :], v[f], preferred_element_type=F32)
            out[f, :, dx * C : (dx + 1) * C] = part.astype(BF)

    def finish(l):
        v = z.at[l]
        for e in range(4):
            @pl.when(edges[e])
            def _():
                for f in range(2):
                    if e < 2:
                        at = CELLS + 16 * e
                        v[f, at : at + 16] = arrived(l, e, f)
                    else:
                        for h in range(2):
                            at = CELLS + 32 + 32 * (e - 2) + 16 * h
                            v[f, at : at + 16] = arrived(l, e, f, h)

        @pl.when(edges[0] | edges[1] | edges[2] | edges[3])
        def _():
            for f in range(2):
                widen(f, v, xf.at[l])

    def correct(x, weights):
        for e in range(4):
            @pl.when(edges[e])
            def _():
                if e < 2:
                    await_bytes(d2r.at[x, 0:5], d2sem.at[x, 0])
                else:
                    await_bytes(d2c.at[x, 0:5], d2sem.at[x, 1])
                size = 16 if e < 2 else 32
                for f in range(2):
                    sg[0, 0:16] = arrived(x, e, f, 0).astype(F32)
                    if e >= 2:
                        sg[1, 0:16] = arrived(x, e, f, 1).astype(F32)
                        sg[0, 13:26] = sg[1, 1:14]
                    else:
                        sg[0, 16:32] = jnp.zeros((16, C), F32)
                    more = None
                    for s, weight in enumerate(weights(f, e)):
                        part = jnp.dot(sg[0, s : s + size].astype(BF), weight, preferred_element_type=F32)
                        more = part if more is None else more + part
                    if e < 2:
                        at = 0 if e == 0 else CELLS - PITCH
                        up[f, at : at + 16] = up[f, at : at + 16] + more
                    else:
                        where = pl.ds(0 if e == 2 else TW - 1, TH, stride=PITCH)
                        up[f, where, :] = up[f, where, :] + more[0:TH]

    def forward_taps(l):
        return lambda f, e: [wst[l, tap] for tap in TAP_TABLE[e]]

    def backward_taps(l):
        def weights(f, e):
            code = trn[mine(f), e]
            other, rev = code % 4, code // 4
            first = jnp.where(other == 1, 6, jnp.where(other == 3, 2, 0))
            step = jnp.where(other < 2, 1, 3)
            out = []
            for s in range(3):
                order = jnp.where(rev == 1, s, 2 - s)
                out.append(wbk[l, first + step * order])
            return out

        return weights

    def reduce_send(l):
        @pl.loop(1, 32)
        def _(i):
            dst = (t + i) % 32

            @pl.when(dst < OWNERS)
            def _():
                send(
                    gb.at[l, pl.ds(dst * CHUNK, CHUNK)], a1.at[l, 31 - i],
                    arsem_s.at[l, 0], arsem_r.at[l, 0], (k, dst),
                )

    def reduce_mid(l):
        @pl.when(owner)
        def _():
            await_bytes(a1.at[l], arsem_r.at[l, 0])
            total = gb[l, pl.ds(t * CHUNK, CHUNK)].astype(F32)
            for s in range(31):
                total = total + a1[l, s].astype(F32)
            pb[l] = total.astype(BF)
            a2[l, k] = pb[l]
            for i in range(1, 8):
                send(pb.at[l], a2.at[l, k], arsem_s.at[l, 1], arsem_r.at[l, 1], ((k + i) % 8, t))

    def reduce_last(l):
        @pl.when(owner)
        def _():
            @pl.when(active)
            def _():
                await_bytes(a2.at[l, 0:5], arsem_r.at[l, 1])

            @pl.when(jnp.logical_not(active))
            def _():
                await_bytes(a2.at[l], arsem_r.at[l, 1])

            total = a2[l, 0].astype(F32)
            for s in range(1, GROUPS):
                total = total + a2[l, s].astype(F32)
            here = pl.ds(t * CHUNK, CHUNK)
            gf[l, here] = total.astype(BF)

            @pl.loop(1, 32)
            def _(i):
                send(gf.at[l, here], gf.at[l, here], arsem_s.at[l, 2], arsem_r.at[l, 2], (k, (t + i) % 32))

    def reduce_drain(l):
        @pl.when(owner)
        def _():
            await_bytes(gf.at[l, 0 : (OWNERS - 1) * CHUNK], arsem_r.at[l, 2])
            await_bytes(a1.at[l], arsem_s.at[l, 2])

            @pl.when(active)
            def _():
                await_bytes(gb.at[l, 0 : (OWNERS - 1) * CHUNK], arsem_s.at[l, 0])
                await_bytes(a1.at[l, 0:7], arsem_s.at[l, 1])

        @pl.when(jnp.logical_not(owner))
        def _():
            await_bytes(gf.at[l], arsem_r.at[l, 2])

            @pl.when(active)
            def _():
                await_bytes(gb.at[l], arsem_s.at[l, 0])

    fetches = [
        pltpu.make_async_copy(src, dst, insem.at[n])
        for n, (src, dst) in enumerate((
            (act_h.at[:, 0], act), (w1_h, wst.at[0]), (spread_h, spread), (nbr_h, nbr), (trn_h, trn),
            (w2_h, wst.at[1]), (w3_h, wst.at[2]), (cot_h.at[:, 0], cot),
        ))
    ]

    @pl.when(active)
    def _():
        for fetch in fetches:
            fetch.start()
        build_sel()
        z[...] = jnp.zeros_like(z)
        up[...] = jnp.zeros_like(up)
        sg[...] = jnp.zeros_like(sg)
        fetches[0].wait()
        for f in range(2):
            for y in range(TH):
                z[0, f, y * PITCH : y * PITCH + TW] = act[f, y]

    pl.semaphore_wait(barrier, 38)

    @pl.when(active)
    def _():
        @pl.loop(0, 3)
        def _(l):
            exchange_send(l, z.at[l])

            @pl.when(l == 0)
            def _():
                for fetch in fetches[1:]:
                    fetch.wait()

            @pl.when(l > 0)
            def _():
                finish(l - 1)

            collect(l)
            halo_local(l, z.at[l])
            for f in range(2):
                widen(f, z.at[l], xf.at[l])
                total = None
                for dy in range(3):
                    part = jnp.dot(
                        xf[l, f, dy * PITCH : dy * PITCH + CELLS, :],
                        wst[l, 3 * dy : 3 * dy + 3].reshape(3 * C, C), preferred_element_type=F32,
                    )
                    total = part if total is None else total + part
                up[f] = total
            correct(l, forward_taps(l))
            for f in range(2):
                hidden, tilt = gelu_parts(up[f])
                slope[l, f] = tilt
                z[l + 1, f, :CELLS] = hidden.astype(BF)

        for f in range(2):
            up[f] = jnp.zeros((CELLS, C), F32)
            for y in range(TH):
                up[f, y * PITCH : y * PITCH + TW] = cot[f, y].astype(F32)

        @pl.loop(0, 3)
        def _(i):
            l = 2 - i
            x = 3 + i
            d = z.at[3]
            for f in range(2):
                d[f, :CELLS] = (up[f] * slope[l, f]).astype(BF)
            exchange_send(x, d)

            @pl.when(i == 0)
            def _():
                finish(2)
                for n in range(3):
                    for tap in range(9):
                        wbk[n, tap] = wst[n, tap].astype(F32).T.astype(BF)

            collect(x)
            for dy in range(3):
                total = None
                for f in range(2):
                    part = lax.dot_general(
                        xf[l, f, dy * PITCH : dy * PITCH + CELLS, :], d[f, :CELLS],
                        (((0,), (0,)), ((), ())), preferred_element_type=F32,
                    )
                    total = part if total is None else total + part
                gb[l, dy * 3 * C : (dy + 1) * 3 * C] = total.astype(BF)
            reduce_send(l)

            @pl.when(i > 0)
            def _():
                reduce_mid(l + 1)

            @pl.when(i > 1)
            def _():
                reduce_last(l + 2)

            halo_local(x, d)
            for f in range(2):
                widen(f, d, xb)
                total = None
                for dy in range(3):
                    for dx in range(3):
                        part = jnp.dot(
                            xb[f, dy * PITCH : dy * PITCH + CELLS, dx * C : (dx + 1) * C], wbk[l, 8 - 3 * dy - dx],
                            preferred_element_type=F32,
                        )
                        total = part if total is None else total + part
                up[f] = total

            @pl.when(i == 2)
            def _():
                reduce_mid(l)

            correct(x, backward_taps(l))

        for f in range(2):
            gin[f] = up[f].astype(BF)
        reduce_last(1)
        reduce_last(0)

        @pl.loop(0, 6)
        def _(x):
            sent(x)

    @pl.when(jnp.logical_not(active))
    def _():
        gin[...] = jnp.zeros_like(gin)
        reduce_last(2)
        reduce_last(1)
        reduce_last(0)

    for l in range(3):
        reduce_drain(l)
        grads[l] = gf[l]


def shards(activation, cotangent, weight_one, weight_two, weight_three, neighbor, turn):
    vmem = pl.BlockSpec(memory_space=pltpu.VMEM)
    hbm = pl.BlockSpec(memory_space=pl.ANY)
    dma = pltpu.SemaphoreType.DMA
    gin, grads = pl.pallas_call(
        kernel,
        out_shape=(
            jax.ShapeDtypeStruct((2, CELLS, C), BF),
            jax.ShapeDtypeStruct((3, 9 * C, C), BF),
        ),
        in_specs=[hbm] * 8,
        out_specs=(vmem, vmem),
        scratch_shapes=[
            pltpu.SMEM((FACES, 4), jnp.int32),
            pltpu.SMEM((FACES, 4), jnp.int32),
            pltpu.VMEM((2, TH, TW, C), BF),
            pltpu.VMEM((2, TH, TW, C), BF),
            pltpu.VMEM((3 * ROWS, KZ), BF),
            pltpu.VMEM((28 * 16, CELLS), BF),
            pltpu.VMEM((4, 2, KZ, C), BF),
            pltpu.VMEM((3, 2, ROWS, 3 * C), BF),
            pltpu.VMEM((2, ROWS, 3 * C), BF),
            pltpu.VMEM((3, 2, CELLS, C), F32),
            pltpu.VMEM((2, CELLS, C), F32),
            pltpu.VMEM((3, 9, C, C), BF),
            pltpu.VMEM((3, 9, C, C), BF),
            pltpu.VMEM((2, 40, C), F32),
            pltpu.VMEM((8, 2, 16, C), BF),
            pltpu.VMEM((6, 28, 2, 16, C), BF),
            pltpu.VMEM((6, 10, 2, 16, C), BF),
            pltpu.VMEM((6, 20, 2, 16, C), BF),
            pltpu.VMEM((6, 2, 16, 2, 16, C), BF),
            pltpu.VMEM((6, GROUPS, 2, 16, C), BF),
            pltpu.VMEM((6, GROUPS, 2, 2, 16, C), BF),
            pltpu.VMEM((6, GROUPS, 2, 16, C), BF),
            pltpu.VMEM((6, GROUPS, 2, 2, 16, C), BF),
            pltpu.VMEM((3, 9 * C, C), BF),
            pltpu.VMEM((3, 31, CHUNK, C), BF),
            pltpu.VMEM((3, CHUNK, C), BF),
            pltpu.VMEM((3, GROUPS, CHUNK, C), BF),
            pltpu.VMEM((3, 9 * C, C), BF),
            dma((8,)),
            dma((6, 4)),
            dma((6, 4)),
            dma((6,)),
            dma((6,)),
            dma((6, 2)),
            dma((6, 2)),
            dma((3, 3)),
            dma((3, 3)),
        ],
        compiler_params=pltpu.CompilerParams(
            collective_id=0, has_side_effects=True, vmem_limit_bytes=48 * 1024 * 1024
        ),
        name="glued_convolutions",
    )(
        neighbor, turn, activation, cotangent, weight_one, weight_two, weight_three,
        jnp.asarray(spread_matrix(), BF),
    )
    grad_input = gin.reshape(2, 1, TH, PITCH, C)[:, :, :, :TW]
    scaled = grads.reshape(3, 9, C, C).astype(F32) * (1.0 / math.sqrt(FACES * NS * NS))
    return grad_input, scaled[0], scaled[1], scaled[2]


def solution(mesh):
    field = P("face", "tile", None, None, None)
    return jax.shard_map(
        shards,
        mesh=mesh,
        in_specs=(field, field, P(), P(), P(), P(), P()),
        out_specs=(field, P(), P(), P()),
        check_vma=False,
    )
```

```python
import math

import jax
import jax.numpy as jnp
import numpy as np
from jax import lax
from jax.experimental import pallas as pl
from jax.experimental.pallas import tpu as pltpu
from jax.sharding import PartitionSpec as P

FACES = 12
TGR = 4
TGC = 8
TH = 24
TW = 12
C = 128
NS = 96
PITCH = 16
CELLS = TH * PITCH
GROUPS = 6
OWNERS = 24
CHUNK = 9 * C // OWNERS
KZ = 512
ROWS = 26 * PITCH
MESH = pl.DeviceIdType.MESH
BF = jnp.bfloat16
F32 = jnp.float32
TAP_TABLE = ((0, 1, 2), (6, 7, 8), (0, 3, 6), (2, 5, 8))


def spread_matrix():
    out = np.zeros((3, ROWS, KZ), np.float32)
    top, bottom, left, right = CELLS, CELLS + 16, CELLS + 32, CELLS + 64
    for dx in range(3):
        for yy in range(26):
            for x in range(TW):
                y, xx = yy - 1, x + dx - 1
                row = out[dx, yy * PITCH + x]
                inside_y, inside_x = 0 <= y < TH, 0 <= xx < TW
                if inside_y and inside_x:
                    row[y * PITCH + xx] = 1
                if y == -1:
                    row[top + xx + 1] = 1
                if y == TH:
                    row[bottom + xx + 1] = 1
                if not inside_x:
                    side = left if xx < 0 else right
                    row[side + (y + 1 if y < TW else 16 + y - TW + 1)] = 1
    return out.reshape(3 * ROWS, KZ)


def gelu_parts(x):
    c = math.sqrt(2.0 / math.pi)
    sq = x * x
    t = jnp.tanh(c * x * (1.0 + 0.044715 * sq))
    half = 0.5 * (1.0 + t)
    slope = half + 0.5 * x * (1.0 - t * t) * (c * (1.0 + 3.0 * 0.044715 * sq))
    return x * half, slope


def kernel(
    nbr_h, trn_h, act_h, cot_h, w1_h, w2_h, w3_h, spread_h,
    gin, grads,
    nbr, trn, pick_at, act, cot, spread, sel, z, xf, xb, slope, up, wst, wbk, sg, line,
    s1, nb, cr, cc, s2r, s2c, d2r, d2c, gb, a1, pb, a2, gf,
    insem, s1sem, nsem, crsem, ccsem, s2sem, d2sem, arsem_s, arsem_r,
):
    k = lax.axis_index("face")
    t = lax.axis_index("tile")
    row = t // TGC
    col = t % TGC
    active = k < GROUPS
    owner = t < OWNERS
    edges = (row == 0, row == TGR - 1, col == 0, col == TGC - 1)
    side = col // 4
    gathers = (row >= 1) & (row <= 2) & (((col >= 1) & (col <= 2)) | ((col >= 5) & (col <= 6)))
    served = 2 * (col - 1 + side * (7 - 2 * col)) + row - 1

    barrier = pltpu.get_barrier_semaphore()
    for i in range(1, 8):
        pl.semaphore_signal(barrier, inc=1, device_id=((k + i) % 8, t), device_id_type=MESH)

    @pl.loop(1, 32)
    def _(i):
        pl.semaphore_signal(barrier, inc=1, device_id=(k, (t + i) % 32), device_id_type=MESH)

    def gatherer(r, far):
        return (1 + r % 2) * TGC + 1 + r // 2 + far * (5 - 2 * (r // 2))

    glued = active & (edges[2] | edges[3])
    gathering = active & gathers

    @pl.when(glued)
    def _():
        for i in range(1, GROUPS):
            pl.semaphore_signal(barrier, inc=1, device_id=((k + i) % GROUPS, gatherer(row, side)), device_id_type=MESH)

    @pl.when(gathering)
    def _():
        for i in range(1, GROUPS):
            there = served * TGC + (TGC - 1) * side
            pl.semaphore_signal(barrier, inc=1, device_id=((k + i) % GROUPS, there), device_id_type=MESH)

    def send(src, dst, ssem, rsem, dev):
        pltpu.make_async_remote_copy(
            src_ref=src, dst_ref=dst, send_sem=ssem, recv_sem=rsem, device_id=dev, device_id_type=MESH
        ).start()

    def await_bytes(ref, sem):
        pltpu.make_async_copy(ref, ref, sem).wait()

    def mine(f):
        return jnp.minimum(2 * k + f, FACES - 1)

    slots = []
    for e in (0, 1):
        for i in range(3):
            slots.append((e, (col + 7 + i) % 8, False))
        for i in range(3):
            slots.append((e, (14 - col + i) % 8, True))
    for e in (2, 3):
        for i in range(4):
            slots.append((e, (2 * row + 7 + i) % 8, False))
        for i in range(4):
            slots.append((e, (13 - 2 * row + i) % 8, True))

    def build_sel():
        j = lax.broadcasted_iota(jnp.int32, (16, CELLS), 0)
        cell = lax.broadcasted_iota(jnp.int32, (16, CELLS), 1)
        for n, (e, w, rev) in enumerate(slots):
            pos = (96 - 12 * w) - j if rev else (12 * w - 1) + j
            local = pos - (12 * col if e < 2 else 24 * row)
            size = TW if e < 2 else TH
            base = (0, (TH - 1) * PITCH, 0, TW - 1)[e]
            stride = 1 if e < 2 else PITCH
            ok = (local >= 0) & (local < size) & (j < 14) & (cell == base + local * stride)
            sel[n * 16 : n * 16 + 16, :] = jnp.where(ok, 1.0, 0.0).astype(BF)

    def messages(x, e):
        span = 3 if e < 2 else 4
        first = 6 * e if e < 2 else 12 + 8 * (e - 2)
        for o in range(2):
            for i in range(span):
                n = first + span * o + i
                w = slots[n][1]
                h = w % 2
                at = 6 * e + 3 * o + i if e < 2 else 12 + 4 * (e - 2) + 2 * o + i // 2
                for far in range(2):
                    yield True, None, n, cr.at[x, at], crsem.at[x], 24 * far + w
                for far in range(2):
                    tile = gatherer(w // 2, far)
                    if e >= 2:
                        yield False, None, n, cc.at[x, h, 8 + 4 * (e - 2) + 2 * o + i // 2], ccsem.at[x], tile
                    elif i == 0:
                        yield False, h == 1, n, cc.at[x, 1, 4 * e + 2 * o], ccsem.at[x], tile
                    elif i == 1:
                        yield False, None, n, cc.at[x, h, 4 * e + 2 * o + h], ccsem.at[x], tile
                    else:
                        yield False, h == 0, n, cc.at[x, 0, 4 * e + 2 * o + 1], ccsem.at[x], tile

    def exchange_send(x, v):
        for f in range(2):
            cut = jnp.dot(sel[...], v[f, :CELLS], preferred_element_type=F32)
            s1[x, :, f] = cut.astype(BF).reshape(28, 16, C)

        for e in range(4):
            @pl.when(edges[e])
            def _():
                for stays, cond, n, dst, sem, tile in messages(x, e):
                    if stays:
                        @pl.when(tile != t)
                        def _():
                            send(s1.at[x, n], dst, s1sem.at[x, e], sem, (k, tile))

                        @pl.when(tile == t)
                        def _():
                            pltpu.make_async_copy(s1.at[x, n], dst, sem).start()
                    elif cond is None:
                        send(s1.at[x, n], dst, s1sem.at[x, e], sem, (k, tile))
                    else:
                        @pl.when(cond)
                        def _():
                            send(s1.at[x, n], dst, s1sem.at[x, e], sem, (k, tile))

        @pl.when(row > 0)
        def _():
            for i in range(3):
                send(s1.at[x, i], nb.at[x, 3 + i], s1sem.at[x, 0], nsem.at[x, 1], (k, (row - 1) * TGC + slots[i][1]))

        @pl.when(row < TGR - 1)
        def _():
            for i in range(3):
                send(s1.at[x, 6 + i], nb.at[x, i], s1sem.at[x, 1], nsem.at[x, 0], (k, (row + 1) * TGC + slots[i][1]))

        @pl.when(col > 0)
        def _():
            send(s1.at[x, 13:15], nb.at[x, 8:10], s1sem.at[x, 2], nsem.at[x, 3], (k, t - 1))

        @pl.when(col < TGC - 1)
        def _():
            send(s1.at[x, 21:23], nb.at[x, 6:8], s1sem.at[x, 3], nsem.at[x, 2], (k, t + 1))

    def sent(x):
        for e in range(4):
            first = 6 * e if e < 2 else 13 + 8 * (e - 2)

            @pl.when(edges[e])
            def _():
                for stays, cond, n, dst, sem, tile in messages(x, e):
                    if stays:
                        cond = tile != t
                    if cond is None:
                        await_bytes(s1.at[x, n], s1sem.at[x, e])
                    else:
                        @pl.when(cond)
                        def _():
                            await_bytes(s1.at[x, n], s1sem.at[x, e])

                if e < 2:
                    await_bytes(s2r.at[x, 0:5], s2sem.at[x, 0])

            @pl.when(jnp.logical_not(edges[e]))
            def _():
                await_bytes(s1.at[x, first : first + (3 if e < 2 else 2)], s1sem.at[x, e])

        @pl.when(gathers)
        def _():
            await_bytes(s2c.at[x], s2sem.at[x, 1])

    def collect(x):
        def lines(buf, row_first, row_count, col_first):
            for e in range(4):
                for o in range(2):
                    if e < 2:
                        first, count = row_first(e, o), row_count
                    else:
                        first, count = col_first(e, o), 2
                    total = buf[first].astype(F32)
                    for n in range(1, count):
                        total = total + buf[first + n].astype(F32)
                    line[2 * e + o] = total.astype(BF)

        def pick(face, e):
            at = pick_at[face, e]
            return line[at // 2, at % 2]

        for e in range(2):
            @pl.when(edges[e])
            def _():
                await_bytes(cr.at[x], crsem.at[x])
                lines(cr.at[x], lambda e, o: 6 * e + 3 * o, 3, lambda e, o: 12 + 4 * (e - 2) + 2 * o)
                for g in range(GROUPS):
                    for f in range(2):
                        s2r[x, g, f] = pick(2 * g + f, e)
                d2r[x, k] = s2r[x, k]
                for i in range(1, GROUPS):
                    g = (k + i) % GROUPS
                    send(s2r.at[x, g], d2r.at[x, k], s2sem.at[x, 0], d2sem.at[x, 0], (g, t))

        @pl.when(gathers)
        def _():
            await_bytes(cc.at[x], ccsem.at[x])
            for h in range(2):
                lines(cc.at[x, h], lambda e, o: 4 * e + 2 * o, 2, lambda e, o: 8 + 4 * (e - 2) + 2 * o)
                for g in range(GROUPS):
                    for f in range(2):
                        s2c[x, g, h, f] = pick(2 * g + f, 2 + side)
            for i in range(GROUPS):
                g = (k + i) % GROUPS
                there = served * TGC + (TGC - 1) * side
                send(s2c.at[x, g], d2c.at[x, k], s2sem.at[x, 1], d2sem.at[x, 1], (g, there))

    def arrived(x, e, f, h=0):
        group = nbr[mine(f), e] // 2
        out = None
        for g in range(GROUPS):
            win = d2r[x, g, f] if e < 2 else d2c[x, g, h, f]
            out = win if out is None else jnp.where(group == g, win, out)
        return out

    def halo_local(x, v):
        for side in (0, 1):
            at = CELLS + 16 * side

            @pl.when(jnp.logical_not(edges[side]))
            def _():
                await_bytes(nb.at[x, 3 * side : 3 * side + 3], nsem.at[x, side])
                for f in range(2):
                    total = nb[x, 3 * side, f].astype(F32) + nb[x, 3 * side + 1, f].astype(F32)
                    v[f, at : at + 16] = (total + nb[x, 3 * side + 2, f].astype(F32)).astype(BF)

            @pl.when(edges[side])
            def _():
                for f in range(2):
                    v[f, at : at + 16] = jnp.zeros((16, C), BF)

        for side in (0, 1):
            at = CELLS + 32 + 32 * side

            @pl.when(jnp.logical_not(edges[2 + side]))
            def _():
                await_bytes(nb.at[x, 6 + 2 * side : 8 + 2 * side], nsem.at[x, 2 + side])
                for f in range(2):
                    for h in range(2):
                        v[f, at + 16 * h : at + 16 * h + 16] = nb[x, 6 + 2 * side + h, f]

            @pl.when(edges[2 + side])
            def _():
                for f in range(2):
                    v[f, at : at + 32] = jnp.zeros((32, C), BF)

    def widen(f, v, out):
        for dx in range(3):
            part = jnp.dot(spread[dx * ROWS : (dx + 1) * ROWS, :], v[f], preferred_element_type=F32)
            out[f, :, dx * C : (dx + 1) * C] = part.astype(BF)

    def finish(l):
        v = z.at[l]
        for e in range(4):
            @pl.when(edges[e])
            def _():
                for f in range(2):
                    if e < 2:
                        at = CELLS + 16 * e
                        v[f, at : at + 16] = arrived(l, e, f)
                    else:
                        for h in range(2):
                            at = CELLS + 32 + 32 * (e - 2) + 16 * h
                            v[f, at : at + 16] = arrived(l, e, f, h)

        @pl.when(edges[0] | edges[1] | edges[2] | edges[3])
        def _():
            for f in range(2):
                widen(f, v, xf.at[l])

    def correct(x, weights):
        for e in range(4):
            @pl.when(edges[e])
            def _():
                if e < 2:
                    await_bytes(d2r.at[x, 0:5], d2sem.at[x, 0])
                else:
                    await_bytes(d2c.at[x], d2sem.at[x, 1])
                size = 16 if e < 2 else 32
                for f in range(2):
                    sg[0, 0:16] = arrived(x, e, f, 0).astype(F32)
                    if e >= 2:
                        sg[1, 0:16] = arrived(x, e, f, 1).astype(F32)
                        sg[0, 13:26] = sg[1, 1:14]
                    else:
                        sg[0, 16:32] = jnp.zeros((16, C), F32)
                    more = None
                    for s, weight in enumerate(weights(f, e)):
                        part = jnp.dot(sg[0, s : s + size].astype(BF), weight, preferred_element_type=F32)
                        more = part if more is None else more + part
                    if e < 2:
                        at = 0 if e == 0 else CELLS - PITCH
                        up[f, at : at + 16] = up[f, at : at + 16] + more
                    else:
                        where = pl.ds(0 if e == 2 else TW - 1, TH, stride=PITCH)
                        up[f, where, :] = up[f, where, :] + more[0:TH]

    def forward_taps(l):
        return lambda f, e: [wst[l, tap] for tap in TAP_TABLE[e]]

    def backward_taps(l):
        def weights(f, e):
            code = trn[mine(f), e]
            other, rev = code % 4, code // 4
            first = jnp.where(other == 1, 6, jnp.where(other == 3, 2, 0))
            step = jnp.where(other < 2, 1, 3)
            out = []
            for s in range(3):
                order = jnp.where(rev == 1, s, 2 - s)
                out.append(wbk[l, first + step * order])
            return out

        return weights

    def reduce_send(l):
        @pl.loop(1, 32)
        def _(i):
            dst = (t + i) % 32

            @pl.when(dst < OWNERS)
            def _():
                send(
                    gb.at[l, pl.ds(dst * CHUNK, CHUNK)], a1.at[l, 31 - i],
                    arsem_s.at[l, 0], arsem_r.at[l, 0], (k, dst),
                )

    def reduce_mid(l):
        @pl.when(owner)
        def _():
            await_bytes(a1.at[l], arsem_r.at[l, 0])
            total = gb[l, pl.ds(t * CHUNK, CHUNK)].astype(F32)
            for s in range(31):
                total = total + a1[l, s].astype(F32)
            pb[l] = total.astype(BF)
            a2[l, k] = pb[l]
            for i in range(1, 8):
                send(pb.at[l], a2.at[l, k], arsem_s.at[l, 1], arsem_r.at[l, 1], ((k + i) % 8, t))

    def reduce_last(l):
        @pl.when(owner)
        def _():
            @pl.when(active)
            def _():
                await_bytes(a2.at[l, 0:5], arsem_r.at[l, 1])

            @pl.when(jnp.logical_not(active))
            def _():
                await_bytes(a2.at[l], arsem_r.at[l, 1])

            total = a2[l, 0].astype(F32)
            for s in range(1, GROUPS):
                total = total + a2[l, s].astype(F32)
            here = pl.ds(t * CHUNK, CHUNK)
            gf[l, here] = total.astype(BF)

            @pl.loop(1, 32)
            def _(i):
                send(gf.at[l, here], gf.at[l, here], arsem_s.at[l, 2], arsem_r.at[l, 2], (k, (t + i) % 32))

    def reduce_drain(l):
        @pl.when(owner)
        def _():
            await_bytes(gf.at[l, 0 : (OWNERS - 1) * CHUNK], arsem_r.at[l, 2])
            await_bytes(a1.at[l], arsem_s.at[l, 2])

            @pl.when(active)
            def _():
                await_bytes(gb.at[l, 0 : (OWNERS - 1) * CHUNK], arsem_s.at[l, 0])
                await_bytes(a1.at[l, 0:7], arsem_s.at[l, 1])

        @pl.when(jnp.logical_not(owner))
        def _():
            await_bytes(gf.at[l], arsem_r.at[l, 2])

            @pl.when(active)
            def _():
                await_bytes(gb.at[l], arsem_s.at[l, 0])

    fetches = [
        pltpu.make_async_copy(src, dst, insem.at[n])
        for n, (src, dst) in enumerate((
            (act_h.at[:, 0], act), (w1_h, wst.at[0]), (spread_h, spread), (nbr_h, nbr), (trn_h, trn),
            (w2_h, wst.at[1]), (w3_h, wst.at[2]), (cot_h.at[:, 0], cot),
        ))
    ]

    @pl.when(active)
    def _():
        for fetch in fetches:
            fetch.start()
        build_sel()
        z[...] = jnp.zeros_like(z)
        up[...] = jnp.zeros_like(up)
        sg[...] = jnp.zeros_like(sg)
        fetches[0].wait()
        for f in range(2):
            for y in range(TH):
                z[0, f, y * PITCH : y * PITCH + TW] = act[f, y]

    @pl.when(glued | gathering)
    def _():
        pl.semaphore_wait(barrier, 38 + GROUPS - 1)

    @pl.when(jnp.logical_not(glued | gathering))
    def _():
        pl.semaphore_wait(barrier, 38)

    @pl.when(active)
    def _():
        @pl.loop(0, 3)
        def _(l):
            exchange_send(l, z.at[l])

            @pl.when(l == 0)
            def _():
                for fetch in fetches[1:]:
                    fetch.wait()
                for face in range(FACES):
                    for e in range(4):
                        code = trn[face, e]
                        pick_at[face, e] = (code % 4) * 4 + (code // 4) * 2 + nbr[face, e] % 2

            @pl.when(l > 0)
            def _():
                finish(l - 1)

            collect(l)
            halo_local(l, z.at[l])
            for f in range(2):
                widen(f, z.at[l], xf.at[l])
                total = None
                for dy in range(3):
                    part = jnp.dot(
                        xf[l, f, dy * PITCH : dy * PITCH + CELLS, :],
                        wst[l, 3 * dy : 3 * dy + 3].reshape(3 * C, C), preferred_element_type=F32,
                    )
                    total = part if total is None else total + part
                up[f] = total
            correct(l, forward_taps(l))
            for f in range(2):
                hidden, tilt = gelu_parts(up[f])
                slope[l, f] = tilt
                z[l + 1, f, :CELLS] = hidden.astype(BF)

        for f in range(2):
            up[f] = jnp.zeros((CELLS, C), F32)
            for y in range(TH):
                up[f, y * PITCH : y * PITCH + TW] = cot[f, y].astype(F32)

        @pl.loop(0, 3)
        def _(i):
            l = 2 - i
            x = 3 + i
            d = z.at[3]
            for f in range(2):
                d[f, :CELLS] = (up[f] * slope[l, f]).astype(BF)
            exchange_send(x, d)

            @pl.when(i == 0)
            def _():
                finish(2)
                for n in range(3):
                    for tap in range(9):
                        wbk[n, tap] = wst[n, tap].astype(F32).T.astype(BF)

            for dy in range(3):
                total = None
                for f in range(2):
                    part = lax.dot_general(
                        xf[l, f, dy * PITCH : dy * PITCH + CELLS, :], d[f, :CELLS],
                        (((0,), (0,)), ((), ())), preferred_element_type=F32,
                    )
                    total = part if total is None else total + part
                gb[l, dy * 3 * C : (dy + 1) * 3 * C] = total.astype(BF)

            @pl.when(i == 2)
            def _():
                reduce_send(l)

            collect(x)

            @pl.when(i < 2)
            def _():
                reduce_send(l)

            @pl.when(i > 0)
            def _():
                reduce_mid(l + 1)

            @pl.when(i > 1)
            def _():
                reduce_last(l + 2)

            halo_local(x, d)
            for f in range(2):
                widen(f, d, xb)
                total = None
                for dy in range(3):
                    for dx in range(3):
                        part = jnp.dot(
                            xb[f, dy * PITCH : dy * PITCH + CELLS, dx * C : (dx + 1) * C], wbk[l, 8 - 3 * dy - dx],
                            preferred_element_type=F32,
                        )
                        total = part if total is None else total + part
                up[f] = total

            @pl.when(i == 2)
            def _():
                reduce_mid(l)
                reduce_last(l + 1)

            correct(x, backward_taps(l))

        for f in range(2):
            gin[f] = up[f].astype(BF)
        reduce_last(0)

        @pl.loop(0, 6)
        def _(x):
            sent(x)

    @pl.when(jnp.logical_not(active))
    def _():
        gin[...] = jnp.zeros_like(gin)
        reduce_last(2)
        reduce_last(1)
        reduce_last(0)

    for l in range(3):
        reduce_drain(l)
        grads[l] = gf[l]


def shards(activation, cotangent, weight_one, weight_two, weight_three, neighbor, turn):
    vmem = pl.BlockSpec(memory_space=pltpu.VMEM)
    hbm = pl.BlockSpec(memory_space=pltpu.HBM)
    dma = pltpu.SemaphoreType.DMA
    gin, grads = pl.pallas_call(
        kernel,
        out_shape=(
            jax.ShapeDtypeStruct((2, CELLS, C), BF),
            jax.ShapeDtypeStruct((3, 9 * C, C), BF),
        ),
        in_specs=[hbm] * 8,
        out_specs=(vmem, vmem),
        scratch_shapes=[
            pltpu.SMEM((FACES, 4), jnp.int32),
            pltpu.SMEM((FACES, 4), jnp.int32),
            pltpu.SMEM((FACES, 4), jnp.int32),
            pltpu.VMEM((2, TH, TW, C), BF),
            pltpu.VMEM((2, TH, TW, C), BF),
            pltpu.VMEM((3 * ROWS, KZ), BF),
            pltpu.VMEM((28 * 16, CELLS), BF),
            pltpu.VMEM((4, 2, KZ, C), BF),
            pltpu.VMEM((3, 2, ROWS, 3 * C), BF),
            pltpu.VMEM((2, ROWS, 3 * C), BF),
            pltpu.VMEM((3, 2, CELLS, C), F32),
            pltpu.VMEM((2, CELLS, C), F32),
            pltpu.VMEM((3, 9, C, C), BF),
            pltpu.VMEM((3, 9, C, C), BF),
            pltpu.VMEM((2, 40, C), F32),
            pltpu.VMEM((8, 2, 16, C), BF),
            pltpu.VMEM((6, 28, 2, 16, C), BF),
            pltpu.VMEM((6, 10, 2, 16, C), BF),
            pltpu.VMEM((6, 20, 2, 16, C), BF),
            pltpu.VMEM((6, 2, 16, 2, 16, C), BF),
            pltpu.VMEM((6, GROUPS, 2, 16, C), BF),
            pltpu.VMEM((6, GROUPS, 2, 2, 16, C), BF),
            pltpu.VMEM((6, GROUPS, 2, 16, C), BF),
            pltpu.VMEM((6, GROUPS, 2, 2, 16, C), BF),
            pltpu.VMEM((3, 9 * C, C), BF),
            pltpu.VMEM((3, 31, CHUNK, C), BF),
            pltpu.VMEM((3, CHUNK, C), BF),
            pltpu.VMEM((3, GROUPS, CHUNK, C), BF),
            pltpu.VMEM((3, 9 * C, C), BF),
            dma((8,)),
            dma((6, 4)),
            dma((6, 4)),
            dma((6,)),
            dma((6,)),
            dma((6, 2)),
            dma((6, 2)),
            dma((3, 3)),
            dma((3, 3)),
        ],
        compiler_params=pltpu.CompilerParams(
            collective_id=0, has_side_effects=True, vmem_limit_bytes=48 * 1024 * 1024
        ),
        name="glued_convolutions",
    )(
        neighbor, turn, activation, cotangent, weight_one, weight_two, weight_three,
        jnp.asarray(spread_matrix(), BF),
    )
    grad_input = gin.reshape(2, 1, TH, PITCH, C)[:, :, :, :TW]
    scaled = grads.reshape(3, 9, C, C).astype(F32) * (1.0 / math.sqrt(FACES * NS * NS))
    return grad_input, scaled[0], scaled[1], scaled[2]


def solution(mesh):
    field = P("face", "tile", None, None, None)
    return jax.shard_map(
        shards,
        mesh=mesh,
        in_specs=(field, field, P(), P(), P(), P(), P()),
        out_specs=(field, P(), P(), P()),
        check_vma=False,
    )
```

```python
import math

import jax
import jax.numpy as jnp
import numpy as np
from jax import lax
from jax.experimental import pallas as pl
from jax.experimental.pallas import tpu as pltpu
from jax.sharding import PartitionSpec as P

FACES = 12
TGR = 4
TGC = 8
TILES = 32
TH = 24
TW = 12
C = 128
NS = 96
PITCH = 16
CELLS = TH * PITCH
GROUPS = 6
OWNERS = 24
CHUNK = 9 * C // OWNERS
KZ = 512
ROWS = 26 * PITCH
MESH = pl.DeviceIdType.MESH
BF = jnp.bfloat16
F32 = jnp.float32
TAP_TABLE = ((0, 1, 2), (6, 7, 8), (0, 3, 6), (2, 5, 8))


def spread_matrix():
    out = np.zeros((3, ROWS, KZ), np.float32)
    top, bottom, left, right = CELLS, CELLS + 16, CELLS + 32, CELLS + 64
    for dx in range(3):
        for yy in range(26):
            for x in range(TW):
                y, xx = yy - 1, x + dx - 1
                row = out[dx, yy * PITCH + x]
                inside_y, inside_x = 0 <= y < TH, 0 <= xx < TW
                if inside_y and inside_x:
                    row[y * PITCH + xx] = 1
                if y == -1:
                    row[top + xx + 1] = 1
                if y == TH:
                    row[bottom + xx + 1] = 1
                if not inside_x:
                    side = left if xx < 0 else right
                    row[side + (y + 1 if y < TW else 16 + y - TW + 1)] = 1
    return out.reshape(3 * ROWS, KZ)


def gelu_parts(x):
    c = math.sqrt(2.0 / math.pi)
    sq = x * x
    t = jnp.tanh(c * x * (1.0 + 0.044715 * sq))
    half = 0.5 * (1.0 + t)
    slope = half + 0.5 * x * (1.0 - t * t) * (c * (1.0 + 3.0 * 0.044715 * sq))
    return x * half, slope


def kernel(
    nbr_h, trn_h, act_h, cot_h, w1_h, w2_h, w3_h, spread_h,
    gin, grads,
    nbr, trn, pick_at, act, cot, spread, order, sel, z, xf, xb, slope, up, wst, wbk, sg, line,
    s1, nb, cr, cc, s2r, s2c, d2r, d2c, gb, a1, pb, a2, gf,
    insem, s1sem, nsem, crsem, ccsem, s2sem, d2sem, arsem_s, arsem_r,
):
    k = lax.axis_index("face")
    t = lax.axis_index("tile")
    row = t // TGC
    col = t % TGC
    active = k < GROUPS
    owner = t < OWNERS
    edges = (row == 0, row == TGR - 1, col == 0, col == TGC - 1)
    gathers = (row >= 1) & (row <= 2) & ((col == 1) | (col == 6))
    served = 2 * (row - 1) + (col - 1) // 5
    lines_up = (edges[0] & (col % 2 == 0)) | (edges[1] & (col % 2 == 1))

    barrier = pltpu.get_barrier_semaphore()
    for i in range(1, 8):
        pl.semaphore_signal(barrier, inc=1, device_id=((k + i) % 8, t), device_id_type=MESH)

    @pl.loop(1, 32)
    def _(i):
        pl.semaphore_signal(barrier, inc=1, device_id=(k, (t + i) % 32), device_id_type=MESH)

    def gatherer(r):
        return (1 + r // 2) * TGC + 1 + 5 * (r % 2)

    def aligner(w):
        return (w % 2) * (TILES - TGC) + w

    def greet(tile):
        for i in range(1, GROUPS):
            pl.semaphore_signal(barrier, inc=1, device_id=((k + i) % GROUPS, tile), device_id_type=MESH)

    for e in range(2):
        @pl.when(active & edges[e])
        def _():
            greet((1 - e) * (TILES - TGC) + col)

    @pl.when(active & (edges[2] | edges[3]))
    def _():
        greet(gatherer(row))

    @pl.when(active & gathers)
    def _():
        for far in range(2):
            greet(served * TGC + (TGC - 1) * far)

    def send(src, dst, ssem, rsem, dev):
        pltpu.make_async_remote_copy(
            src_ref=src, dst_ref=dst, send_sem=ssem, recv_sem=rsem, device_id=dev, device_id_type=MESH
        ).start()

    def await_bytes(ref, sem):
        pltpu.make_async_copy(ref, ref, sem).wait()

    def reorder(cells):
        return jnp.dot(order[...], cells, preferred_element_type=F32)

    def mine(f):
        return jnp.minimum(2 * k + f, FACES - 1)

    slots = []
    for e in (0, 1):
        for i in range(3):
            slots.append((e, (col + 7 + i) % 8, False))
        for i in range(3):
            slots.append((e, (14 - col + i) % 8, True))
    for e in (2, 3):
        for i in range(4):
            slots.append((e, (2 * row + 7 + i) % 8, False))
        for i in range(4):
            slots.append((e, (13 - 2 * row + i) % 8, True))

    def build_sel():
        j = lax.broadcasted_iota(jnp.int32, (16, CELLS), 0)
        cell = lax.broadcasted_iota(jnp.int32, (16, CELLS), 1)
        for n, (e, w, rev) in enumerate(slots):
            pos = (96 - 12 * w) - j if rev else (12 * w - 1) + j
            local = pos - (12 * col if e < 2 else 24 * row)
            size = TW if e < 2 else TH
            base = (0, (TH - 1) * PITCH, 0, TW - 1)[e]
            stride = 1 if e < 2 else PITCH
            ok = (local >= 0) & (local < size) & (j < 14) & (cell == base + local * stride)
            sel[n * 16 : n * 16 + 16, :] = jnp.where(ok, 1.0, 0.0).astype(BF)

    def messages(x, e):
        span = 3 if e < 2 else 4
        first = 6 * e if e < 2 else 12 + 8 * (e - 2)
        for o in range(2):
            for i in range(span):
                n = first + span * o + i
                w = slots[n][1]
                h = w % 2
                at = 6 * e + 3 * o + i if e < 2 else 12 + 4 * (e - 2) + 2 * o + i // 2
                yield True, None, n, cr.at[x, at], crsem.at[x], aligner(w)
                tile = gatherer(w // 2)
                if e >= 2:
                    yield False, None, n, cc.at[x, h, 8 + 4 * (e - 2) + 2 * o + i // 2], ccsem.at[x], tile
                elif i == 0:
                    yield False, h == 1, n, cc.at[x, 1, 4 * e + 2 * o], ccsem.at[x], tile
                elif i == 1:
                    yield False, None, n, cc.at[x, h, 4 * e + 2 * o + h], ccsem.at[x], tile
                else:
                    yield False, h == 0, n, cc.at[x, 0, 4 * e + 2 * o + 1], ccsem.at[x], tile

    def exchange_send(x, v):
        for f in range(2):
            cut = jnp.dot(sel[...], v[f, :CELLS], preferred_element_type=F32)
            s1[x, :, f] = cut.astype(BF).reshape(28, 16, C)

        for e in range(4):
            @pl.when(edges[e])
            def _():
                for stays, cond, n, dst, sem, tile in messages(x, e):
                    if stays:
                        @pl.when(tile != t)
                        def _():
                            send(s1.at[x, n], dst, s1sem.at[x, e], sem, (k, tile))

                        @pl.when(tile == t)
                        def _():
                            pltpu.make_async_copy(s1.at[x, n], dst, sem).start()
                    elif cond is None:
                        send(s1.at[x, n], dst, s1sem.at[x, e], sem, (k, tile))
                    else:
                        @pl.when(cond)
                        def _():
                            send(s1.at[x, n], dst, s1sem.at[x, e], sem, (k, tile))

        @pl.when(row > 0)
        def _():
            for i in range(3):
                send(s1.at[x, i], nb.at[x, 3 + i], s1sem.at[x, 0], nsem.at[x, 1], (k, (row - 1) * TGC + slots[i][1]))

        @pl.when(row < TGR - 1)
        def _():
            for i in range(3):
                send(s1.at[x, 6 + i], nb.at[x, i], s1sem.at[x, 1], nsem.at[x, 0], (k, (row + 1) * TGC + slots[i][1]))

        @pl.when(col > 0)
        def _():
            send(s1.at[x, 13:15], nb.at[x, 8:10], s1sem.at[x, 2], nsem.at[x, 3], (k, t - 1))

        @pl.when(col < TGC - 1)
        def _():
            send(s1.at[x, 21:23], nb.at[x, 6:8], s1sem.at[x, 3], nsem.at[x, 2], (k, t + 1))

    def sent(x):
        for e in range(4):
            first = 6 * e if e < 2 else 13 + 8 * (e - 2)

            @pl.when(edges[e])
            def _():
                for stays, cond, n, dst, sem, tile in messages(x, e):
                    if stays:
                        cond = tile != t
                    if cond is None:
                        await_bytes(s1.at[x, n], s1sem.at[x, e])
                    else:
                        @pl.when(cond)
                        def _():
                            await_bytes(s1.at[x, n], s1sem.at[x, e])

            @pl.when(jnp.logical_not(edges[e]))
            def _():
                await_bytes(s1.at[x, first : first + (3 if e < 2 else 2)], s1sem.at[x, e])

        @pl.when(gathers)
        def _():
            await_bytes(s2c.at[x], s2sem.at[x, 1])

        @pl.when(lines_up)
        def _():
            await_bytes(s2r.at[x, 0], s2sem.at[x, 0])
            await_bytes(s2r.at[x, 1, 0:5], s2sem.at[x, 0])

    def collect(x):
        def lines(buf, row_first, row_count, col_first):
            for e in range(4):
                for o in range(2):
                    if e < 2:
                        first, count = row_first(e, o), row_count
                    else:
                        first, count = col_first(e, o), 2
                    total = buf[first].astype(F32)
                    for n in range(1, count):
                        total = total + buf[first + n].astype(F32)
                    line[2 * e + o] = total.astype(BF)

        def pick(face, e):
            at = pick_at[face, e]
            return line[at // 2, at % 2]

        @pl.when(lines_up)
        def _():
            await_bytes(cr.at[x], crsem.at[x])
            lines(cr.at[x], lambda e, o: 6 * e + 3 * o, 3, lambda e, o: 12 + 4 * (e - 2) + 2 * o)
            for e in range(2):
                tile = (TILES - TGC) * e + col
                for g in range(GROUPS):
                    for f in range(2):
                        s2r[x, e, g, f] = pick(2 * g + f, e)
                for i in range(1, GROUPS):
                    g = (k + i) % GROUPS
                    send(s2r.at[x, e, g], d2r.at[x, k], s2sem.at[x, 0], d2sem.at[x, 0], (g, tile))

                @pl.when(tile != t)
                def _():
                    send(s2r.at[x, e, k], d2r.at[x, k], s2sem.at[x, 0], d2sem.at[x, 0], (k, tile))

                @pl.when(tile == t)
                def _():
                    pltpu.make_async_copy(s2r.at[x, e, k], d2r.at[x, k], d2sem.at[x, 0]).start()

        @pl.when(gathers)
        def _():
            await_bytes(cc.at[x], ccsem.at[x])
            for h in range(2):
                lines(cc.at[x, h], lambda e, o: 4 * e + 2 * o, 2, lambda e, o: 8 + 4 * (e - 2) + 2 * o)
                for far in range(2):
                    for g in range(GROUPS):
                        for f in range(2):
                            s2c[x, far, g, h, f] = pick(2 * g + f, 2 + far)
            for i in range(GROUPS):
                g = (k + i) % GROUPS
                for far in range(2):
                    there = served * TGC + (TGC - 1) * far
                    send(s2c.at[x, far, g], d2c.at[x, k], s2sem.at[x, 1], d2sem.at[x, 1], (g, there))

    def arrived(x, e, f, h=0):
        group = nbr[e, mine(f)] // 2
        out = None
        for g in range(GROUPS):
            win = d2r[x, g, f] if e < 2 else d2c[x, g, h, f]
            out = win if out is None else jnp.where(group == g, win, out)
        return out

    def halo_local(x, v):
        for side in (0, 1):
            at = CELLS + 16 * side

            @pl.when(jnp.logical_not(edges[side]))
            def _():
                await_bytes(nb.at[x, 3 * side : 3 * side + 3], nsem.at[x, side])
                for f in range(2):
                    total = nb[x, 3 * side, f].astype(F32) + nb[x, 3 * side + 1, f].astype(F32)
                    v[f, at : at + 16] = (total + nb[x, 3 * side + 2, f].astype(F32)).astype(BF)

            @pl.when(edges[side])
            def _():
                for f in range(2):
                    v[f, at : at + 16] = jnp.zeros((16, C), BF)

        for side in (0, 1):
            at = CELLS + 32 + 32 * side

            @pl.when(jnp.logical_not(edges[2 + side]))
            def _():
                await_bytes(nb.at[x, 6 + 2 * side : 8 + 2 * side], nsem.at[x, 2 + side])
                for f in range(2):
                    for h in range(2):
                        v[f, at + 16 * h : at + 16 * h + 16] = nb[x, 6 + 2 * side + h, f]

            @pl.when(edges[2 + side])
            def _():
                for f in range(2):
                    v[f, at : at + 32] = jnp.zeros((32, C), BF)

    def widen(f, v, out):
        for dx in range(3):
            part = jnp.dot(spread[dx * ROWS : (dx + 1) * ROWS, :], v[f], preferred_element_type=F32)
            out[f, :, dx * C : (dx + 1) * C] = part.astype(BF)

    def finish(l):
        v = z.at[l]
        for e in range(4):
            @pl.when(edges[e])
            def _():
                for f in range(2):
                    if e < 2:
                        at = CELLS + 16 * e
                        v[f, at : at + 16] = arrived(l, e, f)
                    else:
                        for h in range(2):
                            at = CELLS + 32 + 32 * (e - 2) + 16 * h
                            v[f, at : at + 16] = arrived(l, e, f, h)

        @pl.when(edges[0] | edges[1] | edges[2] | edges[3])
        def _():
            for f in range(2):
                widen(f, v, xf.at[l])

    def correct(x, weights):
        for e in range(4):
            @pl.when(edges[e])
            def _():
                if e < 2:
                    await_bytes(d2r.at[x], d2sem.at[x, 0])
                else:
                    await_bytes(d2c.at[x], d2sem.at[x, 1])
                size = 16 if e < 2 else 32
                for f in range(2):
                    sg[0, 0:16] = arrived(x, e, f, 0).astype(F32)
                    if e >= 2:
                        sg[1, 0:16] = arrived(x, e, f, 1).astype(F32)
                        sg[0, 13:26] = sg[1, 1:14]
                    else:
                        sg[0, 16:32] = jnp.zeros((16, C), F32)
                    more = None
                    for s, weight in enumerate(weights(f, e)):
                        part = jnp.dot(sg[0, s : s + size].astype(BF), weight, preferred_element_type=F32)
                        more = part if more is None else more + part
                    if e < 2:
                        at = 0 if e == 0 else CELLS - PITCH
                        up[f, at : at + 16] = up[f, at : at + 16] + more
                    else:
                        where = pl.ds(0 if e == 2 else TW - 1, TH, stride=PITCH)
                        up[f, where, :] = up[f, where, :] + more[0:TH]

    def forward_taps(l):
        return lambda f, e: [wst[l, tap] for tap in TAP_TABLE[e]]

    def backward_taps(l):
        def weights(f, e):
            code = trn[e, mine(f)]
            other, rev = code % 4, code // 4
            first = jnp.where(other == 1, 6, jnp.where(other == 3, 2, 0))
            step = jnp.where(other < 2, 1, 3)
            out = []
            for s in range(3):
                order = jnp.where(rev == 1, s, 2 - s)
                out.append(wbk[l, first + step * order])
            return out

        return weights

    def reduce_send(l):
        @pl.loop(1, 32)
        def _(i):
            dst = (t + i) % 32

            @pl.when(dst < OWNERS)
            def _():
                send(
                    gb.at[l, pl.ds(dst * CHUNK, CHUNK)], a1.at[l, 31 - i],
                    arsem_s.at[l, 0], arsem_r.at[l, 0], (k, dst),
                )

    def reduce_mid(l):
        @pl.when(owner)
        def _():
            await_bytes(a1.at[l], arsem_r.at[l, 0])
            total = gb[l, pl.ds(t * CHUNK, CHUNK)].astype(F32)
            for s in range(31):
                total = total + a1[l, s].astype(F32)
            pb[l] = total.astype(BF)
            a2[l, k] = pb[l]
            for i in range(1, 8):
                send(pb.at[l], a2.at[l, k], arsem_s.at[l, 1], arsem_r.at[l, 1], ((k + i) % 8, t))

    def reduce_last(l):
        @pl.when(owner)
        def _():
            @pl.when(active)
            def _():
                await_bytes(a2.at[l, 0:5], arsem_r.at[l, 1])

            @pl.when(jnp.logical_not(active))
            def _():
                await_bytes(a2.at[l], arsem_r.at[l, 1])

            total = a2[l, 0].astype(F32)
            for s in range(1, GROUPS):
                total = total + a2[l, s].astype(F32)
            here = pl.ds(t * CHUNK, CHUNK)
            gf[l, here] = total.astype(BF)

            @pl.loop(1, 32)
            def _(i):
                send(gf.at[l, here], gf.at[l, here], arsem_s.at[l, 2], arsem_r.at[l, 2], (k, (t + i) % 32))

    def reduce_drain(l):
        @pl.when(owner)
        def _():
            await_bytes(gf.at[l, 0 : (OWNERS - 1) * CHUNK], arsem_r.at[l, 2])
            await_bytes(a1.at[l], arsem_s.at[l, 2])

            @pl.when(active)
            def _():
                await_bytes(gb.at[l, 0 : (OWNERS - 1) * CHUNK], arsem_s.at[l, 0])
                await_bytes(a1.at[l, 0:7], arsem_s.at[l, 1])

        @pl.when(jnp.logical_not(owner))
        def _():
            await_bytes(gf.at[l], arsem_r.at[l, 2])

            @pl.when(active)
            def _():
                await_bytes(gb.at[l], arsem_s.at[l, 0])

    fetches = [
        pltpu.make_async_copy(src, dst, insem.at[n])
        for n, (src, dst) in enumerate((
            (act_h, act), (w1_h, wst.at[0]), (spread_h, spread), (nbr_h, nbr), (trn_h, trn),
            (w2_h, wst.at[1]), (w3_h, wst.at[2]), (cot_h, cot),
        ))
    ]

    @pl.when(active)
    def _():
        for fetch in fetches:
            fetch.start()
        place = lax.broadcasted_iota(jnp.int32, (CELLS, TW * TH), 0)
        given = lax.broadcasted_iota(jnp.int32, (CELLS, TW * TH), 1)
        order[...] = jnp.where((given % TH) * PITCH + given // TH == place, 1.0, 0.0).astype(BF)
        build_sel()
        z[...] = jnp.zeros_like(z)
        up[...] = jnp.zeros_like(up)
        sg[...] = jnp.zeros_like(sg)
        fetches[0].wait()
        for f in range(2):
            z[0, f, :CELLS] = reorder(act[f]).astype(BF)

    across, along = edges[0] | edges[1], edges[2] | edges[3]
    most = active & ((across & along) | gathers)
    some = active & (across ^ along)

    @pl.when(most)
    def _():
        pl.semaphore_wait(barrier, 38 + 2 * (GROUPS - 1))

    @pl.when(some)
    def _():
        pl.semaphore_wait(barrier, 38 + GROUPS - 1)

    @pl.when(jnp.logical_not(most | some))
    def _():
        pl.semaphore_wait(barrier, 38)

    @pl.when(active)
    def _():
        @pl.loop(0, 3)
        def _(l):
            exchange_send(l, z.at[l])

            @pl.when(l == 0)
            def _():
                for fetch in fetches[1:]:
                    fetch.wait()
                for face in range(FACES):
                    for e in range(4):
                        code = trn[e, face]
                        pick_at[face, e] = (code % 4) * 4 + (code // 4) * 2 + nbr[e, face] % 2

            @pl.when(l > 0)
            def _():
                finish(l - 1)

            collect(l)
            halo_local(l, z.at[l])
            for f in range(2):
                widen(f, z.at[l], xf.at[l])
                total = None
                for dy in range(3):
                    part = jnp.dot(
                        xf[l, f, dy * PITCH : dy * PITCH + CELLS, :],
                        wst[l, 3 * dy : 3 * dy + 3].reshape(3 * C, C), preferred_element_type=F32,
                    )
                    total = part if total is None else total + part
                up[f] = total
            correct(l, forward_taps(l))
            for f in range(2):
                hidden, tilt = gelu_parts(up[f])
                slope[l, f] = tilt
                z[l + 1, f, :CELLS] = hidden.astype(BF)

        for f in range(2):
            up[f] = reorder(cot[f])

        @pl.loop(0, 3)
        def _(i):
            l = 2 - i
            x = 3 + i
            d = z.at[3]
            for f in range(2):
                d[f, :CELLS] = (up[f] * slope[l, f]).astype(BF)
            exchange_send(x, d)

            @pl.when(i == 0)
            def _():
                finish(2)
                for n in range(3):
                    for tap in range(9):
                        wbk[n, tap] = wst[n, tap].astype(F32).T.astype(BF)

            for dy in range(3):
                total = None
                for f in range(2):
                    part = lax.dot_general(
                        xf[l, f, dy * PITCH : dy * PITCH + CELLS, :], d[f, :CELLS],
                        (((0,), (0,)), ((), ())), preferred_element_type=F32,
                    )
                    total = part if total is None else total + part
                gb[l, dy * 3 * C : (dy + 1) * 3 * C] = total.astype(BF)

            @pl.when(i == 2)
            def _():
                reduce_send(l)

            collect(x)

            @pl.when(i < 2)
            def _():
                reduce_send(l)

            @pl.when(i > 0)
            def _():
                reduce_mid(l + 1)

            @pl.when(i > 1)
            def _():
                reduce_last(l + 2)

            halo_local(x, d)
            for f in range(2):
                widen(f, d, xb)
                total = None
                for dy in range(3):
                    for dx in range(3):
                        part = jnp.dot(
                            xb[f, dy * PITCH : dy * PITCH + CELLS, dx * C : (dx + 1) * C], wbk[l, 8 - 3 * dy - dx],
                            preferred_element_type=F32,
                        )
                        total = part if total is None else total + part
                up[f] = total

            @pl.when(i == 2)
            def _():
                reduce_mid(l)
                reduce_last(l + 1)

            correct(x, backward_taps(l))

        for f in range(2):
            gin[f] = lax.dot_general(
                order[...], up[f].astype(BF), (((0,), (0,)), ((), ())), preferred_element_type=F32
            ).astype(BF)
        reduce_last(0)

        @pl.loop(0, 6)
        def _(x):
            sent(x)

    @pl.when(jnp.logical_not(active))
    def _():
        gin[...] = jnp.zeros_like(gin)
        reduce_last(2)
        reduce_last(1)
        reduce_last(0)

    for l in range(3):
        reduce_drain(l)
        grads[l] = gf[l]


def shards(activation, cotangent, weight_one, weight_two, weight_three, neighbor, turn):
    def flipped(field):
        return field.transpose(0, 1, 3, 2, 4).reshape(2, TW * TH, C)

    vmem = pl.BlockSpec(memory_space=pltpu.VMEM)
    hbm = pl.BlockSpec(memory_space=pltpu.HBM)
    dma = pltpu.SemaphoreType.DMA
    gin, grads = pl.pallas_call(
        kernel,
        out_shape=(
            jax.ShapeDtypeStruct((2, TW * TH, C), BF),
            jax.ShapeDtypeStruct((3, 9 * C, C), BF),
        ),
        in_specs=[hbm] * 8,
        out_specs=(vmem, vmem),
        scratch_shapes=[
            pltpu.SMEM((4, FACES), jnp.int32),
            pltpu.SMEM((4, FACES), jnp.int32),
            pltpu.SMEM((FACES, 4), jnp.int32),
            pltpu.VMEM((2, TW * TH, C), BF),
            pltpu.VMEM((2, TW * TH, C), BF),
            pltpu.VMEM((3 * ROWS, KZ), BF),
            pltpu.VMEM((CELLS, TW * TH), BF),
            pltpu.VMEM((28 * 16, CELLS), BF),
            pltpu.VMEM((4, 2, KZ, C), BF),
            pltpu.VMEM((3, 2, ROWS, 3 * C), BF),
            pltpu.VMEM((2, ROWS, 3 * C), BF),
            pltpu.VMEM((3, 2, CELLS, C), F32),
            pltpu.VMEM((2, CELLS, C), F32),
            pltpu.VMEM((3, 9, C, C), BF),
            pltpu.VMEM((3, 9, C, C), BF),
            pltpu.VMEM((2, 40, C), F32),
            pltpu.VMEM((8, 2, 16, C), BF),
            pltpu.VMEM((6, 28, 2, 16, C), BF),
            pltpu.VMEM((6, 10, 2, 16, C), BF),
            pltpu.VMEM((6, 20, 2, 16, C), BF),
            pltpu.VMEM((6, 2, 16, 2, 16, C), BF),
            pltpu.VMEM((6, 2, GROUPS, 2, 16, C), BF),
            pltpu.VMEM((6, 2, GROUPS, 2, 2, 16, C), BF),
            pltpu.VMEM((6, GROUPS, 2, 16, C), BF),
            pltpu.VMEM((6, GROUPS, 2, 2, 16, C), BF),
            pltpu.VMEM((3, 9 * C, C), BF),
            pltpu.VMEM((3, 31, CHUNK, C), BF),
            pltpu.VMEM((3, CHUNK, C), BF),
            pltpu.VMEM((3, GROUPS, CHUNK, C), BF),
            pltpu.VMEM((3, 9 * C, C), BF),
            dma((8,)),
            dma((6, 4)),
            dma((6, 4)),
            dma((6,)),
            dma((6,)),
            dma((6, 2)),
            dma((6, 2)),
            dma((3, 3)),
            dma((3, 3)),
        ],
        compiler_params=pltpu.CompilerParams(
            collective_id=0, has_side_effects=True, vmem_limit_bytes=62 * 1024 * 1024
        ),
        name="glued_convolutions",
    )(
        neighbor.T, turn.T, flipped(activation), flipped(cotangent), weight_one, weight_two, weight_three,
        jnp.asarray(spread_matrix(), BF),
    )
    grad_input = gin.reshape(2, 1, TW, TH, C).transpose(0, 1, 3, 2, 4)
    scaled = grads.reshape(3, 9, C, C).astype(F32) * (1.0 / math.sqrt(FACES * NS * NS))
    return grad_input, scaled[0], scaled[1], scaled[2]


def solution(mesh):
    field = P("face", "tile", None, None, None)
    return jax.shard_map(
        shards,
        mesh=mesh,
        in_specs=(field, field, P(), P(), P(), P(), P()),
        out_specs=(field, P(), P(), P()),
        check_vma=False,
    )
```

```python
import math

import jax
import jax.numpy as jnp
import numpy as np
from jax import lax
from jax.experimental import pallas as pl
from jax.experimental.pallas import tpu as pltpu
from jax.sharding import PartitionSpec as P

FACES = 12
TGR = 4
TGC = 8
TILES = 32
TH = 24
TW = 12
C = 128
NS = 96
PITCH = 16
CELLS = TH * PITCH
GROUPS = 6
OWNERS = 24
CHUNK = 9 * C // OWNERS
KZ = 512
ROWS = 26 * PITCH
MESH = pl.DeviceIdType.MESH
BF = jnp.bfloat16
F32 = jnp.float32
TAP_TABLE = ((0, 1, 2), (6, 7, 8), (0, 3, 6), (2, 5, 8))


def spread_matrix():
    out = np.zeros((3, ROWS, KZ), np.float32)
    top, bottom, left, right = CELLS, CELLS + 16, CELLS + 32, CELLS + 64
    for dx in range(3):
        for yy in range(26):
            for x in range(TW):
                y, xx = yy - 1, x + dx - 1
                row = out[dx, yy * PITCH + x]
                inside_y, inside_x = 0 <= y < TH, 0 <= xx < TW
                if inside_y and inside_x:
                    row[y * PITCH + xx] = 1
                if y == -1:
                    row[top + xx + 1] = 1
                if y == TH:
                    row[bottom + xx + 1] = 1
                if not inside_x:
                    side = left if xx < 0 else right
                    row[side + (y + 1 if y < TW else 16 + y - TW + 1)] = 1
    return out.reshape(3 * ROWS, KZ)


def gelu_parts(x):
    c = math.sqrt(2.0 / math.pi)
    sq = x * x
    t = jnp.tanh(c * x * (1.0 + 0.044715 * sq))
    half = 0.5 * (1.0 + t)
    slope = half + 0.5 * x * (1.0 - t * t) * (c * (1.0 + 3.0 * 0.044715 * sq))
    return x * half, slope


def kernel(
    nbr_h, trn_h, act_h, cot_h, w1_h, w2_h, w3_h, spread_h,
    gin, grads,
    nbr, trn, pick_at, act, cot, spread, order, sel, z, xf, xb, slope, up, wst, wbk, sg, line,
    s1, nb, cr, cc, s2r, s2c, d2r, d2c, gb, a1, pb, a2, gf,
    insem, s1sem, nsem, crsem, ccsem, s2sem, d2sem, arsem_s, arsem_r,
):
    k = lax.axis_index("face")
    t = lax.axis_index("tile")
    row = t // TGC
    col = t % TGC
    active = k < GROUPS
    owner = t < OWNERS
    edges = (row == 0, row == TGR - 1, col == 0, col == TGC - 1)
    gathers = (row >= 1) & (row <= 2) & (((col >= 1) & (col <= 2)) | ((col >= 5) & (col <= 6)))
    served = 2 * (row - 1) + col // 4
    part = (col - 1 + (col // 4) * (7 - 2 * col)) % 2
    lines_up = (edges[0] & (col % 2 == 0)) | (edges[1] & (col % 2 == 1))

    barrier = pltpu.get_barrier_semaphore()
    for i in range(1, 8):
        pl.semaphore_signal(barrier, inc=1, device_id=((k + i) % 8, t), device_id_type=MESH)

    @pl.loop(1, 32)
    def _(i):
        pl.semaphore_signal(barrier, inc=1, device_id=(k, (t + i) % 32), device_id_type=MESH)

    def gatherer(r, h):
        return (1 + r // 2) * TGC + 1 + h + (r % 2) * (5 - 2 * h)

    def aligner(w):
        return (w % 2) * (TILES - TGC) + w

    def greet(tile):
        for i in range(1, GROUPS):
            pl.semaphore_signal(barrier, inc=1, device_id=((k + i) % GROUPS, tile), device_id_type=MESH)

    for e in range(2):
        @pl.when(active & edges[e])
        def _():
            greet((1 - e) * (TILES - TGC) + col)

    @pl.when(active & (edges[2] | edges[3]))
    def _():
        greet(gatherer(row, 0))
        greet(gatherer(row, 1))

    @pl.when(active & gathers)
    def _():
        for far in range(2):
            greet(served * TGC + (TGC - 1) * far)

    def send(src, dst, ssem, rsem, dev):
        pltpu.make_async_remote_copy(
            src_ref=src, dst_ref=dst, send_sem=ssem, recv_sem=rsem, device_id=dev, device_id_type=MESH
        ).start()

    def await_bytes(ref, sem):
        pltpu.make_async_copy(ref, ref, sem).wait()

    def reorder(cells):
        return jnp.dot(order[...], cells, preferred_element_type=F32)

    def mine(f):
        return jnp.minimum(2 * k + f, FACES - 1)

    slots = []
    for e in (0, 1):
        for i in range(3):
            slots.append((e, (col + 7 + i) % 8, False))
        for i in range(3):
            slots.append((e, (14 - col + i) % 8, True))
    for e in (2, 3):
        for i in range(4):
            slots.append((e, (2 * row + 7 + i) % 8, False))
        for i in range(4):
            slots.append((e, (13 - 2 * row + i) % 8, True))

    def build_sel():
        j = lax.broadcasted_iota(jnp.int32, (16, CELLS), 0)
        cell = lax.broadcasted_iota(jnp.int32, (16, CELLS), 1)
        for n, (e, w, rev) in enumerate(slots):
            pos = (96 - 12 * w) - j if rev else (12 * w - 1) + j
            local = pos - (12 * col if e < 2 else 24 * row)
            size = TW if e < 2 else TH
            base = (0, (TH - 1) * PITCH, 0, TW - 1)[e]
            stride = 1 if e < 2 else PITCH
            ok = (local >= 0) & (local < size) & (j < 14) & (cell == base + local * stride)
            sel[n * 16 : n * 16 + 16, :] = jnp.where(ok, 1.0, 0.0).astype(BF)

    def messages(x, e):
        span = 3 if e < 2 else 4
        first = 6 * e if e < 2 else 12 + 8 * (e - 2)
        for o in range(2):
            for i in range(span):
                n = first + span * o + i
                w = slots[n][1]
                h = w % 2
                at = 6 * e + 3 * o + i if e < 2 else 12 + 4 * (e - 2) + 2 * o + i // 2
                yield True, None, n, cr.at[x, at], crsem.at[x], aligner(w)
                tile = gatherer(w // 2, h)
                if e >= 2:
                    yield False, None, n, cc.at[x, 8 + 4 * (e - 2) + 2 * o + i // 2], ccsem.at[x], tile
                elif i == 0:
                    yield False, h == 1, n, cc.at[x, 4 * e + 2 * o], ccsem.at[x], tile
                elif i == 1:
                    yield False, None, n, cc.at[x, 4 * e + 2 * o + h], ccsem.at[x], tile
                else:
                    yield False, h == 0, n, cc.at[x, 4 * e + 2 * o + 1], ccsem.at[x], tile

    def exchange_send(x, v):
        for f in range(2):
            cut = jnp.dot(sel[...], v[f, :CELLS], preferred_element_type=F32)
            s1[x, :, f] = cut.astype(BF).reshape(28, 16, C)

        for e in range(4):
            @pl.when(edges[e])
            def _():
                for stays, cond, n, dst, sem, tile in messages(x, e):
                    if stays:
                        @pl.when(tile != t)
                        def _():
                            send(s1.at[x, n], dst, s1sem.at[x, e], sem, (k, tile))

                        @pl.when(tile == t)
                        def _():
                            pltpu.make_async_copy(s1.at[x, n], dst, sem).start()
                    elif cond is None:
                        send(s1.at[x, n], dst, s1sem.at[x, e], sem, (k, tile))
                    else:
                        @pl.when(cond)
                        def _():
                            send(s1.at[x, n], dst, s1sem.at[x, e], sem, (k, tile))

        @pl.when(row > 0)
        def _():
            for i in range(3):
                send(s1.at[x, i], nb.at[x, 3 + i], s1sem.at[x, 0], nsem.at[x, 1], (k, (row - 1) * TGC + slots[i][1]))

        @pl.when(row < TGR - 1)
        def _():
            for i in range(3):
                send(s1.at[x, 6 + i], nb.at[x, i], s1sem.at[x, 1], nsem.at[x, 0], (k, (row + 1) * TGC + slots[i][1]))

        @pl.when(col > 0)
        def _():
            send(s1.at[x, 13:15], nb.at[x, 8:10], s1sem.at[x, 2], nsem.at[x, 3], (k, t - 1))

        @pl.when(col < TGC - 1)
        def _():
            send(s1.at[x, 21:23], nb.at[x, 6:8], s1sem.at[x, 3], nsem.at[x, 2], (k, t + 1))

    def sent(x):
        for e in range(4):
            first = 6 * e if e < 2 else 13 + 8 * (e - 2)

            @pl.when(edges[e])
            def _():
                for stays, cond, n, dst, sem, tile in messages(x, e):
                    if stays:
                        cond = tile != t
                    if cond is None:
                        await_bytes(s1.at[x, n], s1sem.at[x, e])
                    else:
                        @pl.when(cond)
                        def _():
                            await_bytes(s1.at[x, n], s1sem.at[x, e])

            @pl.when(jnp.logical_not(edges[e]))
            def _():
                await_bytes(s1.at[x, first : first + (3 if e < 2 else 2)], s1sem.at[x, e])

        @pl.when(gathers)
        def _():
            await_bytes(s2c.at[x], s2sem.at[x, 1])

        @pl.when(lines_up)
        def _():
            await_bytes(s2r.at[x, 0], s2sem.at[x, 0])
            await_bytes(s2r.at[x, 1, 0:5], s2sem.at[x, 0])

    def collect(x):
        def lines(buf, row_first, row_count, col_first):
            for e in range(4):
                for o in range(2):
                    if e < 2:
                        first, count = row_first(e, o), row_count
                    else:
                        first, count = col_first(e, o), 2
                    total = buf[first].astype(F32)
                    for n in range(1, count):
                        total = total + buf[first + n].astype(F32)
                    line[2 * e + o] = total.astype(BF)

        def pick(face, e):
            at = pick_at[face, e]
            return line[at // 2, at % 2]

        @pl.when(lines_up)
        def _():
            await_bytes(cr.at[x], crsem.at[x])
            lines(cr.at[x], lambda e, o: 6 * e + 3 * o, 3, lambda e, o: 12 + 4 * (e - 2) + 2 * o)
            for e in range(2):
                tile = (TILES - TGC) * e + col
                for g in range(GROUPS):
                    for f in range(2):
                        s2r[x, e, g, f] = pick(2 * g + f, e)
                for i in range(1, GROUPS):
                    g = (k + i) % GROUPS
                    send(s2r.at[x, e, g], d2r.at[x, k], s2sem.at[x, 0], d2sem.at[x, 0], (g, tile))

                @pl.when(tile != t)
                def _():
                    send(s2r.at[x, e, k], d2r.at[x, k], s2sem.at[x, 0], d2sem.at[x, 0], (k, tile))

                @pl.when(tile == t)
                def _():
                    pltpu.make_async_copy(s2r.at[x, e, k], d2r.at[x, k], d2sem.at[x, 0]).start()

        @pl.when(gathers)
        def _():
            await_bytes(cc.at[x], ccsem.at[x])
            lines(cc.at[x], lambda e, o: 4 * e + 2 * o, 2, lambda e, o: 8 + 4 * (e - 2) + 2 * o)
            for far in range(2):
                there = served * TGC + (TGC - 1) * far
                for g in range(GROUPS):
                    for f in range(2):
                        s2c[x, far, g, f] = pick(2 * g + f, 2 + far)
                for i in range(GROUPS):
                    g = (k + i) % GROUPS
                    send(s2c.at[x, far, g], d2c.at[x, k, part], s2sem.at[x, 1], d2sem.at[x, 1], (g, there))

    def arrived(x, e, f, h=0):
        group = nbr[e, mine(f)] // 2
        out = None
        for g in range(GROUPS):
            win = d2r[x, g, f] if e < 2 else d2c[x, g, h, f]
            out = win if out is None else jnp.where(group == g, win, out)
        return out

    def halo_local(x, v):
        for side in (0, 1):
            at = CELLS + 16 * side

            @pl.when(jnp.logical_not(edges[side]))
            def _():
                await_bytes(nb.at[x, 3 * side : 3 * side + 3], nsem.at[x, side])
                for f in range(2):
                    total = nb[x, 3 * side, f].astype(F32) + nb[x, 3 * side + 1, f].astype(F32)
                    v[f, at : at + 16] = (total + nb[x, 3 * side + 2, f].astype(F32)).astype(BF)

            @pl.when(edges[side])
            def _():
                for f in range(2):
                    v[f, at : at + 16] = jnp.zeros((16, C), BF)

        for side in (0, 1):
            at = CELLS + 32 + 32 * side

            @pl.when(jnp.logical_not(edges[2 + side]))
            def _():
                await_bytes(nb.at[x, 6 + 2 * side : 8 + 2 * side], nsem.at[x, 2 + side])
                for f in range(2):
                    for h in range(2):
                        v[f, at + 16 * h : at + 16 * h + 16] = nb[x, 6 + 2 * side + h, f]

            @pl.when(edges[2 + side])
            def _():
                for f in range(2):
                    v[f, at : at + 32] = jnp.zeros((32, C), BF)

    def widen(f, v, out):
        for dx in range(3):
            part = jnp.dot(spread[dx * ROWS : (dx + 1) * ROWS, :], v[f], preferred_element_type=F32)
            out[f, :, dx * C : (dx + 1) * C] = part.astype(BF)

    def finish(l):
        v = z.at[l]
        for e in range(4):
            @pl.when(edges[e])
            def _():
                for f in range(2):
                    if e < 2:
                        at = CELLS + 16 * e
                        v[f, at : at + 16] = arrived(l, e, f)
                    else:
                        for h in range(2):
                            at = CELLS + 32 + 32 * (e - 2) + 16 * h
                            v[f, at : at + 16] = arrived(l, e, f, h)

        @pl.when(edges[0] | edges[1] | edges[2] | edges[3])
        def _():
            for f in range(2):
                widen(f, v, xf.at[l])

    def correct(x, weights):
        for e in range(4):
            @pl.when(edges[e])
            def _():
                if e < 2:
                    await_bytes(d2r.at[x], d2sem.at[x, 0])
                else:
                    await_bytes(d2c.at[x], d2sem.at[x, 1])
                size = 16 if e < 2 else 32
                for f in range(2):
                    win = sg.at[2 * e + f]
                    win[0:16] = arrived(x, e, f, 0).astype(F32)
                    if e >= 2:
                        win[48:64] = arrived(x, e, f, 1).astype(F32)
                        win[13:26] = win[49:62]
                moved = []
                for f in range(2):
                    more = None
                    for s, weight in enumerate(weights(f, e)):
                        part = jnp.dot(sg[2 * e + f, s : s + size].astype(BF), weight, preferred_element_type=F32)
                        more = part if more is None else more + part
                    moved.append(more)
                for f, more in enumerate(moved):
                    if e < 2:
                        at = 0 if e == 0 else CELLS - PITCH
                        up[f, at : at + 16] = up[f, at : at + 16] + more
                    else:
                        where = pl.ds(0 if e == 2 else TW - 1, TH, stride=PITCH)
                        up[f, where, :] = up[f, where, :] + more[0:TH]

    def forward_taps(l):
        return lambda f, e: [wst[l, tap] for tap in TAP_TABLE[e]]

    def backward_taps(l):
        def weights(f, e):
            code = trn[e, mine(f)]
            other, rev = code % 4, code // 4
            first = jnp.where(other == 1, 6, jnp.where(other == 3, 2, 0))
            step = jnp.where(other < 2, 1, 3)
            out = []
            for s in range(3):
                order = jnp.where(rev == 1, s, 2 - s)
                out.append(wbk[l, first + step * order])
            return out

        return weights

    def reduce_send(l):
        @pl.loop(1, 32)
        def _(i):
            dst = (t + i) % 32

            @pl.when(dst < OWNERS)
            def _():
                send(
                    gb.at[l, pl.ds(dst * CHUNK, CHUNK)], a1.at[l, 31 - i],
                    arsem_s.at[l, 0], arsem_r.at[l, 0], (k, dst),
                )

    def reduce_mid(l):
        @pl.when(owner)
        def _():
            await_bytes(a1.at[l], arsem_r.at[l, 0])
            total = gb[l, pl.ds(t * CHUNK, CHUNK)].astype(F32)
            for s in range(31):
                total = total + a1[l, s].astype(F32)
            pb[l] = total.astype(BF)
            a2[l, k] = pb[l]
            for i in range(1, 8):
                send(pb.at[l], a2.at[l, k], arsem_s.at[l, 1], arsem_r.at[l, 1], ((k + i) % 8, t))

    def reduce_last(l):
        @pl.when(owner)
        def _():
            @pl.when(active)
            def _():
                await_bytes(a2.at[l, 0:5], arsem_r.at[l, 1])

            @pl.when(jnp.logical_not(active))
            def _():
                await_bytes(a2.at[l], arsem_r.at[l, 1])

            total = a2[l, 0].astype(F32)
            for s in range(1, GROUPS):
                total = total + a2[l, s].astype(F32)
            here = pl.ds(t * CHUNK, CHUNK)
            gf[l, here] = total.astype(BF)

            @pl.loop(1, 32)
            def _(i):
                send(gf.at[l, here], gf.at[l, here], arsem_s.at[l, 2], arsem_r.at[l, 2], (k, (t + i) % 32))

    def reduce_drain(l):
        @pl.when(owner)
        def _():
            await_bytes(gf.at[l, 0 : (OWNERS - 1) * CHUNK], arsem_r.at[l, 2])
            await_bytes(a1.at[l], arsem_s.at[l, 2])

            @pl.when(active)
            def _():
                await_bytes(gb.at[l, 0 : (OWNERS - 1) * CHUNK], arsem_s.at[l, 0])
                await_bytes(a1.at[l, 0:7], arsem_s.at[l, 1])

        @pl.when(jnp.logical_not(owner))
        def _():
            await_bytes(gf.at[l], arsem_r.at[l, 2])

            @pl.when(active)
            def _():
                await_bytes(gb.at[l], arsem_s.at[l, 0])

    fetches = [
        pltpu.make_async_copy(src, dst, insem.at[n])
        for n, (src, dst) in enumerate((
            (act_h, act), (w1_h, wst.at[0]), (spread_h, spread), (nbr_h, nbr), (trn_h, trn),
            (w2_h, wst.at[1]), (w3_h, wst.at[2]), (cot_h, cot),
        ))
    ]

    @pl.when(active)
    def _():
        for fetch in fetches:
            fetch.start()
        place = lax.broadcasted_iota(jnp.int32, (CELLS, TW * TH), 0)
        given = lax.broadcasted_iota(jnp.int32, (CELLS, TW * TH), 1)
        order[...] = jnp.where((given % TH) * PITCH + given // TH == place, 1.0, 0.0).astype(BF)
        build_sel()
        z[...] = jnp.zeros_like(z)
        up[...] = jnp.zeros_like(up)
        sg[...] = jnp.zeros_like(sg)
        fetches[0].wait()
        for f in range(2):
            z[0, f, :CELLS] = reorder(act[f]).astype(BF)

    across, along = edges[0] | edges[1], edges[2] | edges[3]
    counts = ((active & across & along, 3), (active & ((along & jnp.logical_not(across)) | gathers), 2), (active & across & jnp.logical_not(along), 1))
    extra = jnp.bool_(False)
    for cond, n in counts:
        extra = extra | cond

        @pl.when(cond)
        def _():
            pl.semaphore_wait(barrier, 38 + n * (GROUPS - 1))

    @pl.when(jnp.logical_not(extra))
    def _():
        pl.semaphore_wait(barrier, 38)

    @pl.when(active)
    def _():
        @pl.loop(0, 3)
        def _(l):
            exchange_send(l, z.at[l])

            @pl.when(l == 0)
            def _():
                for fetch in fetches[1:]:
                    fetch.wait()
                for face in range(FACES):
                    for e in range(4):
                        code = trn[e, face]
                        pick_at[face, e] = (code % 4) * 4 + (code // 4) * 2 + nbr[e, face] % 2

            @pl.when(l > 0)
            def _():
                finish(l - 1)

            collect(l)
            halo_local(l, z.at[l])
            for f in range(2):
                widen(f, z.at[l], xf.at[l])
                total = None
                for dy in range(3):
                    part = jnp.dot(
                        xf[l, f, dy * PITCH : dy * PITCH + CELLS, :],
                        wst[l, 3 * dy : 3 * dy + 3].reshape(3 * C, C), preferred_element_type=F32,
                    )
                    total = part if total is None else total + part
                up[f] = total
            correct(l, forward_taps(l))
            for f in range(2):
                hidden, tilt = gelu_parts(up[f])
                slope[l, f] = tilt
                z[l + 1, f, :CELLS] = hidden.astype(BF)

        for f in range(2):
            up[f] = reorder(cot[f])

        @pl.loop(0, 3)
        def _(i):
            l = 2 - i
            x = 3 + i
            d = z.at[3]
            for f in range(2):
                d[f, :CELLS] = (up[f] * slope[l, f]).astype(BF)
            exchange_send(x, d)

            @pl.when(i == 0)
            def _():
                finish(2)
                for n in range(3):
                    for tap in range(9):
                        wbk[n, tap] = wst[n, tap].astype(F32).T.astype(BF)

            for dy in range(3):
                total = None
                for f in range(2):
                    part = lax.dot_general(
                        xf[l, f, dy * PITCH : dy * PITCH + CELLS, :], d[f, :CELLS],
                        (((0,), (0,)), ((), ())), preferred_element_type=F32,
                    )
                    total = part if total is None else total + part
                gb[l, dy * 3 * C : (dy + 1) * 3 * C] = total.astype(BF)

            @pl.when(i == 2)
            def _():
                reduce_send(l)

            @pl.when(i > 0)
            def _():
                reduce_mid(l + 1)

            collect(x)

            @pl.when(i < 2)
            def _():
                reduce_send(l)

            @pl.when(i == 2)
            def _():
                reduce_mid(l)

            @pl.when(i > 0)
            def _():
                reduce_last(l + 1)

            halo_local(x, d)
            for f in range(2):
                widen(f, d, xb)
                total = None
                for dy in range(3):
                    for dx in range(3):
                        part = jnp.dot(
                            xb[f, dy * PITCH : dy * PITCH + CELLS, dx * C : (dx + 1) * C], wbk[l, 8 - 3 * dy - dx],
                            preferred_element_type=F32,
                        )
                        total = part if total is None else total + part
                up[f] = total

            @pl.when(i == 2)
            def _():
                reduce_last(l)

            correct(x, backward_taps(l))

        for f in range(2):
            gin[f] = lax.dot_general(
                order[...], up[f].astype(BF), (((0,), (0,)), ((), ())), preferred_element_type=F32
            ).astype(BF)

        @pl.loop(0, 6)
        def _(x):
            sent(x)

    @pl.when(jnp.logical_not(active))
    def _():
        gin[...] = jnp.zeros_like(gin)
        reduce_last(2)
        reduce_last(1)
        reduce_last(0)

    for l in range(3):
        reduce_drain(l)
        grads[l] = gf[l]


def shards(activation, cotangent, weight_one, weight_two, weight_three, neighbor, turn):
    def flipped(field):
        return field.transpose(0, 1, 3, 2, 4).reshape(2, TW * TH, C)

    vmem = pl.BlockSpec(memory_space=pltpu.VMEM)
    hbm = pl.BlockSpec(memory_space=pltpu.HBM)
    dma = pltpu.SemaphoreType.DMA
    gin, grads = pl.pallas_call(
        kernel,
        out_shape=(
            jax.ShapeDtypeStruct((2, TW * TH, C), BF),
            jax.ShapeDtypeStruct((3, 9 * C, C), BF),
        ),
        in_specs=[hbm] * 8,
        out_specs=(vmem, vmem),
        scratch_shapes=[
            pltpu.SMEM((4, FACES), jnp.int32),
            pltpu.SMEM((4, FACES), jnp.int32),
            pltpu.SMEM((FACES, 4), jnp.int32),
            pltpu.VMEM((2, TW * TH, C), BF),
            pltpu.VMEM((2, TW * TH, C), BF),
            pltpu.VMEM((3 * ROWS, KZ), BF),
            pltpu.VMEM((CELLS, TW * TH), BF),
            pltpu.VMEM((28 * 16, CELLS), BF),
            pltpu.VMEM((4, 2, KZ, C), BF),
            pltpu.VMEM((3, 2, ROWS, 3 * C), BF),
            pltpu.VMEM((2, ROWS, 3 * C), BF),
            pltpu.VMEM((3, 2, CELLS, C), F32),
            pltpu.VMEM((2, CELLS, C), F32),
            pltpu.VMEM((3, 9, C, C), BF),
            pltpu.VMEM((3, 9, C, C), BF),
            pltpu.VMEM((8, 64, C), F32),
            pltpu.VMEM((8, 2, 16, C), BF),
            pltpu.VMEM((6, 28, 2, 16, C), BF),
            pltpu.VMEM((6, 10, 2, 16, C), BF),
            pltpu.VMEM((6, 20, 2, 16, C), BF),
            pltpu.VMEM((6, 16, 2, 16, C), BF),
            pltpu.VMEM((6, 2, GROUPS, 2, 16, C), BF),
            pltpu.VMEM((6, 2, GROUPS, 2, 16, C), BF),
            pltpu.VMEM((6, GROUPS, 2, 16, C), BF),
            pltpu.VMEM((6, GROUPS, 2, 2, 16, C), BF),
            pltpu.VMEM((3, 9 * C, C), BF),
            pltpu.VMEM((3, 31, CHUNK, C), BF),
            pltpu.VMEM((3, CHUNK, C), BF),
            pltpu.VMEM((3, GROUPS, CHUNK, C), BF),
            pltpu.VMEM((3, 9 * C, C), BF),
            dma((8,)),
            dma((6, 4)),
            dma((6, 4)),
            dma((6,)),
            dma((6,)),
            dma((6, 2)),
            dma((6, 2)),
            dma((3, 3)),
            dma((3, 3)),
        ],
        compiler_params=pltpu.CompilerParams(
            collective_id=0, has_side_effects=True, vmem_limit_bytes=62 * 1024 * 1024
        ),
        name="glued_convolutions",
    )(
        neighbor.T, turn.T, flipped(activation), flipped(cotangent), weight_one, weight_two, weight_three,
        jnp.asarray(spread_matrix(), BF),
    )
    grad_input = gin.reshape(2, 1, TW, TH, C).transpose(0, 1, 3, 2, 4)
    scaled = grads.reshape(3, 9, C, C).astype(F32) * (1.0 / math.sqrt(FACES * NS * NS))
    return grad_input, scaled[0], scaled[1], scaled[2]


def solution(mesh):
    field = P("face", "tile", None, None, None)
    return jax.shard_map(
        shards,
        mesh=mesh,
        in_specs=(field, field, P(), P(), P(), P(), P()),
        out_specs=(field, P(), P(), P()),
        check_vma=False,
    )
```

```python
import math

import jax
import jax.numpy as jnp
import numpy as np
from jax import lax
from jax.experimental import pallas as pl
from jax.experimental.pallas import tpu as pltpu
from jax.sharding import PartitionSpec as P

FACES = 12
TGR = 4
TGC = 8
TILES = 32
TH = 24
TW = 12
C = 128
NS = 96
PITCH = 16
CELLS = TH * PITCH
GROUPS = 6
OWNERS = 24
CHUNK = 9 * C // OWNERS
KZ = 512
ROWS = 26 * PITCH
MESH = pl.DeviceIdType.MESH
BF = jnp.bfloat16
F32 = jnp.float32
TAP_TABLE = ((0, 1, 2), (6, 7, 8), (0, 3, 6), (2, 5, 8))


def spread_matrix():
    out = np.zeros((3, ROWS, KZ), np.float32)
    top, bottom, left, right = CELLS, CELLS + 16, CELLS + 32, CELLS + 64
    for dx in range(3):
        for yy in range(26):
            for x in range(TW):
                y, xx = yy - 1, x + dx - 1
                row = out[dx, yy * PITCH + x]
                inside_y, inside_x = 0 <= y < TH, 0 <= xx < TW
                if inside_y and inside_x:
                    row[y * PITCH + xx] = 1
                if y == -1:
                    row[top + xx + 1] = 1
                if y == TH:
                    row[bottom + xx + 1] = 1
                if not inside_x:
                    side = left if xx < 0 else right
                    row[side + (y + 1 if y < TW else 16 + y - TW + 1)] = 1
    return out.reshape(3 * ROWS, KZ)


def gelu(x):
    c = math.sqrt(2.0 / math.pi)
    return x * (0.5 * (1.0 + jnp.tanh(c * x * (1.0 + 0.044715 * (x * x)))))


def gelu_slope(x):
    c = math.sqrt(2.0 / math.pi)
    sq = x * x
    t = jnp.tanh(c * x * (1.0 + 0.044715 * sq))
    return 0.5 * (1.0 + t) + 0.5 * x * (1.0 - t * t) * (c * (1.0 + 3.0 * 0.044715 * sq))


def kernel(
    nbr_h, trn_h, act_h, cot_h, w1_h, w2_h, w3_h, spread_h,
    gin, grads,
    nbr, trn, pick_at, act, cot, spread, order, sel, z, xf, xb, slope, up, wst, wbk, sg, line,
    s1, nb, cr, cc, s2r, s2c, d2r, d2c, gb, a1, pb, a2, gf,
    insem, s1sem, nsem, crsem, ccsem, s2sem, d2sem, arsem_s, arsem_r,
):
    k = lax.axis_index("face")
    t = lax.axis_index("tile")
    row = t // TGC
    col = t % TGC
    active = k < GROUPS
    owner = t < OWNERS
    spreads = owner & (t // (OWNERS // 2) == k % 2)
    mate = k + 1 - 2 * (k % 2)
    edges = (row == 0, row == TGR - 1, col == 0, col == TGC - 1)
    gathers = (row >= 1) & (row <= 2) & (((col >= 1) & (col <= 2)) | ((col >= 5) & (col <= 6)))
    served = 2 * (row - 1) + col // 4
    part = (col - 1 + (col // 4) * (7 - 2 * col)) % 2
    lines_up = (edges[0] & (col % 2 == 0)) | (edges[1] & (col % 2 == 1))

    barrier = pltpu.get_barrier_semaphore()
    for i in range(1, 8):
        pl.semaphore_signal(barrier, inc=1, device_id=((k + i) % 8, t), device_id_type=MESH)

    @pl.loop(1, 32)
    def _(i):
        pl.semaphore_signal(barrier, inc=1, device_id=(k, (t + i) % 32), device_id_type=MESH)

    def gatherer(r, h):
        return (1 + r // 2) * TGC + 1 + h + (r % 2) * (5 - 2 * h)

    def aligner(w):
        return (w % 2) * (TILES - TGC) + w

    def greet(tile):
        for i in range(1, GROUPS):
            pl.semaphore_signal(barrier, inc=1, device_id=((k + i) % GROUPS, tile), device_id_type=MESH)

    for e in range(2):
        @pl.when(active & edges[e])
        def _():
            greet((1 - e) * (TILES - TGC) + col)

    @pl.when(active & (edges[2] | edges[3]))
    def _():
        greet(gatherer(row, 0))
        greet(gatherer(row, 1))

    @pl.when(active & gathers)
    def _():
        for far in range(2):
            greet(served * TGC + (TGC - 1) * far)

    def send(src, dst, ssem, rsem, dev):
        pltpu.make_async_remote_copy(
            src_ref=src, dst_ref=dst, send_sem=ssem, recv_sem=rsem, device_id=dev, device_id_type=MESH
        ).start()

    def await_bytes(ref, sem):
        pltpu.make_async_copy(ref, ref, sem).wait()

    def reorder(cells):
        return jnp.dot(order[...], cells, preferred_element_type=F32)

    def mine(f):
        return jnp.minimum(2 * k + f, FACES - 1)

    slots = []
    for e in (0, 1):
        for i in range(3):
            slots.append((e, (col + 7 + i) % 8, False))
        for i in range(3):
            slots.append((e, (14 - col + i) % 8, True))
    for e in (2, 3):
        for i in range(4):
            slots.append((e, (2 * row + 7 + i) % 8, False))
        for i in range(4):
            slots.append((e, (13 - 2 * row + i) % 8, True))

    def build_sel():
        j = lax.broadcasted_iota(jnp.int32, (16, CELLS), 0)
        cell = lax.broadcasted_iota(jnp.int32, (16, CELLS), 1)
        for n, (e, w, rev) in enumerate(slots):
            pos = (96 - 12 * w) - j if rev else (12 * w - 1) + j
            local = pos - (12 * col if e < 2 else 24 * row)
            size = TW if e < 2 else TH
            base = (0, (TH - 1) * PITCH, 0, TW - 1)[e]
            stride = 1 if e < 2 else PITCH
            ok = (local >= 0) & (local < size) & (j < 14) & (cell == base + local * stride)
            sel[n * 16 : n * 16 + 16, :] = jnp.where(ok, 1.0, 0.0).astype(BF)

    def messages(x, e):
        span = 3 if e < 2 else 4
        first = 6 * e if e < 2 else 12 + 8 * (e - 2)
        for o in range(2):
            for i in range(span):
                n = first + span * o + i
                w = slots[n][1]
                h = w % 2
                at = 6 * e + 3 * o + i if e < 2 else 12 + 4 * (e - 2) + 2 * o + i // 2
                yield True, None, n, cr.at[x, at], crsem.at[x], aligner(w)
                tile = gatherer(w // 2, h)
                if e >= 2:
                    yield False, None, n, cc.at[x, 8 + 4 * (e - 2) + 2 * o + i // 2], ccsem.at[x], tile
                elif i == 0:
                    yield False, h == 1, n, cc.at[x, 4 * e + 2 * o], ccsem.at[x], tile
                elif i == 1:
                    yield False, None, n, cc.at[x, 4 * e + 2 * o + h], ccsem.at[x], tile
                else:
                    yield False, h == 0, n, cc.at[x, 4 * e + 2 * o + 1], ccsem.at[x], tile

    def exchange_send(x, v):
        for f in range(2):
            cut = jnp.dot(sel[...], v[f, :CELLS], preferred_element_type=F32)
            s1[x, :, f] = cut.astype(BF).reshape(28, 16, C)

        for e in range(4):
            @pl.when(edges[e])
            def _():
                for stays, cond, n, dst, sem, tile in messages(x, e):
                    if stays:
                        @pl.when(tile != t)
                        def _():
                            send(s1.at[x, n], dst, s1sem.at[x, e], sem, (k, tile))

                        @pl.when(tile == t)
                        def _():
                            pltpu.make_async_copy(s1.at[x, n], dst, sem).start()
                    elif cond is None:
                        send(s1.at[x, n], dst, s1sem.at[x, e], sem, (k, tile))
                    else:
                        @pl.when(cond)
                        def _():
                            send(s1.at[x, n], dst, s1sem.at[x, e], sem, (k, tile))

        @pl.when(row > 0)
        def _():
            for i in range(3):
                send(s1.at[x, i], nb.at[x, 3 + i], s1sem.at[x, 0], nsem.at[x, 1], (k, (row - 1) * TGC + slots[i][1]))

        @pl.when(row < TGR - 1)
        def _():
            for i in range(3):
                send(s1.at[x, 6 + i], nb.at[x, i], s1sem.at[x, 1], nsem.at[x, 0], (k, (row + 1) * TGC + slots[i][1]))

        @pl.when(col > 0)
        def _():
            send(s1.at[x, 13:15], nb.at[x, 8:10], s1sem.at[x, 2], nsem.at[x, 3], (k, t - 1))

        @pl.when(col < TGC - 1)
        def _():
            send(s1.at[x, 21:23], nb.at[x, 6:8], s1sem.at[x, 3], nsem.at[x, 2], (k, t + 1))

    def sent(x):
        for e in range(4):
            first = 6 * e if e < 2 else 13 + 8 * (e - 2)

            @pl.when(edges[e])
            def _():
                for stays, cond, n, dst, sem, tile in messages(x, e):
                    if stays:
                        cond = tile != t
                    if cond is None:
                        await_bytes(s1.at[x, n], s1sem.at[x, e])
                    else:
                        @pl.when(cond)
                        def _():
                            await_bytes(s1.at[x, n], s1sem.at[x, e])

            @pl.when(jnp.logical_not(edges[e]))
            def _():
                await_bytes(s1.at[x, first : first + (3 if e < 2 else 2)], s1sem.at[x, e])

        @pl.when(gathers)
        def _():
            await_bytes(s2c.at[x], s2sem.at[x, 1])

        @pl.when(lines_up)
        def _():
            await_bytes(s2r.at[x, 0], s2sem.at[x, 0])
            await_bytes(s2r.at[x, 1, 0:5], s2sem.at[x, 0])

    def collect(x):
        def lines(buf, row_first, row_count, col_first):
            for e in range(4):
                for o in range(2):
                    if e < 2:
                        first, count = row_first(e, o), row_count
                    else:
                        first, count = col_first(e, o), 2
                    total = buf[first]
                    for n in range(1, count):
                        total = total + buf[first + n]
                    line[2 * e + o] = total

        def pick(face, e):
            at = pick_at[face, e]
            return line[at // 2, at % 2]

        @pl.when(lines_up)
        def _():
            await_bytes(cr.at[x], crsem.at[x])
            lines(cr.at[x], lambda e, o: 6 * e + 3 * o, 3, lambda e, o: 12 + 4 * (e - 2) + 2 * o)
            for e in range(2):
                tile = (TILES - TGC) * e + col
                for g in range(GROUPS):
                    for f in range(2):
                        s2r[x, e, g, f] = pick(2 * g + f, e)
                for i in range(1, GROUPS):
                    g = (k + i) % GROUPS
                    send(s2r.at[x, e, g], d2r.at[x, k], s2sem.at[x, 0], d2sem.at[x, 0], (g, tile))

                @pl.when(tile != t)
                def _():
                    send(s2r.at[x, e, k], d2r.at[x, k], s2sem.at[x, 0], d2sem.at[x, 0], (k, tile))

                @pl.when(tile == t)
                def _():
                    pltpu.make_async_copy(s2r.at[x, e, k], d2r.at[x, k], d2sem.at[x, 0]).start()

        @pl.when(gathers)
        def _():
            await_bytes(cc.at[x], ccsem.at[x])
            lines(cc.at[x], lambda e, o: 4 * e + 2 * o, 2, lambda e, o: 8 + 4 * (e - 2) + 2 * o)
            for far in range(2):
                there = served * TGC + (TGC - 1) * far
                for g in range(GROUPS):
                    for f in range(2):
                        s2c[x, far, g, f] = pick(2 * g + f, 2 + far)
                for i in range(GROUPS):
                    g = (k + i) % GROUPS
                    send(s2c.at[x, far, g], d2c.at[x, k, part], s2sem.at[x, 1], d2sem.at[x, 1], (g, there))

    def arrived(x, e, f, h=0):
        group = nbr[e, mine(f)] // 2
        out = None
        for g in range(GROUPS):
            win = d2r[x, g, f] if e < 2 else d2c[x, g, h, f]
            out = win if out is None else jnp.where(group == g, win, out)
        return out

    def halo_local(x, v):
        for side in (0, 1):
            at = CELLS + 16 * side

            @pl.when(jnp.logical_not(edges[side]))
            def _():
                await_bytes(nb.at[x, 3 * side : 3 * side + 3], nsem.at[x, side])
                for f in range(2):
                    v[f, at : at + 16] = nb[x, 3 * side, f] + nb[x, 3 * side + 1, f] + nb[x, 3 * side + 2, f]

            @pl.when(edges[side])
            def _():
                for f in range(2):
                    v[f, at : at + 16] = jnp.zeros((16, C), BF)

        for side in (0, 1):
            at = CELLS + 32 + 32 * side

            @pl.when(jnp.logical_not(edges[2 + side]))
            def _():
                await_bytes(nb.at[x, 6 + 2 * side : 8 + 2 * side], nsem.at[x, 2 + side])
                for f in range(2):
                    for h in range(2):
                        v[f, at + 16 * h : at + 16 * h + 16] = nb[x, 6 + 2 * side + h, f]

            @pl.when(edges[2 + side])
            def _():
                for f in range(2):
                    v[f, at : at + 32] = jnp.zeros((32, C), BF)

    def widen(f, v, out):
        for dx in range(3):
            part = jnp.dot(spread[dx * ROWS : (dx + 1) * ROWS, :], v[f], preferred_element_type=F32)
            out[f, :, dx * C : (dx + 1) * C] = part.astype(BF)

    def finish(l):
        v = z.at[l]
        for e in range(4):
            @pl.when(edges[e])
            def _():
                for f in range(2):
                    if e < 2:
                        at = CELLS + 16 * e
                        v[f, at : at + 16] = arrived(l, e, f)
                    else:
                        for h in range(2):
                            at = CELLS + 32 + 32 * (e - 2) + 16 * h
                            v[f, at : at + 16] = arrived(l, e, f, h)

        @pl.when(edges[0] | edges[1] | edges[2] | edges[3])
        def _():
            for f in range(2):
                widen(f, v, xf.at[l])

    def correct(x, weights):
        for e in range(4):
            @pl.when(edges[e])
            def _():
                if e < 2:
                    await_bytes(d2r.at[x], d2sem.at[x, 0])
                else:
                    await_bytes(d2c.at[x], d2sem.at[x, 1])
                size = 16 if e < 2 else 32
                for f in range(2):
                    win = sg.at[2 * e + f]
                    win[0:16] = arrived(x, e, f, 0).astype(F32)
                    if e >= 2:
                        win[48:64] = arrived(x, e, f, 1).astype(F32)
                        win[13:26] = win[49:62]
                moved = []
                for f in range(2):
                    more = None
                    for s, weight in enumerate(weights(f, e)):
                        part = jnp.dot(sg[2 * e + f, s : s + size].astype(BF), weight, preferred_element_type=F32)
                        more = part if more is None else more + part
                    moved.append(more)
                for f, more in enumerate(moved):
                    if e < 2:
                        at = 0 if e == 0 else CELLS - PITCH
                        up[f, at : at + 16] = up[f, at : at + 16] + more
                    else:
                        where = pl.ds(0 if e == 2 else TW - 1, TH, stride=PITCH)
                        up[f, where, :] = up[f, where, :] + more[0:TH]

    def forward_taps(l):
        return lambda f, e: [wst[l, tap] for tap in TAP_TABLE[e]]

    def backward_taps(l):
        def weights(f, e):
            code = trn[e, mine(f)]
            other, rev = code % 4, code // 4
            first = jnp.where(other == 1, 6, jnp.where(other == 3, 2, 0))
            step = jnp.where(other < 2, 1, 3)
            out = []
            for s in range(3):
                order = jnp.where(rev == 1, s, 2 - s)
                out.append(wbk[l, first + step * order])
            return out

        return weights

    def reduce_send(l):
        @pl.loop(1, 32)
        def _(i):
            dst = (t + i) % 32

            @pl.when(dst < OWNERS)
            def _():
                send(
                    gb.at[l, pl.ds(dst * CHUNK, CHUNK)], a1.at[l, 31 - i],
                    arsem_s.at[l, 0], arsem_r.at[l, 0], (k, dst),
                )

    def reduce_mid(l):
        @pl.when(owner)
        def _():
            await_bytes(a1.at[l], arsem_r.at[l, 0])
            total = gb[l, pl.ds(t * CHUNK, CHUNK)].astype(F32)
            for s in range(31):
                total = total + a1[l, s].astype(F32)
            pb[l] = total.astype(BF)
            for i in range(1, 4):
                there = (2 * (k // 2) + 2 * i) % 8 + t // (OWNERS // 2)
                send(pb.at[l], a2.at[l, k], arsem_s.at[l, 1], arsem_r.at[l, 1], (there, t))

            @pl.when(spreads)
            def _():
                a2[l, k] = pb[l]

            @pl.when(jnp.logical_not(spreads))
            def _():
                send(pb.at[l], a2.at[l, k], arsem_s.at[l, 1], arsem_r.at[l, 1], (mate, t))

    def reduce_last(l):
        @pl.when(spreads)
        def _():
            @pl.when(active)
            def _():
                await_bytes(a2.at[l, 0:5], arsem_r.at[l, 1])

            @pl.when(jnp.logical_not(active))
            def _():
                await_bytes(a2.at[l], arsem_r.at[l, 1])

            total = a2[l, 0].astype(F32)
            for s in range(1, GROUPS):
                total = total + a2[l, s].astype(F32)
            here = pl.ds(t * CHUNK, CHUNK)
            gf[l, here] = total.astype(BF)

            @pl.loop(1, 32)
            def _(i):
                send(gf.at[l, here], gf.at[l, here], arsem_s.at[l, 2], arsem_r.at[l, 2], (k, (t + i) % 32))

    def reduce_swap(l):
        here = (k % 2) * (OWNERS // 2) * CHUNK
        half = gf.at[l, pl.ds(here, OWNERS // 2 * CHUNK)]

        @pl.when(spreads)
        def _():
            await_bytes(gf.at[l, 0 : (OWNERS // 2 - 1) * CHUNK], arsem_r.at[l, 2])

        @pl.when(jnp.logical_not(spreads))
        def _():
            await_bytes(gf.at[l, 0 : OWNERS // 2 * CHUNK], arsem_r.at[l, 2])

        send(half, half, arsem_s.at[l, 3], arsem_r.at[l, 3], (mate, t))

    def reduce_drain(l):
        await_bytes(gf.at[l, 0 : OWNERS // 2 * CHUNK], arsem_r.at[l, 3])
        await_bytes(gf.at[l, 0 : OWNERS // 2 * CHUNK], arsem_s.at[l, 3])

        @pl.when(spreads)
        def _():
            await_bytes(a1.at[l], arsem_s.at[l, 2])

        @pl.when(active & owner)
        def _():
            await_bytes(gb.at[l, 0 : (OWNERS - 1) * CHUNK], arsem_s.at[l, 0])

        @pl.when(active & jnp.logical_not(owner))
        def _():
            await_bytes(gb.at[l], arsem_s.at[l, 0])

        @pl.when(active & spreads)
        def _():
            await_bytes(a1.at[l, 0:3], arsem_s.at[l, 1])

        @pl.when(active & owner & jnp.logical_not(spreads))
        def _():
            await_bytes(a1.at[l, 0:4], arsem_s.at[l, 1])

    fetches = [
        pltpu.make_async_copy(src, dst, insem.at[n])
        for n, (src, dst) in enumerate((
            (act_h, act), (w1_h, wst.at[0]), (spread_h, spread), (nbr_h, nbr), (trn_h, trn),
            (w2_h, wst.at[1]), (w3_h, wst.at[2]), (cot_h, cot),
        ))
    ]

    @pl.when(active)
    def _():
        for fetch in fetches:
            fetch.start()
        place = lax.broadcasted_iota(jnp.int32, (CELLS, TW * TH), 0)
        given = lax.broadcasted_iota(jnp.int32, (CELLS, TW * TH), 1)
        order[...] = jnp.where((given % TH) * PITCH + given // TH == place, 1.0, 0.0).astype(BF)
        build_sel()
        z[...] = jnp.zeros_like(z)
        up[...] = jnp.zeros_like(up)
        sg[...] = jnp.zeros_like(sg)
        fetches[0].wait()
        for f in range(2):
            z[0, f, :CELLS] = reorder(act[f]).astype(BF)

    across, along = edges[0] | edges[1], edges[2] | edges[3]
    counts = ((active & across & along, 3), (active & ((along & jnp.logical_not(across)) | gathers), 2), (active & across & jnp.logical_not(along), 1))
    extra = jnp.bool_(False)
    for cond, n in counts:
        extra = extra | cond

        @pl.when(cond)
        def _():
            pl.semaphore_wait(barrier, 38 + n * (GROUPS - 1))

    @pl.when(jnp.logical_not(extra))
    def _():
        pl.semaphore_wait(barrier, 38)

    @pl.when(active)
    def _():
        @pl.loop(0, 3)
        def _(l):
            exchange_send(l, z.at[l])

            @pl.when(l == 0)
            def _():
                for fetch in fetches[1:]:
                    fetch.wait()
                for face in range(FACES):
                    for e in range(4):
                        code = trn[e, face]
                        pick_at[face, e] = (code % 4) * 4 + (code // 4) * 2 + nbr[e, face] % 2

            @pl.when(l > 0)
            def _():
                for f in range(2):
                    slope[l - 1, f] = gelu_slope(up[f])
                finish(l - 1)

            collect(l)
            halo_local(l, z.at[l])
            for f in range(2):
                widen(f, z.at[l], xf.at[l])
                total = None
                for dy in range(3):
                    part = jnp.dot(
                        xf[l, f, dy * PITCH : dy * PITCH + CELLS, :],
                        wst[l, 3 * dy : 3 * dy + 3].reshape(3 * C, C), preferred_element_type=F32,
                    )
                    total = part if total is None else total + part
                up[f] = total
            correct(l, forward_taps(l))

            @pl.when(l < 2)
            def _():
                for f in range(2):
                    z[l + 1, f, :CELLS] = gelu(up[f]).astype(BF)

        for f in range(2):
            slope[2, f] = gelu_slope(up[f])
            up[f] = reorder(cot[f])

        @pl.loop(0, 3)
        def _(i):
            l = 2 - i
            x = 3 + i
            d = z.at[3]
            for f in range(2):
                d[f, :CELLS] = (up[f] * slope[l, f]).astype(BF)
            exchange_send(x, d)

            @pl.when(i == 0)
            def _():
                finish(2)
                for n in range(3):
                    for tap in range(9):
                        wbk[n, tap] = wst[n, tap].astype(F32).T.astype(BF)

            for dy in range(3):
                total = None
                for f in range(2):
                    part = lax.dot_general(
                        xf[l, f, dy * PITCH : dy * PITCH + CELLS, :], d[f, :CELLS],
                        (((0,), (0,)), ((), ())), preferred_element_type=F32,
                    )
                    total = part if total is None else total + part
                gb[l, dy * 3 * C : (dy + 1) * 3 * C] = total.astype(BF)

            @pl.when(i == 2)
            def _():
                reduce_send(l)

            @pl.when(i > 0)
            def _():
                reduce_mid(l + 1)

            collect(x)

            @pl.when(i < 2)
            def _():
                reduce_send(l)

            @pl.when(i == 2)
            def _():
                reduce_mid(l)

            @pl.when(i > 0)
            def _():
                reduce_last(l + 1)

            halo_local(x, d)
            for f in range(2):
                widen(f, d, xb)
                total = None
                for dy in range(3):
                    for dx in range(3):
                        part = jnp.dot(
                            xb[f, dy * PITCH : dy * PITCH + CELLS, dx * C : (dx + 1) * C], wbk[l, 8 - 3 * dy - dx],
                            preferred_element_type=F32,
                        )
                        total = part if total is None else total + part
                up[f] = total

            @pl.when(i == 2)
            def _():
                reduce_last(l)

            correct(x, backward_taps(l))

        for f in range(2):
            gin[f] = lax.dot_general(
                order[...], up[f].astype(BF), (((0,), (0,)), ((), ())), preferred_element_type=F32
            ).astype(BF)

        @pl.loop(0, 6)
        def _(x):
            sent(x)

    @pl.when(jnp.logical_not(active))
    def _():
        gin[...] = jnp.zeros_like(gin)
        reduce_last(2)
        reduce_last(1)
        reduce_last(0)

    for l in (2, 1, 0):
        reduce_swap(l)
    for l in (2, 1, 0):
        reduce_drain(l)
        grads[l] = gf[l]


def shards(activation, cotangent, weight_one, weight_two, weight_three, neighbor, turn):
    def flipped(field):
        return field.transpose(0, 1, 3, 2, 4).reshape(2, TW * TH, C)

    vmem = pl.BlockSpec(memory_space=pltpu.VMEM)
    hbm = pl.BlockSpec(memory_space=pltpu.HBM)
    dma = pltpu.SemaphoreType.DMA
    gin, grads = pl.pallas_call(
        kernel,
        out_shape=(
            jax.ShapeDtypeStruct((2, TW * TH, C), BF),
            jax.ShapeDtypeStruct((3, 9 * C, C), BF),
        ),
        in_specs=[hbm] * 8,
        out_specs=(vmem, vmem),
        scratch_shapes=[
            pltpu.SMEM((4, FACES), jnp.int32),
            pltpu.SMEM((4, FACES), jnp.int32),
            pltpu.SMEM((FACES, 4), jnp.int32),
            pltpu.VMEM((2, TW * TH, C), BF),
            pltpu.VMEM((2, TW * TH, C), BF),
            pltpu.VMEM((3 * ROWS, KZ), BF),
            pltpu.VMEM((CELLS, TW * TH), BF),
            pltpu.VMEM((28 * 16, CELLS), BF),
            pltpu.VMEM((4, 2, KZ, C), BF),
            pltpu.VMEM((3, 2, ROWS, 3 * C), BF),
            pltpu.VMEM((2, ROWS, 3 * C), BF),
            pltpu.VMEM((3, 2, CELLS, C), F32),
            pltpu.VMEM((2, CELLS, C), F32),
            pltpu.VMEM((3, 9, C, C), BF),
            pltpu.VMEM((3, 9, C, C), BF),
            pltpu.VMEM((8, 64, C), F32),
            pltpu.VMEM((8, 2, 16, C), BF),
            pltpu.VMEM((6, 28, 2, 16, C), BF),
            pltpu.VMEM((6, 10, 2, 16, C), BF),
            pltpu.VMEM((6, 20, 2, 16, C), BF),
            pltpu.VMEM((6, 16, 2, 16, C), BF),
            pltpu.VMEM((6, 2, GROUPS, 2, 16, C), BF),
            pltpu.VMEM((6, 2, GROUPS, 2, 16, C), BF),
            pltpu.VMEM((6, GROUPS, 2, 16, C), BF),
            pltpu.VMEM((6, GROUPS, 2, 2, 16, C), BF),
            pltpu.VMEM((3, 9 * C, C), BF),
            pltpu.VMEM((3, 31, CHUNK, C), BF),
            pltpu.VMEM((3, CHUNK, C), BF),
            pltpu.VMEM((3, GROUPS, CHUNK, C), BF),
            pltpu.VMEM((3, 9 * C, C), BF),
            dma((8,)),
            dma((6, 4)),
            dma((6, 4)),
            dma((6,)),
            dma((6,)),
            dma((6, 2)),
            dma((6, 2)),
            dma((3, 4)),
            dma((3, 4)),
        ],
        compiler_params=pltpu.CompilerParams(
            collective_id=0, has_side_effects=True, vmem_limit_bytes=62 * 1024 * 1024
        ),
        name="glued_convolutions",
    )(
        neighbor.T, turn.T, flipped(activation), flipped(cotangent), weight_one, weight_two, weight_three,
        jnp.asarray(spread_matrix(), BF),
    )
    grad_input = gin.reshape(2, 1, TW, TH, C).transpose(0, 1, 3, 2, 4)
    scaled = grads.reshape(3, 9, C, C).astype(F32) * (1.0 / math.sqrt(FACES * NS * NS))
    return grad_input, scaled[0], scaled[1], scaled[2]


def solution(mesh):
    field = P("face", "tile", None, None, None)
    return jax.shard_map(
        shards,
        mesh=mesh,
        in_specs=(field, field, P(), P(), P(), P(), P()),
        out_specs=(field, P(), P(), P()),
        check_vma=False,
    )
```

```python
import math

import jax
import jax.numpy as jnp
import numpy as np
from jax import lax
from jax.experimental import pallas as pl
from jax.experimental.pallas import tpu as pltpu
from jax.sharding import PartitionSpec as P

FACES = 12
TGR = 4
TGC = 8
TILES = 32
TH = 24
TW = 12
C = 128
NS = 96
PITCH = 16
CELLS = TH * PITCH
GROUPS = 6
OWNERS = 24
CHUNK = 9 * C // OWNERS
KZ = 512
ROWS = 26 * PITCH
MESH = pl.DeviceIdType.MESH
BF = jnp.bfloat16
F32 = jnp.float32
TAP_TABLE = ((0, 1, 2), (6, 7, 8), (0, 3, 6), (2, 5, 8))


def spread_matrix():
    out = np.zeros((3, ROWS, KZ), np.float32)
    top, bottom, left, right = CELLS, CELLS + 16, CELLS + 32, CELLS + 64
    for dx in range(3):
        for yy in range(26):
            for x in range(TW):
                y, xx = yy - 1, x + dx - 1
                row = out[dx, yy * PITCH + x]
                inside_y, inside_x = 0 <= y < TH, 0 <= xx < TW
                if inside_y and inside_x:
                    row[y * PITCH + xx] = 1
                if y == -1:
                    row[top + xx + 1] = 1
                if y == TH:
                    row[bottom + xx + 1] = 1
                if not inside_x:
                    side = left if xx < 0 else right
                    row[side + (y + 1 if y < TW else 16 + y - TW + 1)] = 1
    return out.reshape(3 * ROWS, KZ)


def gelu(x):
    c = math.sqrt(2.0 / math.pi)
    return x * (0.5 * (1.0 + jnp.tanh(c * x * (1.0 + 0.044715 * (x * x)))))


def gelu_slope(x):
    c = math.sqrt(2.0 / math.pi)
    sq = x * x
    t = jnp.tanh(c * x * (1.0 + 0.044715 * sq))
    return 0.5 * (1.0 + t) + 0.5 * x * (1.0 - t * t) * (c * (1.0 + 3.0 * 0.044715 * sq))


def kernel(
    nbr_h, trn_h, act_h, cot_h, w1_h, w2_h, w3_h, spread_h,
    gin, grads,
    nbr, trn, pick_at, act, cot, spread, order, sel, z, xf, xb, slope, up, wst, wbk, sg, line,
    s1, nb, cr, cc, s2r, s2c, d2r, d2c, gb, a1, pb, a2, gf,
    insem, s1sem, nsem, crsem, ccsem, s2sem, d2sem, arsem_s, arsem_r,
):
    k = lax.axis_index("face")
    t = lax.axis_index("tile")
    row = t // TGC
    col = t % TGC
    active = k < GROUPS
    owner = t < OWNERS
    spreads = owner & (t // (OWNERS // 2) == k % 2)
    mate = k + 1 - 2 * (k % 2)
    edges = (row == 0, row == TGR - 1, col == 0, col == TGC - 1)
    gathers = (row >= 1) & (row <= 2) & (((col >= 1) & (col <= 2)) | ((col >= 5) & (col <= 6)))
    served = 2 * (row - 1) + col // 4
    part = (col - 1 + (col // 4) * (7 - 2 * col)) % 2
    lines_up = (edges[0] & (col % 2 == 0)) | (edges[1] & (col % 2 == 1))

    barrier = pltpu.get_barrier_semaphore()
    for i in range(1, 8):
        pl.semaphore_signal(barrier, inc=1, device_id=((k + i) % 8, t), device_id_type=MESH)

    @pl.loop(1, 32)
    def _(i):
        pl.semaphore_signal(barrier, inc=1, device_id=(k, (t + i) % 32), device_id_type=MESH)

    def gatherer(r, h):
        return (1 + r // 2) * TGC + 1 + h + (r % 2) * (5 - 2 * h)

    def aligner(w):
        return (w % 2) * (TILES - TGC) + w

    def greet(tile):
        for i in range(1, GROUPS):
            pl.semaphore_signal(barrier, inc=1, device_id=((k + i) % GROUPS, tile), device_id_type=MESH)

    for e in range(2):
        @pl.when(active & edges[e])
        def _():
            greet((1 - e) * (TILES - TGC) + col)

    @pl.when(active & (edges[2] | edges[3]))
    def _():
        greet(gatherer(row, 0))
        greet(gatherer(row, 1))

    @pl.when(active & gathers)
    def _():
        for far in range(2):
            greet(served * TGC + (TGC - 1) * far)

    def send(src, dst, ssem, rsem, dev):
        pltpu.make_async_remote_copy(
            src_ref=src, dst_ref=dst, send_sem=ssem, recv_sem=rsem, device_id=dev, device_id_type=MESH
        ).start()

    def await_bytes(ref, sem):
        pltpu.make_async_copy(ref, ref, sem).wait()

    def reorder(cells):
        return jnp.dot(order[...], cells, preferred_element_type=F32)

    def mine(f):
        return jnp.minimum(2 * k + f, FACES - 1)

    slots = []
    for e in (0, 1):
        for i in range(3):
            slots.append((e, (col + 7 + i) % 8, False))
        for i in range(3):
            slots.append((e, (14 - col + i) % 8, True))
    for e in (2, 3):
        for i in range(4):
            slots.append((e, (2 * row + 7 + i) % 8, False))
        for i in range(4):
            slots.append((e, (13 - 2 * row + i) % 8, True))

    def build_sel():
        j = lax.broadcasted_iota(jnp.int32, (16, CELLS), 0)
        cell = lax.broadcasted_iota(jnp.int32, (16, CELLS), 1)
        for n, (e, w, rev) in enumerate(slots):
            pos = (96 - 12 * w) - j if rev else (12 * w - 1) + j
            local = pos - (12 * col if e < 2 else 24 * row)
            size = TW if e < 2 else TH
            base = (0, (TH - 1) * PITCH, 0, TW - 1)[e]
            stride = 1 if e < 2 else PITCH
            ok = (local >= 0) & (local < size) & (j < 14) & (cell == base + local * stride)
            sel[n * 16 : n * 16 + 16, :] = jnp.where(ok, 1.0, 0.0).astype(BF)

    def messages(x, e):
        span = 3 if e < 2 else 4
        first = 6 * e if e < 2 else 12 + 8 * (e - 2)
        for o in range(2):
            for i in range(span):
                n = first + span * o + i
                w = slots[n][1]
                h = w % 2
                at = 6 * e + 3 * o + i if e < 2 else 12 + 4 * (e - 2) + 2 * o + i // 2
                yield True, None, n, cr.at[x, at], crsem.at[x], aligner(w)
                tile = gatherer(w // 2, h)
                if e >= 2:
                    yield False, None, n, cc.at[x, 8 + 4 * (e - 2) + 2 * o + i // 2], ccsem.at[x], tile
                elif i == 0:
                    yield False, h == 1, n, cc.at[x, 4 * e + 2 * o], ccsem.at[x], tile
                elif i == 1:
                    yield False, None, n, cc.at[x, 4 * e + 2 * o + h], ccsem.at[x], tile
                else:
                    yield False, h == 0, n, cc.at[x, 4 * e + 2 * o + 1], ccsem.at[x], tile

    def cut_windows(x, v):
        for f in range(2):
            cut = jnp.dot(sel[...], v[f, :CELLS], preferred_element_type=F32)
            s1[x, :, f] = cut.astype(BF).reshape(28, 16, C)

    def exchange_send(x):
        for e in range(4):
            @pl.when(edges[e])
            def _():
                for stays, cond, n, dst, sem, tile in messages(x, e):
                    if stays:
                        @pl.when(tile != t)
                        def _():
                            send(s1.at[x, n], dst, s1sem.at[x, e], sem, (k, tile))

                        @pl.when(tile == t)
                        def _():
                            pltpu.make_async_copy(s1.at[x, n], dst, sem).start()
                    elif cond is None:
                        send(s1.at[x, n], dst, s1sem.at[x, e], sem, (k, tile))
                    else:
                        @pl.when(cond)
                        def _():
                            send(s1.at[x, n], dst, s1sem.at[x, e], sem, (k, tile))

        @pl.when(row > 0)
        def _():
            for i in range(3):
                send(s1.at[x, i], nb.at[x, 3 + i], s1sem.at[x, 0], nsem.at[x, 1], (k, (row - 1) * TGC + slots[i][1]))

        @pl.when(row < TGR - 1)
        def _():
            for i in range(3):
                send(s1.at[x, 6 + i], nb.at[x, i], s1sem.at[x, 1], nsem.at[x, 0], (k, (row + 1) * TGC + slots[i][1]))

        @pl.when(col > 0)
        def _():
            send(s1.at[x, 13:15], nb.at[x, 8:10], s1sem.at[x, 2], nsem.at[x, 3], (k, t - 1))

        @pl.when(col < TGC - 1)
        def _():
            send(s1.at[x, 21:23], nb.at[x, 6:8], s1sem.at[x, 3], nsem.at[x, 2], (k, t + 1))

    def sent(x):
        for e in range(4):
            first = 6 * e if e < 2 else 13 + 8 * (e - 2)

            @pl.when(edges[e])
            def _():
                for stays, cond, n, dst, sem, tile in messages(x, e):
                    if stays:
                        cond = tile != t
                    if cond is None:
                        await_bytes(s1.at[x, n], s1sem.at[x, e])
                    else:
                        @pl.when(cond)
                        def _():
                            await_bytes(s1.at[x, n], s1sem.at[x, e])

            @pl.when(jnp.logical_not(edges[e]))
            def _():
                await_bytes(s1.at[x, first : first + (3 if e < 2 else 2)], s1sem.at[x, e])

        @pl.when(gathers)
        def _():
            await_bytes(s2c.at[x], s2sem.at[x, 1])

        @pl.when(lines_up)
        def _():
            await_bytes(s2r.at[x, 0], s2sem.at[x, 0])
            await_bytes(s2r.at[x, 1, 0:5], s2sem.at[x, 0])

    def collect(x):
        def lines(buf, row_first, row_count, col_first):
            for e in range(4):
                for o in range(2):
                    if e < 2:
                        first, count = row_first(e, o), row_count
                    else:
                        first, count = col_first(e, o), 2
                    total = buf[first]
                    for n in range(1, count):
                        total = total + buf[first + n]
                    line[2 * e + o] = total

        def pick(face, e):
            at = pick_at[face, e]
            return line[at // 2, at % 2]

        @pl.when(lines_up)
        def _():
            await_bytes(cr.at[x], crsem.at[x])
            lines(cr.at[x], lambda e, o: 6 * e + 3 * o, 3, lambda e, o: 12 + 4 * (e - 2) + 2 * o)
            for e in range(2):
                tile = (TILES - TGC) * e + col
                for g in range(GROUPS):
                    for f in range(2):
                        s2r[x, e, g, f] = pick(2 * g + f, e)
                for i in range(1, GROUPS):
                    g = (k + i) % GROUPS
                    send(s2r.at[x, e, g], d2r.at[x, k], s2sem.at[x, 0], d2sem.at[x, 0], (g, tile))

                @pl.when(tile != t)
                def _():
                    send(s2r.at[x, e, k], d2r.at[x, k], s2sem.at[x, 0], d2sem.at[x, 0], (k, tile))

                @pl.when(tile == t)
                def _():
                    pltpu.make_async_copy(s2r.at[x, e, k], d2r.at[x, k], d2sem.at[x, 0]).start()

        @pl.when(gathers)
        def _():
            await_bytes(cc.at[x], ccsem.at[x])
            lines(cc.at[x], lambda e, o: 4 * e + 2 * o, 2, lambda e, o: 8 + 4 * (e - 2) + 2 * o)
            for far in range(2):
                there = served * TGC + (TGC - 1) * far
                for g in range(GROUPS):
                    for f in range(2):
                        s2c[x, far, g, f] = pick(2 * g + f, 2 + far)
                for i in range(GROUPS):
                    g = (k + i) % GROUPS
                    send(s2c.at[x, far, g], d2c.at[x, k, part], s2sem.at[x, 1], d2sem.at[x, 1], (g, there))

    def arrived(x, e, f, h=0):
        group = nbr[e, mine(f)] // 2
        out = None
        for g in range(GROUPS):
            win = d2r[x, g, f] if e < 2 else d2c[x, g, h, f]
            out = win if out is None else jnp.where(group == g, win, out)
        return out

    def halo_local(x, v):
        for side in (0, 1):
            at = CELLS + 16 * side

            @pl.when(jnp.logical_not(edges[side]))
            def _():
                await_bytes(nb.at[x, 3 * side : 3 * side + 3], nsem.at[x, side])
                for f in range(2):
                    v[f, at : at + 16] = nb[x, 3 * side, f] + nb[x, 3 * side + 1, f] + nb[x, 3 * side + 2, f]

            @pl.when(edges[side])
            def _():
                for f in range(2):
                    v[f, at : at + 16] = jnp.zeros((16, C), BF)

        for side in (0, 1):
            at = CELLS + 32 + 32 * side

            @pl.when(jnp.logical_not(edges[2 + side]))
            def _():
                await_bytes(nb.at[x, 6 + 2 * side : 8 + 2 * side], nsem.at[x, 2 + side])
                for f in range(2):
                    for h in range(2):
                        v[f, at + 16 * h : at + 16 * h + 16] = nb[x, 6 + 2 * side + h, f]

            @pl.when(edges[2 + side])
            def _():
                for f in range(2):
                    v[f, at : at + 32] = jnp.zeros((32, C), BF)

    def widen(f, v, out):
        for dx in range(3):
            part = jnp.dot(spread[dx * ROWS : (dx + 1) * ROWS, :], v[f], preferred_element_type=F32)
            out[f, :, dx * C : (dx + 1) * C] = part.astype(BF)

    def finish(l):
        v = z.at[l]
        for e in range(4):
            @pl.when(edges[e])
            def _():
                for f in range(2):
                    if e < 2:
                        at = CELLS + 16 * e
                        v[f, at : at + 16] = arrived(l, e, f)
                    else:
                        for h in range(2):
                            at = CELLS + 32 + 32 * (e - 2) + 16 * h
                            v[f, at : at + 16] = arrived(l, e, f, h)

        @pl.when(edges[0] | edges[1] | edges[2] | edges[3])
        def _():
            for f in range(2):
                widen(f, v, xf.at[l])

    def correct(x, weights):
        for e in range(4):
            @pl.when(edges[e])
            def _():
                if e < 2:
                    await_bytes(d2r.at[x], d2sem.at[x, 0])
                else:
                    await_bytes(d2c.at[x], d2sem.at[x, 1])
                size = 16 if e < 2 else 32
                for f in range(2):
                    win = sg.at[2 * e + f]
                    win[0:16] = arrived(x, e, f, 0).astype(F32)
                    if e >= 2:
                        win[48:64] = arrived(x, e, f, 1).astype(F32)
                        win[13:26] = win[49:62]
                moved = []
                for f in range(2):
                    more = None
                    for s, weight in enumerate(weights(f, e)):
                        part = jnp.dot(sg[2 * e + f, s : s + size].astype(BF), weight, preferred_element_type=F32)
                        more = part if more is None else more + part
                    moved.append(more)
                for f, more in enumerate(moved):
                    if e < 2:
                        at = 0 if e == 0 else CELLS - PITCH
                        up[f, at : at + 16] = up[f, at : at + 16] + more
                    else:
                        where = pl.ds(0 if e == 2 else TW - 1, TH, stride=PITCH)
                        up[f, where, :] = up[f, where, :] + more[0:TH]

    def forward_taps(l):
        return lambda f, e: [wst[l, tap] for tap in TAP_TABLE[e]]

    def backward_taps(l):
        def weights(f, e):
            code = trn[e, mine(f)]
            other, rev = code % 4, code // 4
            first = jnp.where(other == 1, 6, jnp.where(other == 3, 2, 0))
            step = jnp.where(other < 2, 1, 3)
            out = []
            for s in range(3):
                order = jnp.where(rev == 1, s, 2 - s)
                out.append(wbk[l, first + step * order])
            return out

        return weights

    def reduce_send(l):
        @pl.loop(1, 32)
        def _(i):
            dst = (t + i) % 32

            @pl.when(dst < OWNERS)
            def _():
                send(
                    gb.at[l, pl.ds(dst * CHUNK, CHUNK)], a1.at[l, 31 - i],
                    arsem_s.at[l, 0], arsem_r.at[l, 0], (k, dst),
                )

    def reduce_mid(l):
        @pl.when(owner)
        def _():
            await_bytes(a1.at[l], arsem_r.at[l, 0])
            total = gb[l, pl.ds(t * CHUNK, CHUNK)].astype(F32)
            for s in range(31):
                total = total + a1[l, s].astype(F32)
            pb[l] = total.astype(BF)
            for i in range(1, 4):
                there = (2 * (k // 2) + 2 * i) % 8 + t // (OWNERS // 2)
                send(pb.at[l], a2.at[l, k], arsem_s.at[l, 1], arsem_r.at[l, 1], (there, t))

            @pl.when(spreads)
            def _():
                a2[l, k] = pb[l]

            @pl.when(jnp.logical_not(spreads))
            def _():
                send(pb.at[l], a2.at[l, k], arsem_s.at[l, 1], arsem_r.at[l, 1], (mate, t))

    def reduce_last(l):
        @pl.when(spreads)
        def _():
            @pl.when(active)
            def _():
                await_bytes(a2.at[l, 0:5], arsem_r.at[l, 1])

            @pl.when(jnp.logical_not(active))
            def _():
                await_bytes(a2.at[l], arsem_r.at[l, 1])

            total = a2[l, 0].astype(F32)
            for s in range(1, GROUPS):
                total = total + a2[l, s].astype(F32)
            here = pl.ds(t * CHUNK, CHUNK)
            gf[l, here] = total.astype(BF)

            @pl.loop(1, 32)
            def _(i):
                send(gf.at[l, here], gf.at[l, here], arsem_s.at[l, 2], arsem_r.at[l, 2], (k, (t + i) % 32))

    def reduce_swap(l):
        here = (k % 2) * (OWNERS // 2) * CHUNK
        half = gf.at[l, pl.ds(here, OWNERS // 2 * CHUNK)]

        @pl.when(spreads)
        def _():
            await_bytes(gf.at[l, 0 : (OWNERS // 2 - 1) * CHUNK], arsem_r.at[l, 2])

        @pl.when(jnp.logical_not(spreads))
        def _():
            await_bytes(gf.at[l, 0 : OWNERS // 2 * CHUNK], arsem_r.at[l, 2])

        send(half, half, arsem_s.at[l, 3], arsem_r.at[l, 3], (mate, t))

    def reduce_drain(l):
        await_bytes(gf.at[l, 0 : OWNERS // 2 * CHUNK], arsem_r.at[l, 3])
        await_bytes(gf.at[l, 0 : OWNERS // 2 * CHUNK], arsem_s.at[l, 3])

        @pl.when(spreads)
        def _():
            await_bytes(a1.at[l], arsem_s.at[l, 2])

        @pl.when(active & owner)
        def _():
            await_bytes(gb.at[l, 0 : (OWNERS - 1) * CHUNK], arsem_s.at[l, 0])

        @pl.when(active & jnp.logical_not(owner))
        def _():
            await_bytes(gb.at[l], arsem_s.at[l, 0])

        @pl.when(active & spreads)
        def _():
            await_bytes(a1.at[l, 0:3], arsem_s.at[l, 1])

        @pl.when(active & owner & jnp.logical_not(spreads))
        def _():
            await_bytes(a1.at[l, 0:4], arsem_s.at[l, 1])

    fetches = [
        pltpu.make_async_copy(src, dst, insem.at[n])
        for n, (src, dst) in enumerate((
            (act_h, act), (w1_h, wst.at[0]), (spread_h, spread), (nbr_h, nbr), (trn_h, trn),
            (w2_h, wst.at[1]), (w3_h, wst.at[2]), (cot_h, cot),
        ))
    ]

    @pl.when(active)
    def _():
        for fetch in fetches:
            fetch.start()
        place = lax.broadcasted_iota(jnp.int32, (CELLS, TW * TH), 0)
        given = lax.broadcasted_iota(jnp.int32, (CELLS, TW * TH), 1)
        order[...] = jnp.where((given % TH) * PITCH + given // TH == place, 1.0, 0.0).astype(BF)
        build_sel()
        z[...] = jnp.zeros_like(z)
        up[...] = jnp.zeros_like(up)
        sg[...] = jnp.zeros_like(sg)
        fetches[0].wait()
        for f in range(2):
            z[0, f, :CELLS] = reorder(act[f]).astype(BF)
        cut_windows(0, z.at[0])

    across, along = edges[0] | edges[1], edges[2] | edges[3]
    counts = ((active & across & along, 3), (active & ((along & jnp.logical_not(across)) | gathers), 2), (active & across & jnp.logical_not(along), 1))
    extra = jnp.bool_(False)
    for cond, n in counts:
        extra = extra | cond

        @pl.when(cond)
        def _():
            pl.semaphore_wait(barrier, 38 + n * (GROUPS - 1))

    @pl.when(jnp.logical_not(extra))
    def _():
        pl.semaphore_wait(barrier, 38)

    @pl.when(active)
    def _():
        @pl.loop(0, 3)
        def _(l):
            exchange_send(l)

            @pl.when(l == 0)
            def _():
                for fetch in fetches[1:]:
                    fetch.wait()
                for face in range(FACES):
                    for e in range(4):
                        code = trn[e, face]
                        pick_at[face, e] = (code % 4) * 4 + (code // 4) * 2 + nbr[e, face] % 2

            @pl.when(l > 0)
            def _():
                for f in range(2):
                    slope[l - 1, f] = gelu_slope(up[f])
                finish(l - 1)

            collect(l)
            halo_local(l, z.at[l])
            for f in range(2):
                widen(f, z.at[l], xf.at[l])
                total = None
                for dy in range(3):
                    part = jnp.dot(
                        xf[l, f, dy * PITCH : dy * PITCH + CELLS, :],
                        wst[l, 3 * dy : 3 * dy + 3].reshape(3 * C, C), preferred_element_type=F32,
                    )
                    total = part if total is None else total + part
                up[f] = total
            correct(l, forward_taps(l))

            @pl.when(l < 2)
            def _():
                for f in range(2):
                    z[l + 1, f, :CELLS] = gelu(up[f]).astype(BF)
                cut_windows(l + 1, z.at[l + 1])

        for f in range(2):
            slope[2, f] = gelu_slope(up[f])
            up[f] = reorder(cot[f])

        @pl.loop(0, 3)
        def _(i):
            l = 2 - i
            x = 3 + i
            d = z.at[3]
            for f in range(2):
                d[f, :CELLS] = (up[f] * slope[l, f]).astype(BF)
            cut_windows(x, d)
            exchange_send(x)

            @pl.when(i == 0)
            def _():
                finish(2)
                for n in range(3):
                    for tap in range(9):
                        wbk[n, tap] = wst[n, tap].astype(F32).T.astype(BF)

            for dy in range(3):
                total = None
                for f in range(2):
                    part = lax.dot_general(
                        xf[l, f, dy * PITCH : dy * PITCH + CELLS, :], d[f, :CELLS],
                        (((0,), (0,)), ((), ())), preferred_element_type=F32,
                    )
                    total = part if total is None else total + part
                gb[l, dy * 3 * C : (dy + 1) * 3 * C] = total.astype(BF)

            @pl.when(i == 2)
            def _():
                reduce_send(l)

            @pl.when(i > 0)
            def _():
                reduce_mid(l + 1)

            collect(x)

            @pl.when(i < 2)
            def _():
                reduce_send(l)

            @pl.when(i == 2)
            def _():
                reduce_mid(l)

            @pl.when(i > 0)
            def _():
                reduce_last(l + 1)

            halo_local(x, d)
            for f in range(2):
                widen(f, d, xb)
                total = None
                for dy in range(3):
                    for dx in range(3):
                        part = jnp.dot(
                            xb[f, dy * PITCH : dy * PITCH + CELLS, dx * C : (dx + 1) * C], wbk[l, 8 - 3 * dy - dx],
                            preferred_element_type=F32,
                        )
                        total = part if total is None else total + part
                up[f] = total

            @pl.when(i == 2)
            def _():
                reduce_last(l)

            correct(x, backward_taps(l))

        for f in range(2):
            gin[f] = lax.dot_general(
                order[...], up[f].astype(BF), (((0,), (0,)), ((), ())), preferred_element_type=F32
            ).astype(BF)

    @pl.when(jnp.logical_not(active))
    def _():
        gin[...] = jnp.zeros_like(gin)
        reduce_last(2)
        reduce_last(1)
        reduce_last(0)

    reduce_swap(2)
    reduce_swap(1)

    @pl.when(active)
    def _():
        @pl.loop(0, 6)
        def _(x):
            sent(x)

    for l in (2, 1):
        reduce_drain(l)
        grads[l] = gf[l]
    reduce_swap(0)
    reduce_drain(0)
    grads[0] = gf[0]


def shards(activation, cotangent, weight_one, weight_two, weight_three, neighbor, turn):
    def flipped(field):
        return field.transpose(0, 1, 3, 2, 4).reshape(2, TW * TH, C)

    vmem = pl.BlockSpec(memory_space=pltpu.VMEM)
    hbm = pl.BlockSpec(memory_space=pltpu.HBM)
    dma = pltpu.SemaphoreType.DMA
    gin, grads = pl.pallas_call(
        kernel,
        out_shape=(
            jax.ShapeDtypeStruct((2, TW * TH, C), BF),
            jax.ShapeDtypeStruct((3, 9 * C, C), BF),
        ),
        in_specs=[hbm] * 8,
        out_specs=(vmem, vmem),
        scratch_shapes=[
            pltpu.SMEM((4, FACES), jnp.int32),
            pltpu.SMEM((4, FACES), jnp.int32),
            pltpu.SMEM((FACES, 4), jnp.int32),
            pltpu.VMEM((2, TW * TH, C), BF),
            pltpu.VMEM((2, TW * TH, C), BF),
            pltpu.VMEM((3 * ROWS, KZ), BF),
            pltpu.VMEM((CELLS, TW * TH), BF),
            pltpu.VMEM((28 * 16, CELLS), BF),
            pltpu.VMEM((4, 2, KZ, C), BF),
            pltpu.VMEM((3, 2, ROWS, 3 * C), BF),
            pltpu.VMEM((2, ROWS, 3 * C), BF),
            pltpu.VMEM((3, 2, CELLS, C), F32),
            pltpu.VMEM((2, CELLS, C), F32),
            pltpu.VMEM((3, 9, C, C), BF),
            pltpu.VMEM((3, 9, C, C), BF),
            pltpu.VMEM((8, 64, C), F32),
            pltpu.VMEM((8, 2, 16, C), BF),
            pltpu.VMEM((6, 28, 2, 16, C), BF),
            pltpu.VMEM((6, 10, 2, 16, C), BF),
            pltpu.VMEM((6, 20, 2, 16, C), BF),
            pltpu.VMEM((6, 16, 2, 16, C), BF),
            pltpu.VMEM((6, 2, GROUPS, 2, 16, C), BF),
            pltpu.VMEM((6, 2, GROUPS, 2, 16, C), BF),
            pltpu.VMEM((6, GROUPS, 2, 16, C), BF),
            pltpu.VMEM((6, GROUPS, 2, 2, 16, C), BF),
            pltpu.VMEM((3, 9 * C, C), BF),
            pltpu.VMEM((3, 31, CHUNK, C), BF),
            pltpu.VMEM((3, CHUNK, C), BF),
            pltpu.VMEM((3, GROUPS, CHUNK, C), BF),
            pltpu.VMEM((3, 9 * C, C), BF),
            dma((8,)),
            dma((6, 4)),
            dma((6, 4)),
            dma((6,)),
            dma((6,)),
            dma((6, 2)),
            dma((6, 2)),
            dma((3, 4)),
            dma((3, 4)),
        ],
        compiler_params=pltpu.CompilerParams(
            collective_id=0, has_side_effects=True, vmem_limit_bytes=62 * 1024 * 1024
        ),
        name="glued_convolutions",
    )(
        neighbor.T, turn.T, flipped(activation), flipped(cotangent), weight_one, weight_two, weight_three,
        jnp.asarray(spread_matrix(), BF),
    )
    grad_input = gin.reshape(2, 1, TW, TH, C).transpose(0, 1, 3, 2, 4)
    scaled = grads.reshape(3, 9, C, C).astype(F32) * (1.0 / math.sqrt(FACES * NS * NS))
    return grad_input, scaled[0], scaled[1], scaled[2]


def solution(mesh):
    field = P("face", "tile", None, None, None)
    return jax.shard_map(
        shards,
        mesh=mesh,
        in_specs=(field, field, P(), P(), P(), P(), P()),
        out_specs=(field, P(), P(), P()),
        check_vma=False,
    )
```

```python
import math

import jax
import jax.numpy as jnp
import numpy as np
from jax import lax
from jax.experimental import pallas as pl
from jax.experimental.pallas import tpu as pltpu
from jax.sharding import PartitionSpec as P

FACES = 12
TGR = 4
TGC = 8
TILES = 32
TH = 24
TW = 12
C = 128
NS = 96
PITCH = 16
CELLS = TH * PITCH
GROUPS = 6
OWNERS = 24
CHUNK = 9 * C // OWNERS
KZ = 512
ROWS = 26 * PITCH
MESH = pl.DeviceIdType.MESH
BF = jnp.bfloat16
F32 = jnp.float32
TAP_TABLE = ((0, 1, 2), (6, 7, 8), (0, 3, 6), (2, 5, 8))


def spread_matrix():
    out = np.zeros((3, ROWS, KZ), np.float32)
    top, bottom, left, right = CELLS, CELLS + 16, CELLS + 32, CELLS + 64
    for dx in range(3):
        for yy in range(26):
            for x in range(TW):
                y, xx = yy - 1, x + dx - 1
                row = out[dx, yy * PITCH + x]
                inside_y, inside_x = 0 <= y < TH, 0 <= xx < TW
                if inside_y and inside_x:
                    row[y * PITCH + xx] = 1
                if y == -1:
                    row[top + xx + 1] = 1
                if y == TH:
                    row[bottom + xx + 1] = 1
                if not inside_x:
                    side = left if xx < 0 else right
                    row[side + (y + 1 if y < TW else 16 + y - TW + 1)] = 1
    return out.reshape(3 * ROWS, KZ)


def gelu(x):
    c = math.sqrt(2.0 / math.pi)
    return x * (0.5 * (1.0 + jnp.tanh(c * x * (1.0 + 0.044715 * (x * x)))))


def gelu_slope(x):
    c = math.sqrt(2.0 / math.pi)
    sq = x * x
    t = jnp.tanh(c * x * (1.0 + 0.044715 * sq))
    return 0.5 * (1.0 + t) + 0.5 * x * (1.0 - t * t) * (c * (1.0 + 3.0 * 0.044715 * sq))


def kernel(
    nbr_h, trn_h, act_h, cot_h, w1_h, w2_h, w3_h, spread_h,
    gin, grads,
    nbr, trn, pick_at, act, cot, spread, order, sel, z, xf, xb, slope, up, wst, wbk, sg, line,
    s1, nb, cr, cc, s2r, s2c, d2r, d2c, gb, a1, pb, a2, gf,
    insem, s1sem, nsem, crsem, ccsem, s2sem, d2sem, arsem_s, arsem_r,
):
    k = lax.axis_index("face")
    t = lax.axis_index("tile")
    row = t // TGC
    col = t % TGC
    active = k < GROUPS
    owner = t < OWNERS
    spreads = owner & (t // (OWNERS // 2) == k % 2)
    mate = k + 1 - 2 * (k % 2)
    edges = (row == 0, row == TGR - 1, col == 0, col == TGC - 1)
    gathers = (row >= 1) & (row <= 2) & (((col >= 1) & (col <= 2)) | ((col >= 5) & (col <= 6)))
    served = 2 * (row - 1) + col // 4
    part = (col - 1 + (col // 4) * (7 - 2 * col)) % 2
    lines_up = (edges[0] & (col % 2 == 0)) | (edges[1] & (col % 2 == 1))

    barrier = pltpu.get_barrier_semaphore()
    for i in range(1, 8):
        pl.semaphore_signal(barrier, inc=1, device_id=((k + i) % 8, t), device_id_type=MESH)

    @pl.loop(1, 32)
    def _(i):
        pl.semaphore_signal(barrier, inc=1, device_id=(k, (t + i) % 32), device_id_type=MESH)

    def gatherer(r, h):
        return (1 + r // 2) * TGC + 1 + h + (r % 2) * (5 - 2 * h)

    def aligner(w):
        return (w % 2) * (TILES - TGC) + w

    def greet(tile):
        for i in range(1, GROUPS):
            pl.semaphore_signal(barrier, inc=1, device_id=((k + i) % GROUPS, tile), device_id_type=MESH)

    for e in range(2):
        @pl.when(active & edges[e])
        def _():
            greet((1 - e) * (TILES - TGC) + col)

    @pl.when(active & (edges[2] | edges[3]))
    def _():
        greet(gatherer(row, 0))
        greet(gatherer(row, 1))

    @pl.when(active & gathers)
    def _():
        for far in range(2):
            greet(served * TGC + (TGC - 1) * far)

    def send(src, dst, ssem, rsem, dev):
        pltpu.make_async_remote_copy(
            src_ref=src, dst_ref=dst, send_sem=ssem, recv_sem=rsem, device_id=dev, device_id_type=MESH
        ).start()

    def await_bytes(ref, sem):
        pltpu.make_async_copy(ref, ref, sem).wait()

    def reorder(cells):
        return jnp.dot(order[...], cells, preferred_element_type=F32)

    def mine(f):
        return jnp.minimum(2 * k + f, FACES - 1)

    slots = []
    for e in (0, 1):
        for i in range(3):
            slots.append((e, (col + 7 + i) % 8, False))
        for i in range(3):
            slots.append((e, (14 - col + i) % 8, True))
    for e in (2, 3):
        for i in range(4):
            slots.append((e, (2 * row + 7 + i) % 8, False))
        for i in range(4):
            slots.append((e, (13 - 2 * row + i) % 8, True))

    def build_sel():
        j = lax.broadcasted_iota(jnp.int32, (16, CELLS), 0)
        cell = lax.broadcasted_iota(jnp.int32, (16, CELLS), 1)
        for n, (e, w, rev) in enumerate(slots):
            pos = (96 - 12 * w) - j if rev else (12 * w - 1) + j
            local = pos - (12 * col if e < 2 else 24 * row)
            size = TW if e < 2 else TH
            base = (0, (TH - 1) * PITCH, 0, TW - 1)[e]
            stride = 1 if e < 2 else PITCH
            ok = (local >= 0) & (local < size) & (j < 14) & (cell == base + local * stride)
            sel[n * 16 : n * 16 + 16, :] = jnp.where(ok, 1.0, 0.0).astype(BF)

    def messages(x, e):
        span = 3 if e < 2 else 4
        first = 6 * e if e < 2 else 12 + 8 * (e - 2)
        for o in range(2):
            for i in range(span):
                n = first + span * o + i
                w = slots[n][1]
                h = w % 2
                at = 6 * e + 3 * o + i if e < 2 else 12 + 4 * (e - 2) + 2 * o + i // 2
                yield True, None, n, cr.at[x, at], crsem.at[x], aligner(w)
                tile = gatherer(w // 2, h)
                if e >= 2:
                    yield False, None, n, cc.at[x, 8 + 4 * (e - 2) + 2 * o + i // 2], ccsem.at[x], tile
                elif i == 0:
                    yield False, h == 1, n, cc.at[x, 4 * e + 2 * o], ccsem.at[x], tile
                elif i == 1:
                    yield False, None, n, cc.at[x, 4 * e + 2 * o + h], ccsem.at[x], tile
                else:
                    yield False, h == 0, n, cc.at[x, 4 * e + 2 * o + 1], ccsem.at[x], tile

    def cut_windows(x, v):
        for f in range(2):
            cut = jnp.dot(sel[...], v[f, :CELLS], preferred_element_type=F32)
            s1[x, :, f] = cut.astype(BF).reshape(28, 16, C)

    def exchange_send(x):
        for e in range(4):
            @pl.when(edges[e])
            def _():
                for stays, cond, n, dst, sem, tile in messages(x, e):
                    if stays:
                        @pl.when(tile != t)
                        def _():
                            send(s1.at[x, n], dst, s1sem.at[x, e], sem, (k, tile))

                        @pl.when(tile == t)
                        def _():
                            pltpu.make_async_copy(s1.at[x, n], dst, sem).start()
                    elif cond is None:
                        send(s1.at[x, n], dst, s1sem.at[x, e], sem, (k, tile))
                    else:
                        @pl.when(cond)
                        def _():
                            send(s1.at[x, n], dst, s1sem.at[x, e], sem, (k, tile))

        @pl.when(row > 0)
        def _():
            for i in range(3):
                send(s1.at[x, i], nb.at[x, 3 + i], s1sem.at[x, 0], nsem.at[x, 1], (k, (row - 1) * TGC + slots[i][1]))

        @pl.when(row < TGR - 1)
        def _():
            for i in range(3):
                send(s1.at[x, 6 + i], nb.at[x, i], s1sem.at[x, 1], nsem.at[x, 0], (k, (row + 1) * TGC + slots[i][1]))

        @pl.when(col > 0)
        def _():
            send(s1.at[x, 13:15], nb.at[x, 8:10], s1sem.at[x, 2], nsem.at[x, 3], (k, t - 1))

        @pl.when(col < TGC - 1)
        def _():
            send(s1.at[x, 21:23], nb.at[x, 6:8], s1sem.at[x, 3], nsem.at[x, 2], (k, t + 1))

    def sent(x):
        for e in range(4):
            first = 6 * e if e < 2 else 13 + 8 * (e - 2)

            @pl.when(edges[e])
            def _():
                for stays, cond, n, dst, sem, tile in messages(x, e):
                    if stays:
                        cond = tile != t
                    if cond is None:
                        await_bytes(s1.at[x, n], s1sem.at[x, e])
                    else:
                        @pl.when(cond)
                        def _():
                            await_bytes(s1.at[x, n], s1sem.at[x, e])

            @pl.when(jnp.logical_not(edges[e]))
            def _():
                await_bytes(s1.at[x, first : first + (3 if e < 2 else 2)], s1sem.at[x, e])

        @pl.when(gathers)
        def _():
            await_bytes(s2c.at[x], s2sem.at[x, 1])

        @pl.when(lines_up)
        def _():
            await_bytes(s2r.at[x, 0], s2sem.at[x, 0])
            await_bytes(s2r.at[x, 1, 0:5], s2sem.at[x, 0])

    def collect(x):
        def lines(buf, row_first, row_count, col_first):
            for e in range(4):
                for o in range(2):
                    if e < 2:
                        first, count = row_first(e, o), row_count
                    else:
                        first, count = col_first(e, o), 2
                    total = buf[first]
                    for n in range(1, count):
                        total = total + buf[first + n]
                    line[2 * e + o] = total

        def pick(face, e):
            at = pick_at[face, e]
            return line[at // 2, at % 2]

        @pl.when(lines_up)
        def _():
            await_bytes(cr.at[x], crsem.at[x])
            lines(cr.at[x], lambda e, o: 6 * e + 3 * o, 3, lambda e, o: 12 + 4 * (e - 2) + 2 * o)
            for e in range(2):
                tile = (TILES - TGC) * e + col
                for g in range(GROUPS):
                    for f in range(2):
                        s2r[x, e, g, f] = pick(2 * g + f, e)
                for i in range(1, GROUPS):
                    g = (k + i) % GROUPS
                    send(s2r.at[x, e, g], d2r.at[x, k], s2sem.at[x, 0], d2sem.at[x, 0], (g, tile))

                @pl.when(tile != t)
                def _():
                    send(s2r.at[x, e, k], d2r.at[x, k], s2sem.at[x, 0], d2sem.at[x, 0], (k, tile))

                @pl.when(tile == t)
                def _():
                    pltpu.make_async_copy(s2r.at[x, e, k], d2r.at[x, k], d2sem.at[x, 0]).start()

        @pl.when(gathers)
        def _():
            await_bytes(cc.at[x], ccsem.at[x])
            lines(cc.at[x], lambda e, o: 4 * e + 2 * o, 2, lambda e, o: 8 + 4 * (e - 2) + 2 * o)
            for far in range(2):
                there = served * TGC + (TGC - 1) * far
                for g in range(GROUPS):
                    for f in range(2):
                        s2c[x, far, g, f] = pick(2 * g + f, 2 + far)
                for i in range(GROUPS):
                    g = (k + i) % GROUPS
                    send(s2c.at[x, far, g], d2c.at[x, k, part], s2sem.at[x, 1], d2sem.at[x, 1], (g, there))

    def arrived(x, e, f, h=0):
        group = nbr[e, mine(f)] // 2
        out = None
        for g in range(GROUPS):
            win = d2r[x, g, f] if e < 2 else d2c[x, g, h, f]
            out = win if out is None else jnp.where(group == g, win, out)
        return out

    def halo_local(x, v):
        for side in (0, 1):
            at = CELLS + 16 * side

            @pl.when(jnp.logical_not(edges[side]))
            def _():
                await_bytes(nb.at[x, 3 * side : 3 * side + 3], nsem.at[x, side])
                for f in range(2):
                    v[f, at : at + 16] = nb[x, 3 * side, f] + nb[x, 3 * side + 1, f] + nb[x, 3 * side + 2, f]

            @pl.when(edges[side])
            def _():
                for f in range(2):
                    v[f, at : at + 16] = jnp.zeros((16, C), BF)

        for side in (0, 1):
            at = CELLS + 32 + 32 * side

            @pl.when(jnp.logical_not(edges[2 + side]))
            def _():
                await_bytes(nb.at[x, 6 + 2 * side : 8 + 2 * side], nsem.at[x, 2 + side])
                for f in range(2):
                    for h in range(2):
                        v[f, at + 16 * h : at + 16 * h + 16] = nb[x, 6 + 2 * side + h, f]

            @pl.when(edges[2 + side])
            def _():
                for f in range(2):
                    v[f, at : at + 32] = jnp.zeros((32, C), BF)

    def widen(f, v, out):
        for dx in range(3):
            part = jnp.dot(spread[dx * ROWS : (dx + 1) * ROWS, :], v[f], preferred_element_type=F32)
            out[f, :, dx * C : (dx + 1) * C] = part.astype(BF)

    def finish(l):
        v = z.at[l]
        for e in range(4):
            @pl.when(edges[e])
            def _():
                for f in range(2):
                    if e < 2:
                        at = CELLS + 16 * e
                        v[f, at : at + 16] = arrived(l, e, f)
                    else:
                        for h in range(2):
                            at = CELLS + 32 + 32 * (e - 2) + 16 * h
                            v[f, at : at + 16] = arrived(l, e, f, h)

        @pl.when(edges[0] | edges[1] | edges[2] | edges[3])
        def _():
            for f in range(2):
                widen(f, v, xf.at[l])

    def correct(x, weights):
        for e in range(4):
            @pl.when(edges[e])
            def _():
                if e < 2:
                    await_bytes(d2r.at[x], d2sem.at[x, 0])
                else:
                    await_bytes(d2c.at[x], d2sem.at[x, 1])
                size = 16 if e < 2 else 32
                for f in range(2):
                    win = sg.at[2 * e + f]
                    win[0:16] = arrived(x, e, f, 0).astype(F32)
                    if e >= 2:
                        win[48:64] = arrived(x, e, f, 1).astype(F32)
                        win[13:26] = win[49:62]
                moved = []
                for f in range(2):
                    more = None
                    for s, weight in enumerate(weights(f, e)):
                        part = jnp.dot(sg[2 * e + f, s : s + size].astype(BF), weight, preferred_element_type=F32)
                        more = part if more is None else more + part
                    moved.append(more)
                for f, more in enumerate(moved):
                    if e < 2:
                        at = 0 if e == 0 else CELLS - PITCH
                        up[f, at : at + 16] = up[f, at : at + 16] + more
                    else:
                        where = pl.ds(0 if e == 2 else TW - 1, TH, stride=PITCH)
                        up[f, where, :] = up[f, where, :] + more[0:TH]

    def forward_taps(l):
        return lambda f, e: [wst[l, tap] for tap in TAP_TABLE[e]]

    def backward_taps(l):
        def weights(f, e):
            code = trn[e, mine(f)]
            other, rev = code % 4, code // 4
            first = jnp.where(other == 1, 6, jnp.where(other == 3, 2, 0))
            step = jnp.where(other < 2, 1, 3)
            out = []
            for s in range(3):
                order = jnp.where(rev == 1, s, 2 - s)
                out.append(wbk[l, first + step * order])
            return out

        return weights

    def reduce_send(l):
        @pl.loop(1, 32)
        def _(i):
            dst = (t + i) % 32

            @pl.when(dst < OWNERS)
            def _():
                send(
                    gb.at[l, pl.ds(dst * CHUNK, CHUNK)], a1.at[l, 31 - i],
                    arsem_s.at[l, 0], arsem_r.at[l, 0], (k, dst),
                )

    def reduce_mid(l):
        @pl.when(owner)
        def _():
            await_bytes(a1.at[l], arsem_r.at[l, 0])
            total = gb[l, pl.ds(t * CHUNK, CHUNK)].astype(F32)
            for s in range(31):
                total = total + a1[l, s].astype(F32)
            pb[l] = total.astype(BF)
            for i in range(1, 4):
                there = (2 * (k // 2) + 2 * i) % 8 + t // (OWNERS // 2)
                send(pb.at[l], a2.at[l, k], arsem_s.at[l, 1], arsem_r.at[l, 1], (there, t))

            @pl.when(spreads)
            def _():
                a2[l, k] = pb[l]

            @pl.when(jnp.logical_not(spreads))
            def _():
                send(pb.at[l], a2.at[l, k], arsem_s.at[l, 1], arsem_r.at[l, 1], (mate, t))

    def reduce_last(l):
        @pl.when(spreads)
        def _():
            @pl.when(active)
            def _():
                await_bytes(a2.at[l, 0:5], arsem_r.at[l, 1])

            @pl.when(jnp.logical_not(active))
            def _():
                await_bytes(a2.at[l], arsem_r.at[l, 1])

            total = a2[l, 0].astype(F32)
            for s in range(1, GROUPS):
                total = total + a2[l, s].astype(F32)
            here = pl.ds(t * CHUNK, CHUNK)
            gf[l, here] = total.astype(BF)

            @pl.loop(1, 32)
            def _(i):
                send(gf.at[l, here], gf.at[l, here], arsem_s.at[l, 2], arsem_r.at[l, 2], (k, (t + i) % 32))

    def reduce_swap(l):
        here = (k % 2) * (OWNERS // 2) * CHUNK
        half = gf.at[l, pl.ds(here, OWNERS // 2 * CHUNK)]

        @pl.when(spreads)
        def _():
            await_bytes(gf.at[l, 0 : (OWNERS // 2 - 1) * CHUNK], arsem_r.at[l, 2])

        @pl.when(jnp.logical_not(spreads))
        def _():
            await_bytes(gf.at[l, 0 : OWNERS // 2 * CHUNK], arsem_r.at[l, 2])

        send(half, half, arsem_s.at[l, 3], arsem_r.at[l, 3], (mate, t))

    def reduce_drain(l):
        await_bytes(gf.at[l, 0 : OWNERS // 2 * CHUNK], arsem_r.at[l, 3])
        await_bytes(gf.at[l, 0 : OWNERS // 2 * CHUNK], arsem_s.at[l, 3])

        @pl.when(spreads)
        def _():
            await_bytes(a1.at[l], arsem_s.at[l, 2])

        @pl.when(active & owner)
        def _():
            await_bytes(gb.at[l, 0 : (OWNERS - 1) * CHUNK], arsem_s.at[l, 0])

        @pl.when(active & jnp.logical_not(owner))
        def _():
            await_bytes(gb.at[l], arsem_s.at[l, 0])

        @pl.when(active & spreads)
        def _():
            await_bytes(a1.at[l, 0:3], arsem_s.at[l, 1])

        @pl.when(active & owner & jnp.logical_not(spreads))
        def _():
            await_bytes(a1.at[l, 0:4], arsem_s.at[l, 1])

    fetches = [
        pltpu.make_async_copy(src, dst, insem.at[n])
        for n, (src, dst) in enumerate((
            (act_h, act), (w1_h, wst.at[0]), (spread_h, spread), (nbr_h, nbr), (trn_h, trn),
            (w2_h, wst.at[1]), (w3_h, wst.at[2]), (cot_h, cot),
        ))
    ]

    @pl.when(active)
    def _():
        for fetch in fetches:
            fetch.start()
        place = lax.broadcasted_iota(jnp.int32, (CELLS, TW * TH), 0)
        given = lax.broadcasted_iota(jnp.int32, (CELLS, TW * TH), 1)
        order[...] = jnp.where((given % TH) * PITCH + given // TH == place, 1.0, 0.0).astype(BF)
        build_sel()
        z[...] = jnp.zeros_like(z)
        up[...] = jnp.zeros_like(up)
        sg[...] = jnp.zeros_like(sg)
        fetches[0].wait()
        for f in range(2):
            z[0, f, :CELLS] = reorder(act[f]).astype(BF)
        cut_windows(0, z.at[0])

    across, along = edges[0] | edges[1], edges[2] | edges[3]
    counts = ((active & across & along, 3), (active & ((along & jnp.logical_not(across)) | gathers), 2), (active & across & jnp.logical_not(along), 1))
    extra = jnp.bool_(False)
    for cond, n in counts:
        extra = extra | cond

        @pl.when(cond)
        def _():
            pl.semaphore_wait(barrier, 38 + n * (GROUPS - 1))

    @pl.when(jnp.logical_not(extra))
    def _():
        pl.semaphore_wait(barrier, 38)

    @pl.when(active)
    def _():
        @pl.loop(0, 3)
        def _(l):
            exchange_send(l)

            @pl.when(l == 0)
            def _():
                for fetch in fetches[1:]:
                    fetch.wait()
                for face in range(FACES):
                    for e in range(4):
                        code = trn[e, face]
                        pick_at[face, e] = (code % 4) * 4 + (code // 4) * 2 + nbr[e, face] % 2
                for n in range(3):
                    for tap in range(9):
                        wbk[n, tap] = wst[n, tap].astype(F32).T.astype(BF)

            @pl.when(l > 0)
            def _():
                for f in range(2):
                    slope[l - 1, f] = gelu_slope(up[f])
                finish(l - 1)

            collect(l)
            halo_local(l, z.at[l])
            for f in range(2):
                widen(f, z.at[l], xf.at[l])
                total = None
                for dy in range(3):
                    part = jnp.dot(
                        xf[l, f, dy * PITCH : dy * PITCH + CELLS, :],
                        wst[l, 3 * dy : 3 * dy + 3].reshape(3 * C, C), preferred_element_type=F32,
                    )
                    total = part if total is None else total + part
                up[f] = total
            correct(l, forward_taps(l))

            @pl.when(l < 2)
            def _():
                for f in range(2):
                    z[l + 1, f, :CELLS] = gelu(up[f]).astype(BF)
                cut_windows(l + 1, z.at[l + 1])

        for f in range(2):
            slope[2, f] = gelu_slope(up[f])
            up[f] = reorder(cot[f])

        @pl.loop(0, 3)
        def _(i):
            l = 2 - i
            x = 3 + i
            d = z.at[3]
            for f in range(2):
                d[f, :CELLS] = (up[f] * slope[l, f]).astype(BF)
            cut_windows(x, d)
            exchange_send(x)

            @pl.when(i == 0)
            def _():
                finish(2)

            for dy in range(3):
                total = None
                for f in range(2):
                    part = lax.dot_general(
                        xf[l, f, dy * PITCH : dy * PITCH + CELLS, :], d[f, :CELLS],
                        (((0,), (0,)), ((), ())), preferred_element_type=F32,
                    )
                    total = part if total is None else total + part
                gb[l, dy * 3 * C : (dy + 1) * 3 * C] = total.astype(BF)

            @pl.when(i == 2)
            def _():
                reduce_send(l)

            @pl.when(i > 0)
            def _():
                reduce_mid(l + 1)

            collect(x)

            @pl.when(i < 2)
            def _():
                reduce_send(l)

            @pl.when(i == 2)
            def _():
                reduce_mid(l)

            @pl.when(i > 0)
            def _():
                reduce_last(l + 1)

            halo_local(x, d)
            for f in range(2):
                widen(f, d, xb)
                total = None
                for dy in range(3):
                    for dx in range(3):
                        part = jnp.dot(
                            xb[f, dy * PITCH : dy * PITCH + CELLS, dx * C : (dx + 1) * C], wbk[l, 8 - 3 * dy - dx],
                            preferred_element_type=F32,
                        )
                        total = part if total is None else total + part
                up[f] = total

            @pl.when(i == 2)
            def _():
                reduce_last(l)

            correct(x, backward_taps(l))

        for f in range(2):
            gin[f] = lax.dot_general(
                order[...], up[f].astype(BF), (((0,), (0,)), ((), ())), preferred_element_type=F32
            ).astype(BF)

    @pl.when(jnp.logical_not(active))
    def _():
        gin[...] = jnp.zeros_like(gin)
        reduce_last(2)
        reduce_last(1)
        reduce_last(0)

    reduce_swap(2)
    reduce_swap(1)

    @pl.when(active)
    def _():
        @pl.loop(0, 6)
        def _(x):
            sent(x)

    for l in (2, 1):
        reduce_drain(l)
        grads[l] = gf[l]
    reduce_swap(0)
    reduce_drain(0)
    grads[0] = gf[0]


def shards(activation, cotangent, weight_one, weight_two, weight_three, neighbor, turn):
    def flipped(field):
        return field.transpose(0, 1, 3, 2, 4).reshape(2, TW * TH, C)

    vmem = pl.BlockSpec(memory_space=pltpu.VMEM)
    hbm = pl.BlockSpec(memory_space=pltpu.HBM)
    dma = pltpu.SemaphoreType.DMA
    gin, grads = pl.pallas_call(
        kernel,
        out_shape=(
            jax.ShapeDtypeStruct((2, TW * TH, C), BF),
            jax.ShapeDtypeStruct((3, 9 * C, C), BF),
        ),
        in_specs=[hbm] * 8,
        out_specs=(vmem, vmem),
        scratch_shapes=[
            pltpu.SMEM((4, FACES), jnp.int32),
            pltpu.SMEM((4, FACES), jnp.int32),
            pltpu.SMEM((FACES, 4), jnp.int32),
            pltpu.VMEM((2, TW * TH, C), BF),
            pltpu.VMEM((2, TW * TH, C), BF),
            pltpu.VMEM((3 * ROWS, KZ), BF),
            pltpu.VMEM((CELLS, TW * TH), BF),
            pltpu.VMEM((28 * 16, CELLS), BF),
            pltpu.VMEM((4, 2, KZ, C), BF),
            pltpu.VMEM((3, 2, ROWS, 3 * C), BF),
            pltpu.VMEM((2, ROWS, 3 * C), BF),
            pltpu.VMEM((3, 2, CELLS, C), F32),
            pltpu.VMEM((2, CELLS, C), F32),
            pltpu.VMEM((3, 9, C, C), BF),
            pltpu.VMEM((3, 9, C, C), BF),
            pltpu.VMEM((8, 64, C), F32),
            pltpu.VMEM((8, 2, 16, C), BF),
            pltpu.VMEM((6, 28, 2, 16, C), BF),
            pltpu.VMEM((6, 10, 2, 16, C), BF),
            pltpu.VMEM((6, 20, 2, 16, C), BF),
            pltpu.VMEM((6, 16, 2, 16, C), BF),
            pltpu.VMEM((6, 2, GROUPS, 2, 16, C), BF),
            pltpu.VMEM((6, 2, GROUPS, 2, 16, C), BF),
            pltpu.VMEM((6, GROUPS, 2, 16, C), BF),
            pltpu.VMEM((6, GROUPS, 2, 2, 16, C), BF),
            pltpu.VMEM((3, 9 * C, C), BF),
            pltpu.VMEM((3, 31, CHUNK, C), BF),
            pltpu.VMEM((3, CHUNK, C), BF),
            pltpu.VMEM((3, GROUPS, CHUNK, C), BF),
            pltpu.VMEM((3, 9 * C, C), BF),
            dma((8,)),
            dma((6, 4)),
            dma((6, 4)),
            dma((6,)),
            dma((6,)),
            dma((6, 2)),
            dma((6, 2)),
            dma((3, 4)),
            dma((3, 4)),
        ],
        compiler_params=pltpu.CompilerParams(
            collective_id=0, has_side_effects=True, vmem_limit_bytes=62 * 1024 * 1024
        ),
        name="glued_convolutions",
    )(
        neighbor.T, turn.T, flipped(activation), flipped(cotangent), weight_one, weight_two, weight_three,
        jnp.asarray(spread_matrix(), BF),
    )
    grad_input = gin.reshape(2, 1, TW, TH, C).transpose(0, 1, 3, 2, 4)
    scaled = grads.reshape(3, 9, C, C).astype(F32) * (1.0 / math.sqrt(FACES * NS * NS))
    return grad_input, scaled[0], scaled[1], scaled[2]


def solution(mesh):
    field = P("face", "tile", None, None, None)
    return jax.shard_map(
        shards,
        mesh=mesh,
        in_specs=(field, field, P(), P(), P(), P(), P()),
        out_specs=(field, P(), P(), P()),
        check_vma=False,
    )
```
